32 devices in a mesh: section: 2 (over x), dp: 4 (over y, core), mp: 4 (over z).
Axes of the slice: x: 2, y: 2, z: 4, core: 2. Of those that a mesh axis runs over, the one named last changes fastest.
Arguments:
- streams: bfloat16 [2, 32, 256, 768], P('section', ('dp', 'mp')), may hold values from -6 to 6
- lengths: int32 [2, 32], P(None, 'dp'), may hold values from 10 to 256, as said below
- vectors: float32 [2, 8, 768], P('section'), may hold values from -1.5 to 1.5
- attn_in: bfloat16 [2, 3, 768, 768], P('section', None, None, 'mp'), may hold values from -0.21875 to 0.21875
- attn_bias: float32 [2, 3, 12, 64], P('section', None, 'mp'), may hold values from -1.5 to 1.5
- attn_out: bfloat16 [2, 768, 768], P('section', 'mp'), may hold values from -0.875 to 0.875
- rel_table: float32 [2, 12, 320], P('section', 'mp'), may hold values from -4 to 4
- cross: bfloat16 [2, 2, 768, 768], P('section', None, None, 'mp'), may hold values from -0.5 to 0.5
- ffn_in: bfloat16 [2, 768, 3072], P('section', None, 'mp'), may hold values from -0.21875 to 0.21875
- ffn_bias: float32 [2, 24, 128], P('section', 'mp'), may hold values from -1.5 to 1.5
- ffn_out: bfloat16 [2, 3072, 768], P('section', 'mp'), may hold values from -0.15625 to 0.15625
- cotangent: bfloat16 [2, 32, 256, 768], P('section', ('dp', 'mp')), may hold values from -6 to 6
Outputs:
- layer_outputs: float32 [2, 32, 256, 768], P('section', ('dp', 'mp'))
- input_grads: float32 [2, 32, 256, 768], P('section', ('dp', 'mp'))
- vectors_grad: float32 [2, 8, 768], P('section', None, ('dp', 'mp'))
- attn_in_grad: float32 [2, 3, 768, 768], P('section', None, 'dp', 'mp')
- attn_bias_grad: float32 [2, 3, 12, 64], P('section', None, 'mp', 'dp')
- attn_out_grad: float32 [2, 768, 768], P('section', 'mp', 'dp')
- rel_grad: float32 [2, 12, 320], P('section', 'mp', 'dp')
- cross_grad: float32 [2, 2, 768, 768], P('section', None, 'dp', 'mp')
- ffn_in_grad: float32 [2, 768, 3072], P('section', 'dp', 'mp')
- ffn_bias_grad: float32 [2, 24, 128], P('section', 'mp', 'dp')
- ffn_out_grad: float32 [2, 3072, 768], P('section', 'mp', 'dp')
The draws below stay inside these ranges and needn't reach their ends.
Inputs may be any that keep to these rules, and one draw needn't show every extreme that they name: `lengths`: row 0 counts frames (10 to 256), row 1 transcript tokens (10 to 250); each group of 8 consecutive utterances has one with 256 frames and 250 tokens.
All inputs are finite; a program needn't handle non-finite values.
Results may differ from the reference program's by a relative error of at most 0.02.
Values may be sent and summed in bfloat16 or wider, within the bound.
A program may use at most 192 MiB of HBM per device.

```python
import jax
import jax.numpy as jnp
from jax import lax

D = 768
H = 12
HD = 64
FF = 3072
SEQ = 256
REL = 320
UTT_DEV = 8
UTT = 32
TEXT_MAX = 250
FFB = 24
N_DP = 4


def draw_lengths(key, part):
    key = jax.random.fold_in(key, 11)
    split_keys = jax.random.split(key, 3)
    blocks = UTT // UTT_DEV
    frames = jax.random.randint(split_keys[0], (UTT,), 10, SEQ + 1, dtype=jnp.int32)
    tokens = jax.random.randint(split_keys[1], (UTT,), 10, TEXT_MAX + 1, dtype=jnp.int32)
    top_slot = jax.random.randint(split_keys[2], (blocks,), 0, UTT_DEV, dtype=jnp.int32) + jnp.arange(blocks, dtype=jnp.int32) * UTT_DEV
    position = jnp.arange(UTT, dtype=jnp.int32)
    longest = jnp.any(position[:, None] == top_slot[None, :], axis=1)
    shortest = position == (top_slot[0] + 1) % UTT_DEV
    frames = jnp.where(longest, SEQ, jnp.where(shortest, 10, frames))
    tokens = jnp.where(longest, TEXT_MAX, jnp.where(shortest, 10, tokens))
    return jnp.stack([frames, tokens]).astype(jnp.int32)


def draw_vectors(key, part):
    key = jax.random.fold_in(key, 12)
    split_keys = jax.random.split(key, 2)
    gains = jax.random.uniform(split_keys[0], (2, 8, D), jnp.float32, 0.5, 1.5)
    shifts = jnp.clip(0.3 * jax.random.normal(split_keys[1], (2, 8, D), jnp.float32), -1.5, 1.5)
    row_index = jnp.arange(8)[None, :, None]
    is_gain = (row_index == 0) | (row_index == 3) | (row_index == 5)
    return jnp.where(is_gain, gains, shifts)


def draw_cross(key, part):
    key = jax.random.fold_in(key, 13)
    base = jax.random.normal(key, (2, 2, D, D), jnp.float32) * D ** (-0.5)
    outer_slot = (jnp.arange(2)[:, None, None, None] == 1) & (jnp.arange(2)[None, :, None, None] == 1)
    return jnp.clip(jnp.where(outer_slot, 4.0 * base, base), -0.5, 0.5).astype(jnp.bfloat16)


def level_of(stream_key, shape, cuts, least, high):
    loudness = 1.0
    for axis_at, shards_of in cuts:
        steps = jax.random.uniform(jax.random.fold_in(jax.random.fold_in(stream_key, 6), axis_at), (shards_of,), jnp.float32, least / len(cuts), high / len(cuts))
        loudness = loudness * jnp.repeat(jnp.exp(steps), shape[axis_at] // shards_of).reshape((-1,) + (1,) * (len(shape) - 1 - axis_at))
    return loudness


def normal_values(stream_key, shape, scale, reach, cuts=(), kind=jnp.bfloat16):
    level = level_of(stream_key, shape, cuts, -0.22, 0.18) if cuts else 1.0
    result = jax.random.normal(stream_key, shape, jnp.float32) * scale * level
    return jnp.minimum(jnp.maximum(result, -reach), reach).astype(kind)


def setup_inputs(seed: int = 0) -> dict:
    seeds = jax.random.split(jax.random.key(seed), 13)
    streams = normal_values(seeds[0], (2, UTT, SEQ, D), 1.0, 6.0, ((0, 2), (1, 16)))
    lengths = draw_lengths(jax.random.fold_in(seeds[12], 71), 0)
    vectors = draw_vectors(jax.random.fold_in(seeds[12], 71), 0)
    attn_in = normal_values(seeds[3], (2, 3, D, D), D ** -0.5, 0.21875, ((0, 2), (3, 4)))
    attn_bias = normal_values(seeds[4], (2, 3, H, HD), 0.3, 1.5, ((0, 2), (2, 4)), jnp.float32)
    attn_out = normal_values(seeds[5], (2, D, D), (D // 16) ** -0.5, 0.875, ((0, 2), (1, 4)))
    rel_table = normal_values(seeds[6], (2, H, REL), 1.0, 4.0, ((0, 2), (1, 4)), jnp.float32)
    cross = draw_cross(jax.random.fold_in(seeds[12], 71), 0)
    ffn_in = normal_values(seeds[8], (2, D, FF), D ** -0.5, 0.21875, ((0, 2), (2, 4)))
    ffn_bias = normal_values(seeds[9], (2, FFB, 128), 0.3, 1.5, ((0, 2), (1, 4)), jnp.float32)
    ffn_out = normal_values(seeds[10], (2, FF, D), (FF // 2) ** -0.5, 0.15625, ((0, 2), (1, 4)))
    cotangent = normal_values(seeds[11], (2, UTT, SEQ, D), 1.0, 6.0, ((0, 2), (1, 16)))
    return dict(streams=streams, lengths=lengths, vectors=vectors, attn_in=attn_in, attn_bias=attn_bias, attn_out=attn_out, rel_table=rel_table, cross=cross, ffn_in=ffn_in, ffn_bias=ffn_bias, ffn_out=ffn_out, cotangent=cotangent)


@jax.custom_vjp
def low(v):
    return lax.optimization_barrier(v.astype(jnp.bfloat16)).astype(jnp.float32)

@jax.custom_vjp
def low_back(v):
    return v

def low_keep(v):
    return (low(v), None)

def low_pass(kept, grad):
    return (grad,)

def back_keep(v):
    return (v, None)

def back_low(kept, grad):
    return (low(grad),)
low.defvjp(low_keep, low_pass)
low_back.defvjp(back_keep, back_low)
HIGHEST = lax.Precision.HIGHEST
EPSILON = 1e-05
MASKED = -1e+30

def layer_norm(values, ln_gain, ln_shift):
    row_mean = lax.optimization_barrier(jnp.mean(values, axis=-1, keepdims=True))
    centred = values - row_mean
    spread = lax.optimization_barrier(jnp.mean(centred * centred, axis=-1, keepdims=True))
    return centred * lax.rsqrt(spread + EPSILON) * ln_gain + ln_shift

def project(left, weight):
    return jnp.einsum('gsd,dc->gsc', left, weight, precision=HIGHEST)

def split_heads(values):
    return values.reshape(values.shape[0], values.shape[1], H, HD)

def relative_bias(rel_rows):
    places = jnp.arange(SEQ, dtype=jnp.int32)
    offsets = jnp.clip(places[None, :] - places[:, None], -(REL // 2), REL // 2 - 1) + REL // 2
    return rel_rows[:, offsets]

def attend(queries, key_rows, values, score_bias, key_valid):
    scores = jnp.einsum('gihd,gjhd->ghij', split_heads(queries), split_heads(key_rows), precision=HIGHEST) * 0.125 + score_bias
    scores = jnp.where(key_valid[:, None], low_back(scores), MASKED)
    attn_probs = jax.nn.softmax(scores, axis=-1)
    context = jnp.einsum('ghij,gjhd->gihd', low(attn_probs), split_heads(values), precision=HIGHEST)
    return low(low_back(context.reshape(queries.shape)))

def self_block(stream, vector, w_in, b_in, w_out, rel_rows, key_valid):
    normed = low(layer_norm(stream, vector[0], vector[1]))
    queries = low(low_back(project(normed, w_in[0]) + b_in[0]))
    key_rows = low(low_back(project(normed, w_in[1])))
    values = low(low_back(project(normed, w_in[2]) + b_in[1]))
    context = attend(queries, key_rows, values, relative_bias(rel_rows)[None], key_valid)
    return stream + low_back(project(context, w_out)) + vector[2]

def feed_forward(stream, vector, w_one, b_one, w_two):
    normed = low(layer_norm(stream, vector[5], vector[6]))
    hidden = low_back(project(normed, w_one) + b_one)
    active = low(jax.nn.gelu(hidden, approximate=False))
    return stream + low_back(project(active, w_two)) + vector[7]

def layers(streams, params, lengths):
    vectors, attn_in, attn_bias, attn_out, rel_table, cross, ffn_in, ffn_bias, ffn_out = params
    b_in = attn_bias.reshape(2, 3, D)
    b_one = ffn_bias.reshape(2, FF)
    places = jnp.arange(SEQ, dtype=jnp.int32)
    causal = places[:, None] >= places[None, :]

    def utterance_group(scan_carry, scan_item):
        frames_in, tokens_in, frame_lens, token_lens = scan_item
        frame_valid = jnp.broadcast_to(places[None, None, :] < frame_lens[:, None, None], (UTT_DEV, SEQ, SEQ))
        token_valid = (places[None, None, :] < token_lens[:, None, None]) & causal[None]
        encoded = self_block(frames_in, vectors[0], attn_in[0], b_in[0], attn_out[0], rel_table[0], frame_valid)
        encoded = feed_forward(encoded, vectors[0], ffn_in[0], b_one[0], ffn_out[0])
        memory = low(layer_norm(encoded, vectors[0, 3], vectors[0, 4]))
        mem_keys = low(low_back(project(memory, cross[0, 0])))
        mem_values = low(low_back(project(memory, cross[0, 1]) + b_in[0, 2]))
        decoded = self_block(tokens_in, vectors[1], attn_in[1], b_in[1], attn_out[1], rel_table[1], token_valid)
        normed = low(layer_norm(decoded, vectors[1, 3], vectors[1, 4]))
        queries = low(low_back(project(normed, cross[1, 0]) + b_in[1, 2]))
        context = attend(queries, mem_keys, mem_values, 0.0, frame_valid)
        decoded = decoded + low_back(jnp.einsum('gsc,dc->gsd', context, cross[1, 1], precision=HIGHEST))
        decoded = feed_forward(decoded, vectors[1], ffn_in[1], b_one[1], ffn_out[1])
        return (scan_carry, (encoded, decoded))
    scan_items = (streams[0].reshape(N_DP, UTT_DEV, SEQ, D), streams[1].reshape(N_DP, UTT_DEV, SEQ, D), lengths[0].reshape(N_DP, UTT_DEV), lengths[1].reshape(N_DP, UTT_DEV))
    _, (encoded, decoded) = lax.scan(jax.checkpoint(utterance_group), jnp.zeros((), jnp.float32), scan_items)
    return jnp.stack([encoded.reshape(UTT, SEQ, D), decoded.reshape(UTT, SEQ, D)])

def reference(streams, lengths, vectors, attn_in, attn_bias, attn_out, rel_table, cross, ffn_in, ffn_bias, ffn_out, cotangent):
    params = (vectors.astype(jnp.float32), attn_in.astype(jnp.float32), attn_bias.astype(jnp.float32), attn_out.astype(jnp.float32), rel_table.astype(jnp.float32), cross.astype(jnp.float32), ffn_in.astype(jnp.float32), ffn_bias.astype(jnp.float32), ffn_out.astype(jnp.float32))
    outputs, pullback = jax.vjp(lambda inputs, weights: layers(inputs, weights, lengths), streams.astype(jnp.float32), params)
    d_streams, weight_grads = pullback(cotangent.astype(jnp.float32))
    return (outputs, d_streams, weight_grads[0], weight_grads[1], weight_grads[2], weight_grads[3], weight_grads[4], weight_grads[5], weight_grads[6], weight_grads[7], weight_grads[8])
```

```python
import functools
import jax
import jax.numpy as jnp
from jax import lax
from jax.experimental import pallas as pl
from jax.experimental.pallas import tpu as pltpu
from jax.sharding import PartitionSpec as P

MESH = pl.DeviceIdType.MESH
ANY = pl.BlockSpec(memory_space=pl.ANY)
VM = pl.BlockSpec(memory_space=pltpu.VMEM)
BLOCKS = 4


def partners(dp_index, step):
    bit = lax.rem(dp_index // step, 2)
    return dp_index + step - 2 * step * bit


def gather_kernel(mp, a_ref, c_ref, w1_ref, w2_ref, small_ref, out_ref, small_out,
                  held, small_held, local_sem, z_send, z_recv, p_send, p_recv, s_send, s_recv):
    me = lax.axis_index("mp")
    dp_index = lax.axis_index("dp")
    decoding = lax.axis_index("section") == 1
    core = partners(dp_index, 1)
    side = partners(dp_index, 2)
    quarter = lax.rem(dp_index, 4)
    side_quarter = quarter + 2 - 4 * (quarter // 2)
    part = a_ref.shape[0] // 4
    own = [a_ref, c_ref, w1_ref, w2_ref]

    barrier = pltpu.get_barrier_semaphore()
    for other in range(mp):
        @pl.when(other != me)
        def _():
            pl.semaphore_signal(barrier, inc=1, device_id={"mp": other}, device_id_type=MESH)
    for other in (core, side):
        pl.semaphore_signal(barrier, inc=1, device_id={"dp": other}, device_id_type=MESH)
    pl.semaphore_wait(barrier, mp + 1)

    def rows(which):
        return pl.ds(pl.multiple_of(which * part, 16), part)

    def along(src, shard, block, way, dist):
        return pltpu.make_async_remote_copy(
            src_ref=src, dst_ref=out_ref.at[shard, block, rows(quarter)],
            send_sem=z_send.at[way, dist - 1, block], recv_sem=z_recv.at[way, dist - 1, block],
            device_id={"mp": me + 1 - 2 * way}, device_id_type=MESH)

    def across(kind, shard, block, which, way, dist, to):
        ref = out_ref.at[shard, block, rows(which)]
        return pltpu.make_async_remote_copy(
            src_ref=ref, dst_ref=ref,
            send_sem=p_send.at[kind, way, dist - 1, block], recv_sem=p_recv.at[kind, way, dist - 1, block],
            device_id={"dp": to}, device_id_type=MESH)

    def small_copy(hop):
        return pltpu.make_async_remote_copy(
            src_ref=small_ref, dst_ref=small_out.at[me],
            send_sem=s_send.at[hop - 1], recv_sem=s_recv.at[hop - 1],
            device_id={"mp": lax.rem(me + hop, mp)}, device_id_type=MESH)

    def needed(block):
        return decoding if block == 1 else me >= 0

    def has_next(way):
        return (me < mp - 1) if way == 0 else (me > 0)

    def has_shard(way, dist):
        return (me >= dist) if way == 0 else (me + dist <= mp - 1)

    for block in range(BLOCKS):
        for way in (0, 1):
            @pl.when(needed(block) & has_next(way))
            def _():
                along(own[block].at[rows(quarter)], me, block, way, 1).start()
        if block == 0:
            for hop in range(1, mp):
                small_copy(hop).start()
            pltpu.make_async_copy(small_ref, small_held, local_sem.at[BLOCKS]).start()
    for block in range(BLOCKS):
        pltpu.make_async_copy(own[block], held.at[block], local_sem.at[block]).start()
    pltpu.make_async_copy(small_ref, small_held, local_sem.at[BLOCKS]).wait()
    pltpu.make_async_copy(small_held, small_out.at[me], local_sem.at[BLOCKS]).start()
    for block in range(BLOCKS):
        pltpu.make_async_copy(own[block], held.at[block], local_sem.at[block]).wait()
        pltpu.make_async_copy(held.at[block], out_ref.at[me, block], local_sem.at[block]).start()

    pieces = [(dist, block, way) for dist in range(1, mp) for block in range(BLOCKS) for way in (0, 1)]

    def shard_at(way, dist):
        return me - dist if way == 0 else me + dist

    def on_line(dist, block, way):
        @pl.when(needed(block) & has_shard(way, dist))
        def _():
            shard = shard_at(way, dist)
            along(out_ref.at[shard, block, rows(quarter)], shard, block, way, dist).wait_recv()
            if dist < mp - 1:
                @pl.when(has_next(way))
                def _():
                    along(out_ref.at[shard, block, rows(quarter)], shard, block, way, dist + 1).start()
            across(1, shard, block, quarter, way, dist, side).start()
            across(0, shard, block, quarter, way, dist, core).start()

    def on_side(dist, block, way):
        @pl.when(needed(block) & has_shard(way, dist))
        def _():
            shard = shard_at(way, dist)
            across(1, shard, block, side_quarter, way, dist, side).wait_recv()
            across(2, shard, block, side_quarter, way, dist, core).start()

    lag = 2
    for index in range(len(pieces) + lag):
        if index < len(pieces):
            on_line(*pieces[index])
        if index >= lag:
            on_side(*pieces[index - lag])

    for block in range(BLOCKS):
        pltpu.make_async_copy(held.at[block], out_ref.at[me, block], local_sem.at[block]).wait()
        for way in (0, 1):
            @pl.when(needed(block) & has_next(way))
            def _():
                along(own[block].at[rows(quarter)], me, block, way, 1).wait_send()
    pltpu.make_async_copy(small_held, small_out.at[me], local_sem.at[BLOCKS]).wait()
    for hop in range(1, mp):
        small_copy(hop).wait_send()
        pltpu.make_async_remote_copy(
            src_ref=small_ref, dst_ref=small_out.at[lax.rem(me + mp - hop, mp)],
            send_sem=s_send.at[hop - 1], recv_sem=s_recv.at[hop - 1],
            device_id={"mp": lax.rem(me + hop, mp)}, device_id_type=MESH).wait_recv()
    core_quarter = quarter + 1 - 2 * lax.rem(quarter, 2)
    core_side_quarter = core_quarter + 2 - 4 * (core_quarter // 2)
    for dist, block, way in pieces:
        @pl.when(needed(block) & has_shard(way, dist))
        def _():
            shard = shard_at(way, dist)
            across(0, shard, block, core_quarter, way, dist, core).wait_recv()
            across(2, shard, block, core_side_quarter, way, dist, core).wait_recv()
            across(0, shard, block, quarter, way, dist, core).wait_send()
            across(1, shard, block, quarter, way, dist, side).wait_send()
            across(2, shard, block, side_quarter, way, dist, core).wait_send()
            if dist < mp - 1:
                @pl.when(has_next(way))
                def _():
                    along(out_ref.at[shard, block, rows(quarter)], shard, block, way, dist + 1).wait_send()


def gather_weights(mp, a, c, w1, w2, small):
    sem = pltpu.SemaphoreType.DMA
    return pl.pallas_call(
        functools.partial(gather_kernel, mp),
        out_shape=(jax.ShapeDtypeStruct((mp, BLOCKS) + a.shape, a.dtype),
                   jax.ShapeDtypeStruct((mp,) + small.shape, small.dtype)),
        in_specs=[ANY] * 5,
        out_specs=(ANY, ANY),
        scratch_shapes=[pltpu.VMEM((BLOCKS,) + a.shape, a.dtype), pltpu.VMEM(small.shape, small.dtype), sem((BLOCKS + 1,)), sem((2, mp - 1, BLOCKS)), sem((2, mp - 1, BLOCKS)),
                        sem((3, 2, mp - 1, BLOCKS)), sem((3, 2, mp - 1, BLOCKS)),
                        sem((mp - 1,)), sem((mp - 1,))],
        compiler_params=pltpu.CompilerParams(collective_id=0, has_side_effects=True, vmem_limit_bytes=16 * 2**20),
        name="gather_weights",
    )(a, c, w1, w2, small)


def scatter_kernel(mp, dp, grad_ref, small_ref, out_ref, small_out,
                   own, from_core, from_side, from_line, small_got,
                   l_sem, c_send, c_recv, y_send, y_recv, z_send, z_recv, s_send, s_recv):
    me = lax.axis_index("mp")
    dp_index = lax.axis_index("dp")
    decoding = lax.axis_index("section") == 1
    near = dp // 4
    core = partners(dp_index, near)
    side = partners(dp_index, 2 * near)
    quarter = dp_index // near
    parity = lax.rem(quarter, 2)
    half = quarter // 2
    part = grad_ref.shape[2] // 4
    count = dp * mp
    line = dp_index * mp + me

    barrier = pltpu.get_barrier_semaphore()

    def at(hop):
        other = lax.rem(line + hop, count)
        return {"dp": other // mp, "mp": lax.rem(other, mp)}

    def greet(hop, carry):
        pl.semaphore_signal(barrier, inc=1, device_id=at(hop), device_id_type=MESH)
        return carry

    lax.fori_loop(1, count, greet, 0)
    pl.semaphore_wait(barrier, count - 1)

    def rows(which):
        return pl.ds(pl.multiple_of(which * part, 16), part)

    def load(m, b, k):
        return pltpu.make_async_copy(grad_ref.at[m, b, rows(2 * k + parity)], own.at[m, b, k], l_sem.at[m, b, k])

    def to_core(m, b, k):
        return pltpu.make_async_remote_copy(
            src_ref=grad_ref.at[m, b, rows(2 * k + 1 - parity)], dst_ref=from_core.at[m, b, k],
            send_sem=c_send.at[m, b, k], recv_sem=c_recv.at[m, b, k],
            device_id={"dp": core}, device_id_type=MESH)

    def to_side(m, b):
        return pltpu.make_async_remote_copy(
            src_ref=own.at[m, b, 1 - half], dst_ref=from_side.at[m, b],
            send_sem=y_send.at[m, b], recv_sem=y_recv.at[m, b],
            device_id={"dp": side}, device_id_type=MESH)

    def on_line(way, m, b):
        return pltpu.make_async_remote_copy(
            src_ref=own.at[m, b, half], dst_ref=from_line.at[way, m, b],
            send_sem=z_send.at[way, m, b], recv_sem=z_recv.at[way, m, b],
            device_id={"mp": me + 1 - 2 * way}, device_id_type=MESH)

    def small_copy(hop):
        return pltpu.make_async_remote_copy(
            src_ref=small_ref.at[lax.rem(line + hop, count)], dst_ref=small_got.at[hop],
            send_sem=s_send.at[hop], recv_sem=s_recv.at[hop], device_id=at(hop), device_id_type=MESH)

    def add(into, other):
        into[...] = (into[...].astype(jnp.float32) + other[...].astype(jnp.float32)).astype(into.dtype)

    def needed(b):
        return decoding if b == 1 else me >= 0

    order = [3, 0, 2, 1] if mp == 4 else list(range(mp))
    units = [(m, b) for b in (1, 2, 3, 0) for m in order]

    def small_send(hop, carry):
        small_copy(hop).start()
        return carry

    lax.fori_loop(1, count, small_send, 0)
    for m, b in units:
        @pl.when(needed(b))
        def _():
            for k in (0, 1):
                to_core(m, b, k).start()
                load(m, b, k).start()

    def stage_core(m, b):
        @pl.when(needed(b))
        def _():
            for k in (0, 1):
                load(m, b, k).wait()
                to_core(m, b, k).wait_recv()
                add(own.at[m, b, k], from_core.at[m, b, k])
            to_side(m, b).start()

    def stage_side(m, b):
        @pl.when(needed(b))
        def _():
            to_side(m, b).wait_recv()
            add(own.at[m, b, half], from_side.at[m, b])
            for way in (0, 1):
                first = (me == 0) if way == 0 else (me == mp - 1)
                @pl.when(first & (me != m))
                def _():
                    on_line(way, m, b).start()

    def stage_line(m, b):
        for way in (0, 1):
            inner = ((me > 0) & (me < m)) if way == 0 else ((me < mp - 1) & (me > m))
            @pl.when(needed(b) & inner)
            def _():
                on_line(way, m, b).wait_recv()
                add(own.at[m, b, half], from_line.at[way, m, b])
                on_line(way, m, b).start()

    lead, lag = 4, 3
    for t in range(len(units) + lead + lag):
        if t < len(units):
            stage_core(*units[t])
        if 0 <= t - lead < len(units):
            stage_side(*units[t - lead])
        if 0 <= t - lead - lag < len(units):
            stage_line(*units[t - lead - lag])

    for b in range(BLOCKS):
        @pl.when(needed(b))
        def _():
            out_ref[b] = own[me, b, half].astype(jnp.float32)
            for way in (0, 1):
                @pl.when((me > 0) if way == 0 else (me < mp - 1))
                def _():
                    on_line(way, me, b).wait_recv()
                    out_ref[b] += from_line[way, me, b].astype(jnp.float32)
        @pl.when(jnp.logical_not(needed(b)))
        def _():
            out_ref[b] = jnp.zeros_like(out_ref[b])

    small_out[...] = small_ref[line]

    def small_add(hop, carry):
        small_copy(hop).wait()
        small_out[...] += small_got[hop]
        return carry

    lax.fori_loop(1, count, small_add, 0)
    for m, b in units:
        @pl.when(needed(b))
        def _():
            for k in (0, 1):
                to_core(m, b, k).wait_send()
            to_side(m, b).wait_send()
            for way in (0, 1):
                @pl.when((me < m) if way == 0 else (me > m))
                def _():
                    on_line(way, m, b).wait_send()


def scatter_grads(mp, dp, grads, small):
    sem = pltpu.SemaphoreType.DMA
    part, width = grads.shape[2] // 4, grads.shape[3]
    block = (part, width)
    vm = lambda *lead: pltpu.VMEM(lead + block, grads.dtype)
    return pl.pallas_call(
        functools.partial(scatter_kernel, mp, dp),
        out_shape=(jax.ShapeDtypeStruct((BLOCKS,) + block, jnp.float32),
                   jax.ShapeDtypeStruct(small.shape[1:], small.dtype)),
        in_specs=[ANY, VM],
        out_specs=(VM, VM),
        scratch_shapes=[vm(mp, BLOCKS, 2), vm(mp, BLOCKS, 2), vm(mp, BLOCKS), vm(2, mp, BLOCKS),
                        pltpu.VMEM(small.shape, small.dtype),
                        sem((mp, BLOCKS, 2)), sem((mp, BLOCKS, 2)), sem((mp, BLOCKS, 2)),
                        sem((mp, BLOCKS)), sem((mp, BLOCKS)), sem((2, mp, BLOCKS)), sem((2, mp, BLOCKS)),
                        sem((dp * mp,)), sem((dp * mp,))],
        compiler_params=pltpu.CompilerParams(collective_id=1, has_side_effects=True, vmem_limit_bytes=48 * 2**20),
        name="scatter_grads",
    )(grads, small)


EPSILON = 1e-05
MASKED = -1e30
HEADS = 3
LANES = 128
Q_SLOTS, K_SLOTS, V_SLOTS, O_SLOTS = (0, 1, 4), (2, 3, 8), (5, 6, 7), (9, 10, 11)
PROJ = 640
CTX = 512
bf16, f32 = jnp.bfloat16, jnp.float32


def nn(a, b):
    return lax.dot_general(a, b, (((1,), (0,)), ((), ())), preferred_element_type=f32)


def nt(a, b):
    return lax.dot_general(a, b, (((1,), (1,)), ((), ())), preferred_element_type=f32)


def tn(a, b):
    return lax.dot_general(a, b, (((0,), (0,)), ((), ())), preferred_element_type=f32)


def norm_parts(x):
    centred = x - jnp.mean(x, axis=-1, keepdims=True)
    r = lax.rsqrt(jnp.mean(centred * centred, axis=-1, keepdims=True) + EPSILON)
    return centred * r, r


def norm(x, gain, shift):
    xh, _ = norm_parts(x)
    return xh * gain + shift


def row_loop(total, size, body):
    def step(i, carry):
        body(pl.ds(pl.multiple_of(i * size, size), size))
        return carry
    lax.fori_loop(0, total // size, step, 0)


def even_lanes(rows):
    return lax.broadcasted_iota(jnp.int32, (rows, LANES), 1) < LANES // 2


def half_mask(half):
    lane = lax.broadcasted_iota(jnp.int32, (1, LANES), 1)
    on = (lane < LANES // 2) if half == 0 else (lane >= LANES // 2)
    return on.astype(f32).astype(bf16)


def slot_row(slots):
    lane = lax.broadcasted_iota(jnp.int32, (1, PROJ), 1)
    on = lane < 0
    for s in slots:
        on = on | ((lane >= 64 * s) & (lane < 64 * s + 64))
    return on


def tile(ref, m, rows, t):
    return ref[m, rows, t * LANES:(t + 1) * LANES]


HEAD_TILES = (((0, 0), (1, 0), (2, 1), (0, 1)),
              ((0, 1), (1, 1), (3, 0), (1, 0)),
              ((2, 0), (4, 0), (3, 1), (1, 1)))


def attend(m, length, utts, qkv_ref, ctx_ref, p_ref, limits, ext_ref):
    key_at = lax.broadcasted_iota(jnp.int32, (length, length), 0)
    even = even_lanes(length)
    parts = [[None] * HEADS for _ in range(utts)]
    for r in range(HEADS):
        (qt, half), (kt, _), (vt, _), _ = HEAD_TILES[r]
        if ext_ref is not None:
            row = ext_ref[m, 3 + r:4 + r, :2 * length]
            bias = pltpu.roll(jnp.broadcast_to(row, (length, 2 * length)), 0, 1, stride=1, stride_axis=0)[:, :length]
        for u in range(utts):
            rows = pl.ds(u * length, length)
            s = nt(tile(qkv_ref, m, rows, kt) * half_mask(half), tile(qkv_ref, m, rows, qt))
            if ext_ref is not None:
                s = s + bias
            s = jnp.where(key_at <= limits[u], s, MASKED)
            e = jnp.exp(s - jnp.max(s, axis=0, keepdims=True))
            p = (e * (1.0 / jnp.sum(e, axis=0, keepdims=True))).astype(bf16)
            p_ref[u, m, r] = p
            parts[u][r] = tn(p, tile(qkv_ref, m, rows, vt))
    for u in range(utts):
        rows = pl.ds(u * length, length)
        ctx_ref[m, rows, :LANES] = jnp.where(even, 0.0, parts[u][0]).astype(bf16)
        ctx_ref[m, rows, LANES:] = jnp.where(even, parts[u][1], parts[u][2]).astype(bf16)


def attend_back(m, length, utts, qkv_ref, p_ref, dctx_ref, out_ref, rel_ref, flip):
    even = even_lanes(length)
    got = [[None] * HEADS for _ in range(utts)]
    for r in range(HEADS):
        (qt, _), (kt, _), (vt, vhalf), (ot, _) = HEAD_TILES[r]
        total = None
        for u in range(utts):
            rows = pl.ds(u * length, length)
            p = p_ref[u, m, r]
            dctx = tile(dctx_ref, m, rows, ot)
            dp = nt(tile(qkv_ref, m, rows, vt) * half_mask(vhalf), dctx)
            pf = p.astype(f32)
            t = pf * dp
            ds = (t - pf * jnp.sum(t, axis=0, keepdims=True)).astype(bf16)
            got[u][r] = (tn(ds, tile(qkv_ref, m, rows, kt)) * 0.125, nn(ds, tile(qkv_ref, m, rows, qt)), nn(p, dctx))
            if rel_ref is not None:
                turned = nn(flip, ds)
                total = turned if total is None else total + turned
        if rel_ref is not None:
            wide = jnp.concatenate([total, jnp.zeros_like(total)], axis=1)
            wide = pltpu.roll(wide, 0, 1, stride=1, stride_axis=0)
            rel_ref[m, 3 + r:4 + r, :2 * length] = jnp.sum(wide, axis=0, keepdims=True)
    for u in range(utts):
        rows = pl.ds(u * length, length)
        (q0, k0, v0), (q1, k1, v1), (q2, k2, v2) = got[u]
        for t, (left, right) in enumerate(((q0, q1), (k0, k1), (q2, v0), (v1, v2), (k2, 0.0))):
            out_ref[m, rows, t * LANES:(t + 1) * LANES] = jnp.where(even, left, right).astype(bf16)


def gelu_both(u):
    cdf = 0.5 + 0.5 * lax.erf(u * 0.7071067811865476)
    return u * cdf, cdf + u * (jnp.exp(-0.5 * u * u) * 0.3989422804014327)


def norm_back(total, x_ref, gain, dh_ref, add_into, vg_ref, gain_row, grad_out=None):
    width = gain.shape[-1]

    def step(i, carry):
        dgain, dshift = carry
        rows = pl.ds(pl.multiple_of(i * 128, 128), 128)
        dh = dh_ref[rows].astype(f32)
        xh, r = norm_parts(x_ref[rows].astype(f32))
        e = dh * gain
        dx = r * (e - jnp.mean(e, axis=-1, keepdims=True) - xh * jnp.mean(e * xh, axis=-1, keepdims=True))
        add_into[rows] = add_into[rows].astype(f32) + dx
        return dgain + jnp.sum(dh * xh, axis=0, keepdims=True), dshift + jnp.sum(dh, axis=0, keepdims=True)

    zero = jnp.zeros((1, width), f32)
    dgain, dshift = lax.fori_loop(0, total // 128, step, (zero, zero))
    vg_ref[gain_row:gain_row + 1, :] = dgain
    vg_ref[gain_row + 1:gain_row + 2, :] = dshift


def ffn_forward(total, mp, x_ref, y_ref, out_ref, h_ref, a_ref, gp_ref, w1_ref, w2_ref, small_ref, vec_ref, wait):
    def prepare(rows):
        x = x_ref[rows]
        h_ref[rows] = norm(x, vec_ref[5:6], vec_ref[6:7]).astype(bf16)
        out_ref[rows] = x + vec_ref[7:8]
    row_loop(total, 128, prepare)

    def shard(m, carry):
        wait(2, m)
        bias = small_ref[m, 2:3, :]

        def inner(rows):
            u = nn(h_ref[rows], w1_ref[m]) + bias
            a, gp = gelu_both(u)
            a_ref[m, rows] = a.astype(bf16)
            gp_ref[m, rows] = gp.astype(bf16)
        row_loop(total, 128, inner)
        wait(3, m)
        out_ref[...] += nn(a_ref[m], w2_ref[m])
        return carry
    lax.fori_loop(0, mp, shard, 0)


def turn(dst_ref, src):
    dst_ref[...] = src.T


def ffn_backward(total, mp, g_ref, x_ref, h_ref, a_ref, gp_ref, w1_ref, w2_ref, dy_ref, dyt_ref, ht_ref, dh_ref,
                 du_ref, vec_ref, vg_ref, sg_ref, sent):
    vg_ref[7:8, :] = jnp.sum(g_ref[...], axis=0, keepdims=True)
    dy_ref[...] = g_ref[...].astype(bf16)
    turn(dyt_ref, dy_ref[...])
    turn(ht_ref, h_ref[...])
    dh_ref[...] = jnp.zeros_like(dh_ref)

    def shard(m, carry):
        def inner(rows):
            da = nt(dy_ref[rows], w2_ref[m])
            du_ref[rows] = (da * gp_ref[m, rows].astype(f32)).astype(bf16)
        row_loop(total, 128, inner)
        du = du_ref[...]
        sg_ref[m, 2:3, :] = jnp.sum(du.astype(f32), axis=0, keepdims=True)
        dh_ref[...] += nt(du, w1_ref[m])
        w2_ref[m] = nn(dyt_ref[...], a_ref[m]).astype(bf16)
        sent(3, m)
        w1_ref[m] = nn(ht_ref[...], du).astype(bf16)
        sent(2, m)
        return carry
    lax.fori_loop(0, mp, shard, 0)
    norm_back(total, x_ref, vec_ref[5:6], dh_ref, g_ref, vg_ref, 5)


def forward_kernel(mp, utts, length, lens_ref, x_ref, vec_ref, small_ref, w_ref,
                   qkv_ref, ctx_ref, p_ref, x1_ref, a_ref, gp_ref, out_ref, mem_ref,
                   wa, w1, w2, h, w_sem):
    decoding = lax.axis_index("section") == 1
    total = utts * length
    bufs = {0: wa, 2: w1, 3: w2}

    def load(b, m):
        return pltpu.make_async_copy(w_ref.at[m, b], bufs[b].at[m], w_sem.at[b, m])

    for m in range(mp):
        load(0, m).start()

    @pl.when(jnp.logical_not(decoding))
    def _():
        for m in range(mp):
            load(2, m).start()
            load(3, m).start()

    def prepare(rows):
        x = x_ref[rows].astype(f32)
        h[rows] = norm(x, vec_ref[0:1], vec_ref[1:2]).astype(bf16)
        x1_ref[rows] = x + vec_ref[2:3]
    row_loop(total, 128, prepare)

    query_at = lax.broadcasted_iota(jnp.int32, (1, length), 1)
    limits = []
    for u in range(utts):
        last = lens_ref[u] - 1
        limits.append(jnp.where(decoding, jnp.minimum(query_at, last), last))
    scale = jnp.where(slot_row(Q_SLOTS), 0.125, 1.0)

    def shard(m, carry):
        load(0, m).wait()
        qkv_ref[m] = ((nt(h[...], wa[m, :PROJ]) + small_ref[m, 0:1, :PROJ]) * scale).astype(bf16)
        attend(m, length, utts, qkv_ref, ctx_ref, p_ref, limits, small_ref)
        x1_ref[...] += nn(ctx_ref[m], wa[m, CTX:])
        return carry
    lax.fori_loop(0, mp, shard, 0)

    @pl.when(jnp.logical_not(decoding))
    def _():
        ffn_forward(total, mp, x1_ref, None, out_ref, h, a_ref, gp_ref, w1, w2, small_ref, vec_ref,
                    lambda b, m: load(b, m).wait())

        def memory(rows):
            mem_ref[rows] = norm(out_ref[rows], vec_ref[3:4], vec_ref[4:5]).astype(bf16)
        row_loop(total, 128, memory)


def middle_kernel(mp, utts, length, lens_ref, y1_ref, mem_ref, cot_ref, vec_ref, small_ref, w_ref,
                  out_ref, g_ref, dmem_ref, vg_ref, sg_ref, grad_ref,
                  wc, w1, w2, y2, h, hc, qkv, ctx, p, a, gp, dy, dyt, ht, memt, dh, dmem, du, dctx, w_sem, g_sem):
    decoding = lax.axis_index("section") == 1
    total = utts * length
    bufs = {1: wc, 2: w1, 3: w2}

    def load(b, m):
        return pltpu.make_async_copy(w_ref.at[m, b], bufs[b].at[m], w_sem.at[b, m])

    def store(b, m):
        return pltpu.make_async_copy(bufs[b].at[m], grad_ref.at[m, b], g_sem.at[b, m])

    @pl.when(decoding)
    def _():
        for b in (1, 2, 3):
            for m in range(mp):
                load(b, m).start()

        def prepare(rows):
            y1 = y1_ref[rows]
            hc[rows] = norm(y1, vec_ref[3:4], vec_ref[4:5]).astype(bf16)
            y2[rows] = y1
        row_loop(total, 128, prepare)
        limits = [jnp.full((1, length), lens_ref[u] - 1, jnp.int32) for u in range(utts)]
        even = even_lanes(total)
        T = LANES

        def shard(m, carry):
            load(1, m).wait()
            bias = small_ref[m, 1:2, :PROJ]
            pq = nt(hc[...], wc[m, :3 * T])
            pk = nt(mem_ref[...], wc[m, T:PROJ])
            qkv[m, :, 0:T] = ((pq[:, :T] + bias[:, :T]) * 0.125).astype(bf16)
            qkv[m, :, T:2 * T] = pk[:, :T].astype(bf16)
            qkv[m, :, 2 * T:3 * T] = jnp.where(even, (pq[:, 2 * T:] + bias[:, 2 * T:3 * T]) * 0.125,
                                               pk[:, T:2 * T] + bias[:, 2 * T:3 * T]).astype(bf16)
            qkv[m, :, 3 * T:4 * T] = (pk[:, 2 * T:3 * T] + bias[:, 3 * T:4 * T]).astype(bf16)
            qkv[m, :, 4 * T:] = pk[:, 3 * T:].astype(bf16)
            attend(m, length, utts, qkv, ctx, p, limits, None)
            y2[...] += nn(ctx[m], wc[m, CTX:])
            return carry
        lax.fori_loop(0, mp, shard, 0)

        ffn_forward(total, mp, y2, None, out_ref, h, a, gp, w1, w2, small_ref, vec_ref,
                    lambda b, m: load(b, m).wait())
        g_ref[...] = cot_ref[...].astype(f32)
        ffn_backward(total, mp, g_ref, y2, h, a, gp, w1, w2, dy, dyt, ht, dh, du, vec_ref, vg_ref, sg_ref,
                     lambda b, m: store(b, m).start())

        dy[...] = g_ref[...].astype(bf16)
        turn(dyt, dy[...])
        turn(ht, hc[...])
        turn(memt, mem_ref[...])
        dh[...] = jnp.zeros_like(dh)
        dmem[...] = jnp.zeros_like(dmem)

        def shard_back(m, carry):
            dctx[m] = nt(dy[...], wc[m, CTX:]).astype(bf16)
            attend_back(m, length, utts, qkv, p, dctx, qkv, None, None)
            d = qkv[m]
            sg_ref[m, 1:2, :PROJ] = jnp.sum(d.astype(f32), axis=0, keepdims=True)
            zero = jnp.zeros((total, T), bf16)
            mixed = d[:, 2 * T:3 * T]
            dq = jnp.concatenate([d[:, :T], jnp.where(even, mixed, zero)], axis=1)
            dkv = jnp.concatenate([d[:, T:2 * T], jnp.where(even, zero, mixed), d[:, 3 * T:]], axis=1)
            wq = jnp.concatenate([wc[m, :T], wc[m, 2 * T:3 * T]], axis=0)
            dh[...] += nn(dq, wq)
            dmem[...] += nn(dkv, wc[m, T:PROJ])
            gq = nn(ht[...], dq)
            gkv = nn(memt[...], dkv)
            go = nn(dyt[...], ctx[m])
            wc[m, :, :T] = gq[:, :T].astype(bf16)
            wc[m, :, T:2 * T] = gkv[:, :T].astype(bf16)
            wc[m, :, 2 * T:3 * T] = (gq[:, T:] + gkv[:, T:2 * T]).astype(bf16)
            wc[m, :, 3 * T:4 * T] = gkv[:, 2 * T:3 * T].astype(bf16)
            wc[m, :, 4 * T:5 * T] = (gkv[:, 3 * T:] + go[:, :T]).astype(bf16)
            wc[m, :, 5 * T:] = go[:, T:].astype(bf16)
            store(1, m).start()
            return carry
        lax.fori_loop(0, mp, shard_back, 0)
        dmem_ref[...] = dmem[...].astype(bf16)
        norm_back(total, y1_ref, vec_ref[3:4], dh, g_ref, vg_ref, 3)
        for b in (1, 2, 3):
            for m in range(mp):
                store(b, m).wait()


def backward_kernel(mp, utts, length, x_ref, x1_ref, out_ref, cot_ref, dmem_ref, cb_ref, g_in, vg_in, sg_in,
                    qkv, ctx, p, a, gp, vec_ref, w_ref, grad_in,
                    dx_ref, vg_ref, sg_ref, grad_ref,
                    wa, w1, w2, h, dy, dyt, ht, dh, du, dctx, dqkv, w_sem, g_sem):
    decoding = lax.axis_index("section") == 1
    total = utts * length
    bufs = {0: wa, 2: w1, 3: w2}

    def load(b, m):
        return pltpu.make_async_copy(w_ref.at[m, b], bufs[b].at[m], w_sem.at[b, m])

    def store(b, m):
        return pltpu.make_async_copy(bufs[b].at[m], grad_ref.at[m, b], g_sem.at[b, m])

    @pl.when(jnp.logical_not(decoding))
    def _():
        for m in range(mp):
            load(2, m).start()
            load(3, m).start()
    for m in range(mp):
        load(0, m).start()
    sg_ref[...] = jnp.zeros_like(sg_ref)

    @pl.when(decoding)
    def _():
        dx_ref[...] = g_in[...]
        vg_ref[...] = vg_in[...]
        sg_ref[:, 1:3, :] = sg_in[:, 1:3, :]

    @pl.when(jnp.logical_not(decoding))
    def _():
        sg_ref[:, 1:2, :PROJ] = cb_ref[...]
        dx_ref[...] = cot_ref[...].astype(f32)
        norm_back(total, out_ref, vec_ref[3:4], dmem_ref, dx_ref, vg_ref, 3)

        def prepare(rows):
            h[rows] = norm(x1_ref[rows], vec_ref[5:6], vec_ref[6:7]).astype(bf16)
        row_loop(total, 128, prepare)
        for m in range(mp):
            load(2, m).wait()
            load(3, m).wait()
        ffn_backward(total, mp, dx_ref, x1_ref, h, a, gp, w1, w2, dy, dyt, ht, dh, du, vec_ref, vg_ref, sg_ref,
                     lambda b, m: store(b, m).start())

    def prepare_self(rows):
        h[rows] = norm(x_ref[rows].astype(f32), vec_ref[0:1], vec_ref[1:2]).astype(bf16)
    row_loop(total, 128, prepare_self)
    vg_ref[2:3, :] = jnp.sum(dx_ref[...], axis=0, keepdims=True)
    dy[...] = dx_ref[...].astype(bf16)
    turn(dyt, dy[...])
    turn(ht, h[...])
    dh[...] = jnp.zeros_like(dh)
    down = lax.broadcasted_iota(jnp.int32, (length, length), 0)
    across = lax.broadcasted_iota(jnp.int32, (length, length), 1)
    flip = (down + across == length - 1).astype(f32).astype(bf16)
    T = LANES

    def shard(m, carry):
        load(0, m).wait()
        dctx[m] = nt(dy[...], wa[m, CTX:]).astype(bf16)
        attend_back(m, length, utts, qkv, p, dctx, dqkv, sg_ref, flip)
        d = dqkv[m]
        sg_ref[m, 0:1, :PROJ] = jnp.sum(d.astype(f32), axis=0, keepdims=True)
        dh[...] += nn(d, wa[m, :PROJ])
        gd = nn(ht[...], d)
        go = nn(dyt[...], ctx[m])
        wa[m, :, :CTX] = gd[:, :CTX].astype(bf16)
        wa[m, :, CTX:PROJ] = (gd[:, CTX:] + go[:, :T]).astype(bf16)
        wa[m, :, PROJ:] = go[:, T:].astype(bf16)
        store(0, m).start()
        return carry
    lax.fori_loop(0, mp, shard, 0)
    norm_back(total, x_ref, vec_ref[0:1], dh, dx_ref, vg_ref, 0)
    for m in range(mp):
        store(0, m).wait()

    @pl.when(jnp.logical_not(decoding))
    def _():
        for m in range(mp):
            store(2, m).wait()
            store(3, m).wait()


SMEM = pl.BlockSpec(memory_space=pltpu.SMEM)


def params(mib=60):
    return pltpu.CompilerParams(vmem_limit_bytes=mib * 2**20)


def forward(mp, utts, length, lens, x, vec, small, w):
    total, width = x.shape
    sds = jax.ShapeDtypeStruct
    shard = w.shape[2:]
    return pl.pallas_call(
        functools.partial(forward_kernel, mp, utts, length),
        out_shape=(sds((mp, total, PROJ), bf16), sds((mp, total, 2 * LANES), bf16),
                   sds((utts, mp, HEADS, length, length), bf16), sds((total, width), f32),
                   sds((mp, total, shard[1]), bf16), sds((mp, total, shard[1]), bf16),
                   sds((total, width), f32), sds((total, width), bf16)),
        in_specs=[SMEM, VM, VM, VM, ANY],
        out_specs=(VM,) * 8,
        scratch_shapes=[pltpu.VMEM((mp,) + shard, bf16)] * 3 + [pltpu.VMEM((total, width), bf16),
                                                               pltpu.SemaphoreType.DMA((BLOCKS, mp))],
        compiler_params=params(), name="layer_forward",
    )(lens, x, vec, small, w)


def middle(mp, utts, length, lens, y1, mem, cot, vec, small, w):
    total, width = y1.shape
    sds = jax.ShapeDtypeStruct
    shard = w.shape[2:]
    v = pltpu.VMEM
    sem = pltpu.SemaphoreType.DMA((BLOCKS, mp))
    return pl.pallas_call(
        functools.partial(middle_kernel, mp, utts, length),
        out_shape=(sds((total, width), f32), sds((total, width), f32), sds((total, width), bf16),
                   sds(vec.shape, f32), sds(small.shape, f32), sds(w.shape, bf16)),
        in_specs=[SMEM, VM, VM, VM, VM, VM, ANY],
        out_specs=(VM,) * 5 + (ANY,),
        scratch_shapes=[v((mp,) + shard, bf16)] * 3 + [
            v((total, width), f32), v((total, width), bf16), v((total, width), bf16),
            v((mp, total, PROJ), bf16), v((mp, total, 2 * LANES), bf16),
            v((utts, mp, HEADS, length, length), bf16),
            v((mp, total, shard[1]), bf16), v((mp, total, shard[1]), bf16),
            v((total, width), bf16), v((width, total), bf16), v((width, total), bf16), v((width, total), bf16),
            v((total, width), f32), v((total, width), f32), v((total, shard[1]), bf16),
            v((mp, total, 2 * LANES), bf16), sem, sem],
        compiler_params=params(), name="decoder_middle",
    )(lens, y1, mem, cot, vec, small, w)


def backward(mp, utts, length, x, x1, out, cot, dmem, cb, g, vg, sg, qkv, ctx, p, a, gp, vec, w, grads):
    total, width = x.shape
    sds = jax.ShapeDtypeStruct
    shard = w.shape[2:]
    v = pltpu.VMEM
    sem = pltpu.SemaphoreType.DMA((BLOCKS, mp))
    return pl.pallas_call(
        functools.partial(backward_kernel, mp, utts, length),
        out_shape=(sds((total, width), f32), sds(vec.shape, f32), sds(sg.shape, f32), sds(w.shape, bf16)),
        in_specs=[VM] * 15 + [ANY, ANY],
        out_specs=(VM, VM, VM, ANY),
        scratch_shapes=[v((mp,) + shard, bf16)] * 3 + [
            v((total, width), bf16), v((total, width), bf16), v((width, total), bf16), v((width, total), bf16),
            v((total, width), f32), v((total, shard[1]), bf16),
            v((mp, total, 2 * LANES), bf16), v((mp, total, PROJ), bf16), sem, sem],
        input_output_aliases={16: 3},
        compiler_params=params(), name="layer_backward",
    )(x, x1, out, cot, dmem, cb, g, vg, sg, qkv, ctx, p, a, gp, vec, w, grads)


def pack_rows(q, k, v, o):
    parts = [q[0:64], q[64:128], k[0:64], k[64:128], q[128:192], v[0:64],
             v[64:128], v[128:192], k[128:192], o[0:64], o[64:128], o[128:192]]
    return jnp.concatenate(parts, axis=0)


def take_slots(values, slots):
    return jnp.concatenate([values[..., 64 * s:64 * s + 64] for s in slots], axis=-1)


def rel_line(table, length):
    half = table.shape[1] // 2
    heads = table.shape[0]
    first = jnp.broadcast_to(table[:, :1], (heads, length - half))
    last = jnp.broadcast_to(table[:, -1:], (heads, length - half))
    return jnp.concatenate([table[:, :half + 1][:, ::-1], first, last, table[:, half + 1:][:, ::-1]], axis=1)


def rel_fold(line, rel):
    length = line.shape[-1] // 2
    half = rel // 2
    low = length - 1 + half
    high = length - half + 1
    return jnp.concatenate([jnp.sum(line[..., low:], axis=-1, keepdims=True), line[..., high:low][..., ::-1],
                            jnp.sum(line[..., :high], axis=-1, keepdims=True)], axis=-1)


def per_device(streams, lengths, vectors, attn_in, attn_bias, attn_out, rel_table, cross, ffn_in, ffn_bias, ffn_out,
               cotangent):
    section = lax.axis_index("section")
    decoding = section == 1
    mp = lax.axis_size("mp")
    dp = lax.axis_size("dp")
    me = lax.axis_index("mp")
    utts, length, width = streams.shape[1:]
    total = utts * length
    rel = rel_table.shape[2]
    x = streams[0].reshape(total, width)
    cot = cotangent[0].reshape(total, width)
    vec = vectors[0]

    lens = lax.dynamic_slice_in_dim(lengths, me * utts, utts, 1)
    own_lens = jnp.where(decoding, lens[1], lens[0])
    frame_lens = lens[0]

    w_in = jnp.swapaxes(attn_in[0], 1, 2)
    w_cross = jnp.swapaxes(cross[0], 1, 2)
    pack_a = pack_rows(w_in[0], w_in[1], w_in[2], attn_out[0])
    pack_c = pack_rows(w_cross[0], w_cross[0], w_cross[1], w_cross[1])
    b_in = attn_bias[0].reshape(3, -1)
    none = jnp.zeros_like(b_in[0])

    def bias_row(q, v):
        return pack_rows(q[:, None], none[:, None], v[:, None], none[:, None])[:, 0]

    ext = rel_line(rel_table[0], length)
    ext = jnp.pad(ext, ((0, 0), (0, width - ext.shape[1])))
    cross_row = bias_row(b_in[2], b_in[2])
    ahead = [(0, 1)]
    got_c, got_row = lax.ppermute((pack_c, cross_row), "section", ahead)
    row_slot = jnp.arange(width) // 64
    from_memory = (row_slot == 2) | (row_slot == 3) | (row_slot == 5) | (row_slot == 6) | (row_slot == 7) | (row_slot == 8)
    pack_c = jnp.where(from_memory[:, None], got_c, pack_c)
    cross_row = jnp.where(from_memory, got_row, cross_row)
    small = jnp.concatenate([bias_row(b_in[0], b_in[1])[None], cross_row[None], ffn_bias[0].reshape(1, -1), ext,
                             jnp.zeros((2, width), f32)], axis=0)

    weights, smalls = gather_weights(mp, pack_a, pack_c, ffn_in[0], ffn_out[0], small)
    qkv, ctx, p, x1, a, gp, enc_out, mem = forward(mp, utts, length, own_lens, x, vec, smalls, weights)
    mem = lax.ppermute(mem, "section", ahead)
    dec_out, g_dec, dmem, vg, sg, grads = middle(mp, utts, length, frame_lens, x1, mem, cot, vec, smalls, weights)
    dmem, cb = lax.ppermute((dmem, sg[:, 1:2, :PROJ]), "section", [(1, 0)])
    dx, vg, sg, grads = backward(mp, utts, length, x, x1, enc_out, cot, dmem, cb, g_dec, vg, sg, qkv, ctx, p, a, gp,
                                 vec, weights, grads)

    spread = mp * dp
    vg_part = jnp.moveaxis(vg.reshape(8, dp, mp, width // spread), 0, 2).reshape(dp, mp, -1)

    def to_targets(values):
        k, n = values.shape[1:]
        return jnp.transpose(values.reshape(mp, k, dp, n // dp), (2, 0, 1, 3)).reshape(dp, mp, -1)

    rows_a, rows_c = sg[:, 0, :PROJ], sg[:, 1, :PROJ]
    cross_bias = jnp.where(decoding, take_slots(rows_c, Q_SLOTS), take_slots(rows_c, V_SLOTS))
    bias_part = jnp.concatenate([take_slots(rows_a, Q_SLOTS), take_slots(rows_a, V_SLOTS), cross_bias], axis=1)
    rel_part = rel_fold(sg[:, 3:3 + HEADS, :2 * length], rel)
    b1_part = sg[:, 2, :]
    pieces = [vg_part, to_targets(bias_part.reshape(mp, 9, 64)), to_targets(rel_part),
              to_targets(b1_part.reshape(mp, -1, 128))]
    sizes = [piece.shape[-1] for piece in pieces]
    packed = jnp.concatenate(pieces, axis=-1)
    packed = jnp.pad(packed, ((0, 0), (0, 0), (0, 1024 - sum(sizes)))).reshape(spread, 8, 128)

    own, small_sum = scatter_grads(mp, dp, grads, packed)
    if dp > 4:
        per = dp // 4
        groups = [[q * per + i for i in range(per)] for q in range(4)]
        own = lax.psum_scatter(own.astype(bf16), "dp", scatter_dimension=1, axis_index_groups=groups,
                               tiled=True).astype(f32)
    flat = small_sum.reshape(-1)
    cuts = []
    start = 0
    for size in sizes:
        cuts.append(flat[start:start + size])
        start += size
    vectors_grad = cuts[0].reshape(1, 8, -1)
    bias_grad = cuts[1].reshape(1, 3, HEADS, -1)
    rel_grad = cuts[2].reshape(1, HEADS, -1)
    b1_grad = cuts[3].reshape(1, -1, 128 // dp)

    pa, pc = own[0], own[1]
    attn_in_grad = jnp.stack([take_slots(pa, Q_SLOTS), take_slots(pa, K_SLOTS), take_slots(pa, V_SLOTS)])[None]
    attn_out_grad = take_slots(pa, O_SLOTS).T[None]
    for_memory = jnp.stack([take_slots(pc, K_SLOTS), take_slots(pc, V_SLOTS)])
    got = lax.ppermute(for_memory.astype(bf16), "section", [(1, 0)]).astype(f32)
    cross_grad = jnp.where(decoding, jnp.stack([take_slots(pc, Q_SLOTS), take_slots(pc, O_SLOTS)]), got)[None]
    shape = (1, utts, length, width)
    return (jnp.where(decoding, dec_out, enc_out).reshape(shape), dx.reshape(shape), vectors_grad, attn_in_grad,
            bias_grad, attn_out_grad, rel_grad, cross_grad, own[2][None], b1_grad, own[3].T[None])


def solution(mesh):
    placed = (
        P("section", ("dp", "mp"), None, None),
        P(None, "dp"),
        P("section", None, None),
        P("section", None, None, "mp"),
        P("section", None, "mp", None),
        P("section", "mp", None),
        P("section", "mp", None),
        P("section", None, None, "mp"),
        P("section", None, "mp"),
        P("section", "mp", None),
        P("section", "mp", None),
        P("section", ("dp", "mp"), None, None),
    )
    return jax.shard_map(
        per_device,
        mesh=mesh,
        in_specs=placed,
        out_specs=(
            P("section", ("dp", "mp"), None, None),
            P("section", ("dp", "mp"), None, None),
            P("section", None, ("dp", "mp")),
            P("section", None, "dp", "mp"),
            P("section", None, "mp", "dp"),
            P("section", "mp", "dp"),
            P("section", "mp", "dp"),
            P("section", None, "dp", "mp"),
            P("section", "dp", "mp"),
            P("section", "mp", "dp"),
            P("section", "mp", "dp"),
        ),
        check_vma=False,
    )
```

```python
import functools
import jax
import jax.numpy as jnp
from jax import lax
from jax.experimental import pallas as pl
from jax.experimental.pallas import tpu as pltpu
from jax.sharding import PartitionSpec as P

MESH = pl.DeviceIdType.MESH
ANY = pl.BlockSpec(memory_space=pl.ANY)
VM = pl.BlockSpec(memory_space=pltpu.VMEM)
BLOCKS = 4


def partners(dp_index, step):
    bit = lax.rem(dp_index // step, 2)
    return dp_index + step - 2 * step * bit


EPSILON = 1e-05
MASKED = -1e30
HEADS = 3
LANES = 128
Q_SLOTS, K_SLOTS, V_SLOTS, O_SLOTS = (0, 1, 4), (2, 3, 8), (5, 6, 7), (9, 10, 11)
PROJ = 640
CTX = 512
bf16, f32 = jnp.bfloat16, jnp.float32


def nn(a, b):
    return lax.dot_general(a, b, (((1,), (0,)), ((), ())), preferred_element_type=f32)


def nt(a, b):
    return lax.dot_general(a, b, (((1,), (1,)), ((), ())), preferred_element_type=f32)


def tn(a, b):
    return lax.dot_general(a, b, (((0,), (0,)), ((), ())), preferred_element_type=f32)


def norm_parts(x):
    centred = x - jnp.mean(x, axis=-1, keepdims=True)
    r = lax.rsqrt(jnp.mean(centred * centred, axis=-1, keepdims=True) + EPSILON)
    return centred * r, r


def norm(x, gain, shift):
    xh, _ = norm_parts(x)
    return xh * gain + shift


def row_loop(total, size, body):
    def step(i, carry):
        body(pl.ds(pl.multiple_of(i * size, size), size))
        return carry
    lax.fori_loop(0, total // size, step, 0)


def even_lanes(rows):
    return lax.broadcasted_iota(jnp.int32, (rows, LANES), 1) < LANES // 2


def half_mask(half):
    lane = lax.broadcasted_iota(jnp.int32, (1, LANES), 1)
    on = (lane < LANES // 2) if half == 0 else (lane >= LANES // 2)
    return on.astype(f32).astype(bf16)


def slot_row(slots):
    lane = lax.broadcasted_iota(jnp.int32, (1, PROJ), 1)
    on = lane < 0
    for s in slots:
        on = on | ((lane >= 64 * s) & (lane < 64 * s + 64))
    return on


def tile(ref, m, rows, t):
    return ref[m, rows, t * LANES:(t + 1) * LANES]


HEAD_TILES = (((0, 0), (1, 0), (2, 1), (0, 1)),
              ((0, 1), (1, 1), (3, 0), (1, 0)),
              ((2, 0), (4, 0), (3, 1), (1, 1)))


def attend(m, length, utts, qkv_ref, ctx_ref, p_ref, limits, ext_ref):
    key_at = lax.broadcasted_iota(jnp.int32, (length, length), 0)
    even = even_lanes(length)
    parts = {u: [None] * HEADS for u in utts}
    for r in range(HEADS):
        (qt, half), (kt, _), (vt, _), _ = HEAD_TILES[r]
        if ext_ref is not None:
            row = ext_ref[m, 3 + r:4 + r, :2 * length]
            bias = pltpu.roll(jnp.broadcast_to(row, (length, 2 * length)), 0, 1, stride=1, stride_axis=0)[:, :length]
        for u in utts:
            rows = pl.ds(u * length, length)
            s = nt(tile(qkv_ref, m, rows, kt) * half_mask(half), tile(qkv_ref, m, rows, qt))
            if ext_ref is not None:
                s = s + bias
            s = jnp.where(key_at <= limits[u], s, MASKED)
            e = jnp.exp(s - jnp.max(s, axis=0, keepdims=True))
            p = (e * (1.0 / jnp.sum(e, axis=0, keepdims=True))).astype(bf16)
            p_ref[u, m, r] = p
            parts[u][r] = tn(p, tile(qkv_ref, m, rows, vt))
    for u in utts:
        rows = pl.ds(u * length, length)
        ctx_ref[m, rows, :LANES] = jnp.where(even, 0.0, parts[u][0]).astype(bf16)
        ctx_ref[m, rows, LANES:] = jnp.where(even, parts[u][1], parts[u][2]).astype(bf16)


def attend_back(m, length, utts, qkv_ref, p_ref, dctx_ref, out_ref, rel_ref, flip):
    even = even_lanes(length)
    got = {u: [None] * HEADS for u in utts}
    for r in range(HEADS):
        (qt, _), (kt, _), (vt, vhalf), (ot, _) = HEAD_TILES[r]
        total = None
        for u in utts:
            rows = pl.ds(u * length, length)
            p = p_ref[u, m, r]
            dctx = tile(dctx_ref, m, rows, ot)
            dp = nt(tile(qkv_ref, m, rows, vt) * half_mask(vhalf), dctx)
            pf = p.astype(f32)
            t = pf * dp
            ds = (t - pf * jnp.sum(t, axis=0, keepdims=True)).astype(bf16)
            got[u][r] = (tn(ds, tile(qkv_ref, m, rows, kt)) * 0.125, nn(ds, tile(qkv_ref, m, rows, qt)), nn(p, dctx))
            if rel_ref is not None:
                turned = nn(flip, ds)
                total = turned if total is None else total + turned
        if rel_ref is not None:
            wide = jnp.concatenate([total, jnp.zeros_like(total)], axis=1)
            wide = pltpu.roll(wide, 0, 1, stride=1, stride_axis=0)
            rel_ref[m, 3 + r:4 + r, :2 * length] = jnp.sum(wide, axis=0, keepdims=True)
    for u in utts:
        rows = pl.ds(u * length, length)
        (q0, k0, v0), (q1, k1, v1), (q2, k2, v2) = got[u]
        for t, (left, right) in enumerate(((q0, q1), (k0, k1), (q2, v0), (v1, v2), (k2, 0.0))):
            out_ref[m, rows, t * LANES:(t + 1) * LANES] = jnp.where(even, left, right).astype(bf16)


def gelu_both(u):
    cdf = 0.5 + 0.5 * lax.erf(u * 0.7071067811865476)
    return u * cdf, cdf + u * (jnp.exp(-0.5 * u * u) * 0.3989422804014327)


def norm_back(total, x_ref, gain, dh_ref, add_into, vg_ref, gain_row, grad_out=None):
    width = gain.shape[-1]

    def step(i, carry):
        dgain, dshift = carry
        rows = pl.ds(pl.multiple_of(i * 128, 128), 128)
        dh = dh_ref[rows].astype(f32)
        xh, r = norm_parts(x_ref[rows].astype(f32))
        e = dh * gain
        dx = r * (e - jnp.mean(e, axis=-1, keepdims=True) - xh * jnp.mean(e * xh, axis=-1, keepdims=True))
        add_into[rows] = add_into[rows].astype(f32) + dx
        return dgain + jnp.sum(dh * xh, axis=0, keepdims=True), dshift + jnp.sum(dh, axis=0, keepdims=True)

    zero = jnp.zeros((1, width), f32)
    dgain, dshift = lax.fori_loop(0, total // 128, step, (zero, zero))
    vg_ref[gain_row:gain_row + 1, :] = dgain
    vg_ref[gain_row + 1:gain_row + 2, :] = dshift


def turn(dst_ref, src):
    dst_ref[...] = src.T


SMEM = pl.BlockSpec(memory_space=pltpu.SMEM)


SEQUENCE = ((0, 1), (1, 1), (2, 1), (0, 2), (1, 2), (3, 1), (0, 3), (1, 3), (2, 2), (3, 2), (2, 3), (3, 3))


def wide_dot(dot, a, b_ref_cols, width, use, step=256):
    for start in range(0, width, step):
        size = min(step, width - start)
        use(slice(start, start + size), dot(a, b_ref_cols(start, size)))


def ffn_shard(m, h, w1, w2, a, gp, bias, out):
    def keep(cols, u):
        act, slope = gelu_both(u + bias[:, cols])
        a[m, :, cols] = act.astype(bf16)
        gp[m, :, cols] = slope.astype(bf16)
    wide_dot(nn, h[...], lambda s, n: w1[m, :, s:s + n], w1.shape[2], keep)
    out[...] += nn(a[m], w2[m])


def ffn_start(total, x_ref, out_ref, h_ref, vec_ref):
    def prepare(rows):
        x = x_ref[rows]
        h_ref[rows] = norm(x, vec_ref[5:6], vec_ref[6:7]).astype(bf16)
        out_ref[rows] = x + vec_ref[7:8]
    row_loop(total, 256, prepare)


def forward_kernel(mp, utts, length,
                   lens_ref, x_ref, cot_ref, vec_ref, small_ref, in_ref, o_ref, cross_ref, w1_ref, w2_ref,
                   qkv, ctx, p, x1, a, gp, out, g, vg, sg, grad_ref, w_out,
                   wa, wc, w1, w2, smalls, peer_small, h, mem, dmem, sg_got,
                   qkvc, ctxc, pc, y2, hc, dy, dyc, dyt, ht, dh, dmem_sum, dctx,
                   l_sem, z_send, z_recv, p_send, p_recv, s_send, s_recv, x_send, x_recv, k_sem, g_sem):
    me = lax.axis_index("mp")
    dp_index = lax.axis_index("dp")
    section = lax.axis_index("section")
    decoding = section == 1
    encoding = section == 0
    core = partners(dp_index, 1)
    side = partners(dp_index, 2)
    quarter = lax.rem(dp_index, 4)
    side_quarter = quarter + 2 - 4 * (quarter // 2)
    core_quarter = quarter + 1 - 2 * lax.rem(quarter, 2)
    diag_quarter = core_quarter + 2 - 4 * (core_quarter // 2)
    part = wa.shape[1] // 4
    total = utts * length
    T = LANES
    bufs = (wa, wc, w1, w2)

    barrier = pltpu.get_barrier_semaphore()
    for hop in range(1, mp):
        pl.semaphore_signal(barrier, inc=1, device_id={"mp": lax.rem(me + hop, mp)}, device_id_type=MESH)
    for other in (core, side):
        pl.semaphore_signal(barrier, inc=1, device_id={"dp": other}, device_id_type=MESH)
    pl.semaphore_signal(barrier, inc=1, device_id={"section": 1 - section}, device_id_type=MESH)
    pl.semaphore_wait(barrier, mp + 2)

    def rows(which):
        return pl.ds(pl.multiple_of(which * part, 16), part)

    def along(src, shard, b, way, dist):
        return pltpu.make_async_remote_copy(
            src_ref=src, dst_ref=bufs[b].at[shard, rows(quarter)],
            send_sem=z_send.at[way, dist - 1, b], recv_sem=z_recv.at[way, dist - 1, b],
            device_id={"mp": me + 1 - 2 * way}, device_id_type=MESH)

    def across(kind, shard, b, which, way, dist, to):
        ref = bufs[b].at[shard, rows(which)]
        return pltpu.make_async_remote_copy(
            src_ref=ref, dst_ref=ref,
            send_sem=p_send.at[kind, way, dist - 1, b], recv_sem=p_recv.at[kind, way, dist - 1, b],
            device_id={"dp": to}, device_id_type=MESH)

    def small_copy(hop, slot):
        return pltpu.make_async_remote_copy(
            src_ref=smalls.at[me], dst_ref=smalls.at[slot],
            send_sem=s_send.at[hop - 1], recv_sem=s_recv.at[hop - 1],
            device_id={"mp": lax.rem(me + hop, mp)}, device_id_type=MESH)

    def over(index, src, dst):
        return pltpu.make_async_remote_copy(
            src_ref=src, dst_ref=dst, send_sem=x_send.at[index], recv_sem=x_recv.at[index],
            device_id={"section": 1 - section}, device_id_type=MESH)

    memory_rows = ((128, 256), (320, 576))

    def over_rows(i):
        low, high = memory_rows[i]
        ref = wc.at[me, low:high]
        return over(i, ref, ref)

    def utt(u):
        return pl.ds(u * length, length)

    def needed(b):
        return decoding if b == 1 else me >= 0

    def has_next(way):
        return (me < mp - 1) if way == 0 else (me > 0)

    def has_shard(way, dist):
        return (me >= dist) if way == 0 else (me + dist <= mp - 1)

    def shard_at(way, dist):
        return me - dist if way == 0 else me + dist

    own_src = {0: wa.at[me, rows(quarter)], 1: wc.at[me, rows(quarter)],
               2: w1_ref.at[rows(quarter)], 3: w2_ref.at[rows(quarter)]}

    def own_send(b):
        for way in (0, 1):
            @pl.when(needed(b) & has_next(way))
            def _():
                along(own_src[b], me, b, way, 1).start()

    def local(b):
        return pltpu.make_async_copy((None, None, w1_ref, w2_ref)[b], bufs[b].at[me], l_sem.at[b])

    q_rows, k_rows, v_rows = in_ref[0].T, in_ref[1].T, in_ref[2].T
    wa[me, 0:128] = q_rows[0:128]
    wa[me, 128:256] = k_rows[0:128]
    wa[me, 256:320] = q_rows[128:192]
    wa[me, 320:384] = v_rows[0:64]
    wa[me, 384:512] = v_rows[64:192]
    wa[me, 512:576] = k_rows[128:192]
    wa[me, 576:768] = o_ref[...]
    own_send(0)
    first, second = cross_ref[0].T, cross_ref[1].T

    @pl.when(encoding)
    def _():
        wc[me, 128:256] = first[0:128]
        wc[me, 320:512] = second[0:192]
        wc[me, 512:576] = first[128:192]
        for i in (0, 1):
            over_rows(i).start()
        over(2, small_ref, peer_small).start()
        smalls[me] = small_ref[...]

    @pl.when(decoding)
    def _():
        wc[me, 0:128] = first[0:128]
        wc[me, 256:320] = first[128:192]
        wc[me, 576:768] = second[0:192]
        over(2, small_ref, peer_small).wait_recv()
        smalls[me] = small_ref[...]
        lane = lax.broadcasted_iota(jnp.int32, (1, small_ref.shape[1]), 1)
        value_lane = (lane >= 320) & (lane < 512)
        smalls[me, 1:2] = jnp.where(value_lane, peer_small[1:2], small_ref[1:2])
        for i in (0, 1):
            over_rows(i).wait_recv()
    own_send(1)
    own_send(2)
    for hop in range(1, mp):
        small_copy(hop, me).start()
    for b in (2, 3):
        local(b).start()

    def on_line(k):
        b, dist = SEQUENCE[k]
        for way in (0, 1):
            @pl.when(needed(b) & has_shard(way, dist))
            def _():
                shard = shard_at(way, dist)
                src = bufs[b].at[shard, rows(quarter)]
                along(src, shard, b, way, dist).wait_recv()
                if dist < mp - 1:
                    @pl.when(has_next(way))
                    def _():
                        along(src, shard, b, way, dist + 1).start()
                across(1, shard, b, quarter, way, dist, side).start()
                across(0, shard, b, quarter, way, dist, core).start()
        if k == 0:
            own_send(3)

    def on_side(k):
        b, dist = SEQUENCE[k]
        for way in (0, 1):
            @pl.when(needed(b) & has_shard(way, dist))
            def _():
                shard = shard_at(way, dist)
                across(1, shard, b, side_quarter, way, dist, side).wait_recv()
                across(2, shard, b, side_quarter, way, dist, core).start()

    def complete(k):
        b, dist = SEQUENCE[k]
        for way in (0, 1):
            @pl.when(needed(b) & has_shard(way, dist))
            def _():
                shard = shard_at(way, dist)
                across(0, shard, b, core_quarter, way, dist, core).wait_recv()
                across(2, shard, b, diag_quarter, way, dist, core).wait_recv()

    def service(k):
        for act, lag in ((on_line, 0), (on_side, 1), (complete, 2)):
            if 0 <= k - lag < len(SEQUENCE):
                act(k - lag)

    def prepare(rws):
        x = x_ref[rws].astype(f32)
        h[rws] = norm(x, vec_ref[0:1], vec_ref[1:2]).astype(bf16)
        x1[rws] = x + vec_ref[2:3]
    row_loop(total, 256, prepare)
    for hop in range(1, mp):
        small_copy(hop, lax.rem(me + mp - hop, mp)).wait_recv()

    query_at = lax.broadcasted_iota(jnp.int32, (1, length), 1)
    limits, frames = [], []
    for u in range(utts):
        last = lens_ref[u] - 1
        limits.append(jnp.where(decoding, jnp.minimum(query_at, last), last))
        frames.append(jnp.full((1, length), lens_ref[utts + u] - 1, jnp.int32))
    scale = jnp.where(slot_row(Q_SLOTS), 0.125, 1.0)

    def self_shard(m, carry):
        def keep(cols, value):
            qkv[m, :, cols] = ((value + smalls[m, 0:1, cols]) * scale[:, cols]).astype(bf16)
        wide_dot(nt, h[...], lambda s, n: wa[m, s:s + n], PROJ, keep)
        attend(m, length, range(utts), qkv, ctx, p, limits, smalls)
        x1[...] += nn(ctx[m], wa[m, CTX:])
        return carry

    for k in range(8):
        service(k)
    complete(6)
    lax.fori_loop(0, mp // 2, self_shard, 0)
    on_line(8)
    on_side(7)
    lax.fori_loop(mp // 2, mp, self_shard, 0)
    service(9)
    for b in (2, 3):
        local(b).wait()

    def ffn_one(m):
        ffn_shard(m, h, w1, w2, a, gp, smalls[m, 2:3], out)

    def ffn_at(dist):
        @pl.when(encoding)
        def _():
            def step(way, carry):
                @pl.when(jnp.where(way == 0, me >= dist, me + dist <= mp - 1))
                def _():
                    ffn_one(jnp.where(way == 0, me - dist, me + dist))
                return carry
            lax.fori_loop(0, 2, step, 0)

    def keep_weights(b, m):
        return pltpu.make_async_copy(bufs[b].at[m], w_out.at[m, b], k_sem.at[b, m])

    for m in range(mp):
        keep_weights(0, m).start()

    @pl.when(encoding)
    def _():
        ffn_start(total, x1, out, h, vec_ref)
        ffn_one(me)

    @pl.when(decoding)
    def _():
        def start_cross(rws):
            y = x1[rws]
            hc[rws] = norm(y, vec_ref[3:4], vec_ref[4:5]).astype(bf16)
            y2[rws] = y
        row_loop(total, 256, start_cross)

    service(10)
    ffn_at(1)

    @pl.when(decoding)
    def _():
        def queries(m, carry):
            bias = smalls[m, 1:2, :PROJ]
            pq = nt(hc[...], jnp.concatenate([wc[m, :T], wc[m, 2 * T:3 * T]], axis=0))
            qkvc[m, :, 0:T] = ((pq[:, :T] + bias[:, :T]) * 0.125).astype(bf16)
            qkvc[m, :, 2 * T:3 * T] = ((pq[:, T:] + bias[:, 2 * T:3 * T]) * 0.125).astype(bf16)
            return carry
        lax.fori_loop(0, mp, queries, 0)

    service(11)
    ffn_at(2)
    service(12)
    service(13)
    ffn_at(3)

    @pl.when(encoding)
    def _():
        for u in range(utts):
            mem[utt(u)] = norm(out[utt(u)], vec_ref[3:4], vec_ref[4:5]).astype(bf16)
            over(3 + u, mem.at[utt(u)], mem.at[utt(u)]).start()
        for b in (2, 3):
            for m in range(mp):
                keep_weights(b, m).start()
        g[...] = cot_ref[...].astype(f32)
        for u in range(utts):
            over(3 + utts + u, dmem.at[utt(u)], dmem.at[utt(u)]).wait_recv()
        norm_back(total, out, vec_ref[3:4], dmem, g, vg, 3)
        over(3 + 2 * utts, sg_got, sg_got).wait_recv()
        sg[...] = sg_got[...]

    def drain():
        for hop in range(1, mp):
            small_copy(hop, me).wait_send()
        for b in range(BLOCKS):
            for way in (0, 1):
                @pl.when(needed(b) & has_next(way))
                def _():
                    along(own_src[b], me, b, way, 1).wait_send()
        for b, dist in SEQUENCE:
            for way in (0, 1):
                @pl.when(needed(b) & has_shard(way, dist))
                def _():
                    shard = shard_at(way, dist)
                    across(0, shard, b, quarter, way, dist, core).wait_send()
                    across(1, shard, b, quarter, way, dist, side).wait_send()
                    across(2, shard, b, side_quarter, way, dist, core).wait_send()
                    if dist < mp - 1:
                        @pl.when(has_next(way))
                        def _():
                            along(bufs[b].at[shard, rows(quarter)], shard, b, way, dist + 1).wait_send()

    def store(b, m):
        return pltpu.make_async_copy(bufs[b].at[m], grad_ref.at[m, b], g_sem.at[b, m])

    @pl.when(decoding)
    def _():
        even = even_lanes(length)
        for u in range(utts):
            over(3 + u, mem.at[utt(u)], mem.at[utt(u)]).wait_recv()
            rws = slice(u * length, (u + 1) * length)

            def cross_shard(m, carry):
                bias = smalls[m, 1:2, :PROJ]
                pk = nt(mem[rws], wc[m, T:PROJ])
                qkvc[m, rws, T:2 * T] = pk[:, :T].astype(bf16)
                qkvc[m, rws, 2 * T:3 * T] = jnp.where(even, qkvc[m, rws, 2 * T:3 * T].astype(f32),
                                                      pk[:, T:2 * T] + bias[:, 2 * T:3 * T]).astype(bf16)
                qkvc[m, rws, 3 * T:4 * T] = (pk[:, 2 * T:3 * T] + bias[:, 3 * T:4 * T]).astype(bf16)
                qkvc[m, rws, 4 * T:] = pk[:, 3 * T:].astype(bf16)
                attend(m, length, (u,), qkvc, ctxc, pc, frames, None)
                y2[rws] += nn(ctxc[m, rws], wc[m, CTX:])
                return carry
            lax.fori_loop(0, mp, cross_shard, 0)

        ffn_start(total, y2, out, h, vec_ref)

        def one(m, carry):
            ffn_one(m)
            return carry
        lax.fori_loop(0, mp, one, 0)
        g[...] = cot_ref[...].astype(f32)
        ffn_dgrad(total, mp, g, y2, gp, w1, w2, dy, dh, vec_ref, vg, sg)

        dyc[...] = g[...].astype(bf16)
        dh[...] = jnp.zeros_like(dh)
        zero = jnp.zeros((length, T), bf16)
        for u in range(utts):
            rws = slice(u * length, (u + 1) * length)
            dmem_sum[...] = jnp.zeros_like(dmem_sum)

            def cross_back(m, carry):
                dctx[m, rws] = nt(dyc[rws], wc[m, CTX:]).astype(bf16)
                attend_back(m, length, (u,), qkvc, pc, dctx, qkvc, None, None)
                d = qkvc[m, rws]
                mixed = d[:, 2 * T:3 * T]
                dq = jnp.concatenate([d[:, :T], jnp.where(even, mixed, zero)], axis=1)
                dkv = jnp.concatenate([d[:, T:2 * T], jnp.where(even, zero, mixed), d[:, 3 * T:]], axis=1)
                dmem_sum[...] += nn(dkv, wc[m, T:PROJ])
                dh[rws] += nn(dq, jnp.concatenate([wc[m, :T], wc[m, 2 * T:3 * T]], axis=0))
                return carry
            lax.fori_loop(0, mp, cross_back, 0)
            dmem[utt(u)] = dmem_sum[...].astype(bf16)
            over(3 + utts + u, dmem.at[utt(u)], dmem.at[utt(u)]).start()

        def row_sums(m, carry):
            sg[m, 1:2, :PROJ] = jnp.sum(qkvc[m].astype(f32), axis=0, keepdims=True)
            return carry
        lax.fori_loop(0, mp, row_sums, 0)
        over(3 + 2 * utts, sg, sg_got).start()
        norm_back(total, x1, vec_ref[3:4], dh, g, vg, 3)

        drain()
        turn(dyt, dy[...])
        turn(ht, h[...])

        def ffn_weights(m, carry):
            w2[m] = nn(dyt[...], a[m]).astype(bf16)
            store(3, m).start()
            w1[m] = nn(ht[...], gp[m]).astype(bf16)
            store(2, m).start()
            return carry
        lax.fori_loop(0, mp, ffn_weights, 0)
        turn(dyt, dyc[...])
        turn(ht, hc[...])
        wide_even = even_lanes(total)
        wide_zero = jnp.zeros((total, T), bf16)

        def cross_weights(m, carry):
            d = qkvc[m]
            mixed = d[:, 2 * T:3 * T]
            dq = jnp.concatenate([d[:, :T], jnp.where(wide_even, mixed, wide_zero)], axis=1)
            dkv = jnp.concatenate([d[:, T:2 * T], jnp.where(wide_even, wide_zero, mixed), d[:, 3 * T:]], axis=1)
            gq = nn(ht[...], dq)
            gkv = tn(mem[...], dkv)
            go = nn(dyt[...], ctxc[m])
            wc[m, :, :T] = gq[:, :T].astype(bf16)
            wc[m, :, T:2 * T] = gkv[:, :T].astype(bf16)
            wc[m, :, 2 * T:3 * T] = (gq[:, T:] + gkv[:, T:2 * T]).astype(bf16)
            wc[m, :, 3 * T:4 * T] = gkv[:, 2 * T:3 * T].astype(bf16)
            wc[m, :, 4 * T:5 * T] = (gkv[:, 3 * T:] + go[:, :T]).astype(bf16)
            wc[m, :, 5 * T:] = go[:, T:].astype(bf16)
            store(1, m).start()
            return carry
        lax.fori_loop(0, mp, cross_weights, 0)

    for m in range(mp):
        keep_weights(0, m).wait()

    @pl.when(encoding)
    def _():
        for b in (2, 3):
            for m in range(mp):
                keep_weights(b, m).wait()
        for i in (0, 1):
            over_rows(i).wait_send()
        over(2, small_ref, peer_small).wait_send()
        for u in range(utts):
            over(3 + u, mem.at[utt(u)], mem.at[utt(u)]).wait_send()

    @pl.when(decoding)
    def _():
        for b in (1, 2, 3):
            for m in range(mp):
                store(b, m).wait()
        for u in range(utts):
            over(3 + utts + u, dmem.at[utt(u)], dmem.at[utt(u)]).wait_send()
        over(3 + 2 * utts, sg, sg_got).wait_send()

    @pl.when(encoding)
    def _():
        drain()


def ffn_dgrad(total, mp, g, x_ref, gp, w1, w2, dy, dh, vec_ref, vg, sg):
    vg[7:8, :] = jnp.sum(g[...], axis=0, keepdims=True)
    dy[...] = g[...].astype(bf16)
    dh[...] = jnp.zeros_like(dh)

    def shard(m, carry):
        ffn_dgrad_shard(m, gp, w1, w2, dy, dh, sg)
        return carry
    lax.fori_loop(0, mp, shard, 0)
    norm_back(total, x_ref, vec_ref[5:6], dh, g, vg, 5)


def ffn_dgrad_shard(m, gp, w1, w2, dy, dh, sg):
    def keep(cols, da):
        du = (da * gp[m, :, cols].astype(f32)).astype(bf16)
        gp[m, :, cols] = du
        sg[m, 2:3, cols] = jnp.sum(du.astype(f32), axis=0, keepdims=True)
    wide_dot(nt, dy[...], lambda s, n: w2[m, s:s + n], w2.shape[1], keep)
    dh[...] += nt(gp[m], w1[m])


def forward(mp, utts, length, lens, x, cot, vec, small, w_in, w_o, w_cross, w_one, w_two):
    total, width = x.shape
    hidden = w_one.shape[1]
    sds = jax.ShapeDtypeStruct
    v = pltpu.VMEM
    sem = pltpu.SemaphoreType.DMA
    shard = (mp, width, hidden)
    everything = (mp, BLOCKS, width, hidden)
    wide_b, wide_f = v((total, width), bf16), v((total, width), f32)
    turned = v((width, total), bf16)
    heads = (utts, mp, HEADS, length, length)
    return pl.pallas_call(
        functools.partial(forward_kernel, mp, utts, length),
        out_shape=(sds((mp, total, PROJ), bf16), sds((mp, total, 2 * LANES), bf16), sds(heads, bf16),
                   sds((total, width), f32), sds((mp, total, hidden), bf16), sds((mp, total, hidden), bf16),
                   sds((total, width), f32), sds((total, width), f32), sds(vec.shape, f32),
                   sds((mp,) + small.shape, f32), sds(everything, bf16), sds(everything, bf16)),
        in_specs=[SMEM] + [VM] * 7 + [ANY] * 2,
        out_specs=(VM,) * 10 + (ANY,) * 2,
        scratch_shapes=[v(shard, bf16)] * 4 + [
            v((mp,) + small.shape, f32), v(small.shape, f32), wide_b, wide_b, wide_b, v((mp,) + small.shape, f32),
            v((mp, total, PROJ), bf16), v((mp, total, 2 * LANES), bf16), v(heads, bf16),
            wide_f, wide_b, wide_b, wide_b, turned, turned, wide_f, v((length, width), f32),
            v((mp, total, 2 * LANES), bf16),
            sem((BLOCKS,)), sem((2, mp - 1, BLOCKS)), sem((2, mp - 1, BLOCKS)),
            sem((3, 2, mp - 1, BLOCKS)), sem((3, 2, mp - 1, BLOCKS)), sem((mp - 1,)), sem((mp - 1,)),
            sem((4 + 2 * utts,)), sem((4 + 2 * utts,)), sem((BLOCKS, mp)), sem((BLOCKS, mp))],
        compiler_params=pltpu.CompilerParams(collective_id=0, has_side_effects=True, vmem_limit_bytes=63 * 2**20),
        name="layers_forward",
    )(lens, x, cot, vec, small, w_in, w_o, w_cross, w_one, w_two)


RING = 6


def backward_kernel(mp, dp, utts, length,
                    x_ref, vec_ref, vg_in, sg_in, x1_in, g_in, qkv_in, ctx_in, p_in, a_in, gp_in, w_ref, grad_ref,
                    dx, in_grad, o_grad, cross_grad, one_grad, two_grad, small_out,
                    wa, wc, w1, w2, x1, qkv, ctx, p, a, gp, h, dy, dyt, ht, dh, dctx, vg, sg,
                    from_core, from_side, from_line, sum_sg, got_small, got_vg, got_sg, cross_got,
                    l_sem, i_sem, c_send, c_recv, y_send, y_recv, z_send, z_recv, credit, a_send, a_recv, b_send, b_recv,
                    x_send, x_recv):
    me = lax.axis_index("mp")
    dp_index = lax.axis_index("dp")
    section = lax.axis_index("section")
    decoding = section == 1
    encoding = section == 0
    near = dp // 4
    core = partners(dp_index, near)
    side = partners(dp_index, 2 * near)
    diag = partners(core, 2 * near)
    quarter = dp_index // near
    parity = lax.rem(quarter, 2)
    half = quarter // 2
    part = wa.shape[1] // 4
    total = utts * length
    T = LANES
    bufs = (wa, wc, w1, w2)

    barrier = pltpu.get_barrier_semaphore()
    for hop in range(1, mp):
        pl.semaphore_signal(barrier, inc=1, device_id={"mp": lax.rem(me + hop, mp)}, device_id_type=MESH)
    for other in (core, side, diag):
        pl.semaphore_signal(barrier, inc=1, device_id={"dp": other}, device_id_type=MESH)
    pl.semaphore_signal(barrier, inc=1, device_id={"section": 1 - section}, device_id_type=MESH)

    def shard_of(i):
        return jnp.where(lax.rem(i, 2) == 0, mp - 1 - i // 2, i // 2)

    per_shard = 2 + section
    spots = mp * per_shard + mp

    def place(b, i):
        return mp * per_shard + i if b == 0 else i * per_shard + (0, 0, per_shard - 1, per_shard - 2)[b]

    def load(b, m):
        return pltpu.make_async_copy(w_ref.at[m, b], bufs[b].at[m], l_sem.at[b, m])

    def load_grad(b, m):
        return pltpu.make_async_copy(grad_ref.at[m, b], bufs[b].at[m], l_sem.at[b, m])

    def piece(b, m, which):
        return bufs[b].at[m, pl.ds(pl.multiple_of(which * part, 16), part)]

    def to_core(b, i, m, k):
        return pltpu.make_async_remote_copy(
            src_ref=piece(b, m, 2 * k + 1 - parity), dst_ref=from_core.at[lax.rem(place(b, i), RING), k],
            send_sem=c_send.at[b, m, k], recv_sem=c_recv.at[b, m, k],
            device_id={"dp": core}, device_id_type=MESH)

    def to_side(b, m):
        return pltpu.make_async_remote_copy(
            src_ref=piece(b, m, 2 * (1 - half) + parity), dst_ref=from_side.at[b, m],
            send_sem=y_send.at[b, m], recv_sem=y_recv.at[b, m],
            device_id={"dp": side}, device_id_type=MESH)

    def line_slot(way, m):
        return m - 1 if way == 0 else m

    def on_line(way, b, m):
        return pltpu.make_async_remote_copy(
            src_ref=piece(b, m, quarter), dst_ref=from_line.at[way, line_slot(way, m), b],
            send_sem=z_send.at[way, b, m], recv_sem=z_recv.at[way, b, m],
            device_id={"mp": me + 1 - 2 * way}, device_id_type=MESH)

    def needed(b):
        return decoding if b == 1 else me >= 0

    def add(b, m, which, other):
        ref = piece(b, m, which)
        ref[...] = (ref[...].astype(f32) + other[...].astype(f32)).astype(bf16)

    def send_core(b, i):
        m = shard_of(i)
        spot = place(b, i)

        @pl.when(needed(b) & (spot >= RING))
        def _():
            pl.semaphore_wait(credit, 1)

        @pl.when(needed(b))
        def _():
            for k in (0, 1):
                to_core(b, i, m, k).start()

    def stage_core(b, i):
        m = shard_of(i)
        spot = place(b, i)

        @pl.when(needed(b))
        def _():
            for k in (0, 1):
                to_core(b, i, m, k).wait_recv()
                add(b, m, 2 * k + parity, from_core.at[lax.rem(spot, RING), k])
            to_side(b, m).start()

            @pl.when(spot + RING < spots)
            def _():
                pl.semaphore_signal(credit, inc=1, device_id={"dp": core}, device_id_type=MESH)

    def stage_side(b, i):
        m = shard_of(i)

        @pl.when(needed(b))
        def _():
            to_side(b, m).wait_recv()
            add(b, m, quarter, from_side.at[b, m])
            for way in (0, 1):
                first = (me == 0) if way == 0 else (me == mp - 1)

                @pl.when(first & (me != m))
                def _():
                    on_line(way, b, m).start()

    def stage_line(b, i):
        m = shard_of(i)
        for way in (0, 1):
            inner = ((me > 0) & (me < m)) if way == 0 else ((me < mp - 1) & (me > m))

            @pl.when(needed(b) & inner)
            def _():
                on_line(way, b, m).wait_recv()
                add(b, m, quarter, from_line.at[way, line_slot(way, m), b])
                on_line(way, b, m).start()

    saved = [pltpu.make_async_copy(src, dst, i_sem.at[j]) for j, (src, dst) in enumerate(
        ((g_in, dx), (x1_in, x1), (gp_in, gp), (a_in, a), (qkv_in, qkv), (ctx_in, ctx), (p_in, p)))]
    saved[0].start()

    @pl.when(encoding)
    def _():
        for j in (1, 2, 3):
            saved[j].start()
        for i in range(mp):
            load(3, shard_of(i)).start()
            load(2, shard_of(i)).start()

    @pl.when(decoding)
    def _():
        for i in range(mp):
            for b in (1, 3, 2):
                load_grad(b, shard_of(i)).start()
    for i in range(mp):
        load(0, shard_of(i)).start()
    for j in (4, 5, 6):
        saved[j].start()
    vg[...] = vg_in[...]
    sg[...] = sg_in[...]
    saved[0].wait()

    @pl.when(encoding)
    def _():
        for j in (1, 2, 3):
            saved[j].wait()

        def prepare(rows):
            h[rows] = norm(x1[rows], vec_ref[5:6], vec_ref[6:7]).astype(bf16)
        row_loop(total, 256, prepare)
        vg[7:8, :] = jnp.sum(dx[...], axis=0, keepdims=True)
        dy[...] = dx[...].astype(bf16)
        turn(dyt, dy[...])
        turn(ht, h[...])
        dh[...] = jnp.zeros_like(dh)
    pl.semaphore_wait(barrier, mp + 3)

    def ffn_step(i, carry):
        m = shard_of(i)

        @pl.when(encoding)
        def _():
            load(3, m).wait()
            load(2, m).wait()
            ffn_dgrad_shard(m, gp, w1, w2, dy, dh, sg)
            w2[m] = nn(dyt[...], a[m]).astype(bf16)
            w1[m] = nn(ht[...], gp[m]).astype(bf16)

        @pl.when(decoding)
        def _():
            for b in (1, 3, 2):
                load_grad(b, m).wait()
        for b in (1, 3, 2):
            send_core(b, i)

        @pl.when(i > 0)
        def _():
            for b in (1, 3, 2):
                stage_core(b, i - 1)
        return carry
    lax.fori_loop(0, mp, ffn_step, 0)
    for b in (1, 3, 2):
        stage_core(b, mp - 1)

    @pl.when(encoding)
    def _():
        norm_back(total, x1, vec_ref[5:6], dh, dx, vg, 5)

    def prepare_self(rows):
        h[rows] = norm(x_ref[rows].astype(f32), vec_ref[0:1], vec_ref[1:2]).astype(bf16)
    row_loop(total, 256, prepare_self)
    vg[2:3, :] = jnp.sum(dx[...], axis=0, keepdims=True)
    dy[...] = dx[...].astype(bf16)
    turn(dyt, dy[...])
    turn(ht, h[...])
    dh[...] = jnp.zeros_like(dh)
    for j in (4, 5, 6):
        saved[j].wait()
    down = lax.broadcasted_iota(jnp.int32, (length, length), 0)
    along = lax.broadcasted_iota(jnp.int32, (length, length), 1)
    flip = (down + along == length - 1).astype(f32).astype(bf16)

    def self_step(i, carry):
        m = shard_of(i)
        load(0, m).wait()
        dctx[m] = nt(dy[...], wa[m, CTX:]).astype(bf16)
        attend_back(m, length, range(utts), qkv, p, dctx, qkv, sg, flip)
        d = qkv[m]
        sg[m, 0:1, :PROJ] = jnp.sum(d.astype(f32), axis=0, keepdims=True)
        dh[...] += nn(d, wa[m, :PROJ])
        gd = nn(ht[...], d)
        go = nn(dyt[...], ctx[m])
        wa[m, :, :CTX] = gd[:, :CTX].astype(bf16)
        wa[m, :, CTX:PROJ] = (gd[:, CTX:] + go[:, :T]).astype(bf16)
        wa[m, :, PROJ:] = go[:, T:].astype(bf16)
        send_core(0, i)

        @pl.when(i > 0)
        def _():
            stage_core(0, i - 1)
            stage_line(2, i - 1)
        stage_side(1, i)
        stage_side(3, i)
        stage_line(1, i)
        stage_side(2, i)
        stage_line(3, i)
        return carry
    lax.fori_loop(0, mp, self_step, 0)
    stage_core(0, mp - 1)
    norm_back(total, x_ref, vec_ref[0:1], dh, dx, vg, 0)

    def group_vg(hop, to):
        return pltpu.make_async_remote_copy(
            src_ref=vg, dst_ref=got_vg.at[hop], send_sem=a_send.at[hop, 1], recv_sem=a_recv.at[hop, 1],
            device_id={"dp": to}, device_id_type=MESH)

    def group_sg(hop, to):
        return pltpu.make_async_remote_copy(
            src_ref=sg, dst_ref=got_sg.at[hop], send_sem=a_send.at[hop, 0], recv_sem=a_recv.at[hop, 0],
            device_id={"dp": to}, device_id_type=MESH)

    mates = (core, side, diag)
    for hop, to in enumerate(mates):
        group_vg(hop, to).start()
        group_sg(hop, to).start()
    stage_line(2, mp - 1)
    stage_side(0, 0)
    sum_sg[pl.ds(0, mp)] = sg[...]
    sum_sg[mp] = vg[...]
    for hop, to in enumerate(mates):
        group_vg(hop, to).wait_recv()
        group_sg(hop, to).wait_recv()
        sum_sg[pl.ds(0, mp)] += got_sg[hop]
        sum_sg[mp] += got_vg[hop]

    def line_small(hop, which):
        peer = lax.rem(me + hop, mp)
        src = sum_sg.at[peer] if which == 0 else sum_sg.at[mp]
        return pltpu.make_async_remote_copy(
            src_ref=src, dst_ref=got_small.at[hop - 1, which],
            send_sem=b_send.at[hop - 1, which], recv_sem=b_recv.at[hop - 1, which],
            device_id={"mp": peer}, device_id_type=MESH)

    for hop in range(1, mp):
        for which in (0, 1):
            line_small(hop, which).start()
    stage_side(0, 1)
    stage_line(0, 0)
    stage_side(0, 2)
    stage_line(0, 1)
    stage_side(0, 3)
    stage_line(0, 2)
    stage_line(0, 3)
    small_out[0] = sum_sg[me]
    small_out[1] = sum_sg[mp]
    for hop in range(1, mp):
        for which in (0, 1):
            line_small(hop, which).wait_recv()
            small_out[which] += got_small[hop - 1, which]

    own_rows = pl.ds(pl.multiple_of(quarter * part, 16), part)

    def finish(b):
        ref = bufs[b].at[me, own_rows]
        for way in (0, 1):
            @pl.when((me > 0) if way == 0 else (me < mp - 1))
            def _():
                on_line(way, b, me).wait_recv()
        low = jnp.where(me > 0, from_line[0, jnp.maximum(me - 1, 0), b].astype(f32), 0.0)
        high = jnp.where(me < mp - 1, from_line[1, jnp.minimum(me, mp - 2), b].astype(f32), 0.0)
        return ref[...].astype(f32) + low + high

    def over(src, dst):
        return pltpu.make_async_remote_copy(
            src_ref=src, dst_ref=dst, send_sem=x_send, recv_sem=x_recv,
            device_id={"section": 1 - section}, device_id_type=MESH)

    def heads(value, slots):
        return jnp.concatenate([value[:, 64 * s:64 * s + 64] for s in slots], axis=1)

    @pl.when(decoding)
    def _():
        mine = finish(1)
        cross_grad[0] = heads(mine, Q_SLOTS)
        cross_grad[1] = heads(mine, O_SLOTS)
        cross_got[0] = heads(mine, K_SLOTS).astype(bf16)
        cross_got[1] = heads(mine, V_SLOTS).astype(bf16)
        over(cross_got.at[pl.ds(0, 2)], cross_got.at[pl.ds(2, 2)]).start()
    two_grad[...] = finish(3).T
    one_grad[...] = finish(2)
    mine = finish(0)
    for t, slots in enumerate((Q_SLOTS, K_SLOTS, V_SLOTS)):
        in_grad[t] = heads(mine, slots)
    o_grad[...] = heads(mine, O_SLOTS).T

    @pl.when(encoding)
    def _():
        over(cross_got.at[pl.ds(0, 2)], cross_got.at[pl.ds(2, 2)]).wait_recv()
        cross_grad[0] = cross_got[2].astype(f32)
        cross_grad[1] = cross_got[3].astype(f32)

    @pl.when(decoding)
    def _():
        over(cross_got.at[pl.ds(0, 2)], cross_got.at[pl.ds(2, 2)]).wait_send()
    for hop, to in enumerate(mates):
        group_vg(hop, to).wait_send()
        group_sg(hop, to).wait_send()
    for hop in range(1, mp):
        for which in (0, 1):
            line_small(hop, which).wait_send()

    def drain(i, carry):
        m = shard_of(i)
        for b in range(BLOCKS):
            @pl.when(needed(b))
            def _():
                for k in (0, 1):
                    to_core(b, i, m, k).wait_send()
                to_side(b, m).wait_send()
                for way in (0, 1):
                    @pl.when((me < m) if way == 0 else (me > m))
                    def _():
                        on_line(way, b, m).wait_send()
        return carry
    lax.fori_loop(0, mp, drain, 0)


def backward(mp, dp, utts, length, x, x1, g, qkv, ctx, p, a, gp, vec, vg, sg, w, grads):
    total, width = x.shape
    hidden = w.shape[3]
    sds = jax.ShapeDtypeStruct
    v = pltpu.VMEM
    sem = pltpu.SemaphoreType.DMA
    shard = (mp, width, hidden)
    part = width // 4
    own = hidden // mp
    piece = (part, hidden)
    small = sg.shape[1:]
    wide_b, wide_f = v((total, width), bf16), v((total, width), f32)
    turned = v((width, total), bf16)
    return pl.pallas_call(
        functools.partial(backward_kernel, mp, dp, utts, length),
        out_shape=(sds((total, width), f32), sds((3, part, own), f32), sds((own, part), f32),
                   sds((2, part, own), f32), sds((part, hidden), f32), sds((hidden, part), f32),
                   sds((2,) + small, f32)),
        in_specs=[VM] * 4 + [ANY] * 9,
        out_specs=(VM,) * 7,
        scratch_shapes=[v(shard, bf16)] * 4 + [
            wide_f, v(qkv.shape, bf16), v(ctx.shape, bf16), v(p.shape, bf16), v(a.shape, bf16), v(gp.shape, bf16), wide_b, wide_b, turned, turned, wide_f, v(ctx.shape, bf16),
            v(vec.shape, f32), v(sg.shape, f32),
            v((RING, 2) + piece, bf16), v((BLOCKS, mp) + piece, bf16), v((2, mp - 1, BLOCKS) + piece, bf16),
            v((mp + 1,) + small, f32), v((mp - 1, 2) + small, f32), v((3,) + small, f32), v((3, mp) + small, f32),
            v((4, part, own), bf16),
            sem((BLOCKS, mp)), sem((7,)), sem((BLOCKS, mp, 2)), sem((BLOCKS, mp, 2)), sem((BLOCKS, mp)), sem((BLOCKS, mp)),
            sem((2, BLOCKS, mp)), sem((2, BLOCKS, mp)), pltpu.SemaphoreType.REGULAR,
            sem((3, 2)), sem((3, 2)), sem((mp - 1, 2)), sem((mp - 1, 2)), sem, sem],
        compiler_params=pltpu.CompilerParams(collective_id=1, has_side_effects=True, vmem_limit_bytes=63 * 2**20),
        name="layers_backward",
    )(x, vec, vg, sg, x1, g, qkv, ctx, p, a, gp, w, grads)


def bias_row(q, v):
    none = jnp.zeros((64,), f32)
    return jnp.concatenate([q[0], q[1], none, none, q[2], v[0], v[1], v[2], none, none, none, none])


def take_slots(values, slots):
    return jnp.concatenate([values[..., 64 * s:64 * s + 64] for s in slots], axis=-1)


def rel_line(table, length):
    half = table.shape[1] // 2
    heads = table.shape[0]
    first = jnp.broadcast_to(table[:, :1], (heads, length - half))
    last = jnp.broadcast_to(table[:, -1:], (heads, length - half))
    return jnp.concatenate([table[:, :half + 1][:, ::-1], first, last, table[:, half + 1:][:, ::-1]], axis=1)


def rel_fold(line, rel):
    length = line.shape[-1] // 2
    half = rel // 2
    low = length - 1 + half
    high = length - half + 1
    return jnp.concatenate([jnp.sum(line[..., low:], axis=-1, keepdims=True), line[..., high:low][..., ::-1],
                            jnp.sum(line[..., :high], axis=-1, keepdims=True)], axis=-1)


def per_device(streams, lengths, vectors, attn_in, attn_bias, attn_out, rel_table, cross, ffn_in, ffn_bias, ffn_out,
               cotangent):
    section = lax.axis_index("section")
    decoding = section == 1
    mp = lax.axis_size("mp")
    dp = lax.axis_size("dp")
    me = lax.axis_index("mp")
    dp_index = lax.axis_index("dp")
    utts, length, width = streams.shape[1:]
    total = utts * length
    rel = rel_table.shape[2]
    x = streams[0].reshape(total, width)
    cot = cotangent[0].reshape(total, width)
    vec = vectors[0]

    lens = lax.dynamic_slice_in_dim(lengths, me * utts, utts, 1)
    lens = jnp.concatenate([jnp.where(decoding, lens[1], lens[0]), lens[0]])
    ext = rel_line(rel_table[0], length)
    biases = attn_bias[0]
    small = jnp.concatenate([bias_row(biases[0], biases[1])[None], bias_row(biases[2], biases[2])[None],
                             ffn_bias[0].reshape(1, -1), jnp.pad(ext, ((0, 2), (0, width - ext.shape[1])))], axis=0)

    qkv, ctx, p, x1, a, gp, out, g, vg, sg, grads, weights = forward(
        mp, utts, length, lens, x, cot, vec, small, attn_in[0], attn_out[0], cross[0], ffn_in[0], ffn_out[0])
    dx, in_grad, o_grad, cross_grad, one_grad, two_grad, small_sum = backward(
        mp, dp, utts, length, x, x1, g, qkv, ctx, p, a, gp, vec, vg, sg, weights, grads)
    if dp > 4:
        per = dp // 4
        groups = [[q * per + i for i in range(per)] for q in range(4)]

        def rest(value, axis):
            return lax.psum_scatter(value.astype(bf16), "dp", scatter_dimension=axis, axis_index_groups=groups,
                                    tiled=True).astype(f32)

        in_grad, o_grad, cross_grad = rest(in_grad, 1), rest(o_grad, 1), rest(cross_grad, 1)
        one_grad, two_grad = rest(one_grad, 0), rest(two_grad, 1)
        strides = [[i + per * q for i in range(per)] for q in range(4)]
        small_sum = lax.psum(small_sum, "dp", axis_index_groups=strides)

    spread = width // (mp * dp)
    vectors_grad = lax.dynamic_slice_in_dim(small_sum[1], (dp_index * mp + me) * spread, spread, 1)
    row_a, row_c = small_sum[0, 0, :PROJ], small_sum[0, 1, :PROJ]
    cross_bias = jnp.where(decoding, take_slots(row_c, Q_SLOTS), take_slots(row_c, V_SLOTS))
    bias_grad = jnp.stack([take_slots(row_a, Q_SLOTS), take_slots(row_a, V_SLOTS), cross_bias]).reshape(3, HEADS, 64)
    rel_grad = rel_fold(small_sum[0, 3:3 + HEADS, :2 * length], rel)
    b1_grad = small_sum[0, 2].reshape(-1, 128)

    def mine(value):
        size = value.shape[-1] // dp
        return lax.dynamic_slice_in_dim(value, dp_index * size, size, value.ndim - 1)[None]

    shape = (1, utts, length, width)
    return (out.reshape(shape), dx.reshape(shape), vectors_grad[None], in_grad[None], mine(bias_grad), o_grad[None],
            mine(rel_grad), cross_grad[None], one_grad[None], mine(b1_grad), two_grad[None])


def solution(mesh):
    placed = (
        P("section", ("dp", "mp"), None, None),
        P(None, "dp"),
        P("section", None, None),
        P("section", None, None, "mp"),
        P("section", None, "mp", None),
        P("section", "mp", None),
        P("section", "mp", None),
        P("section", None, None, "mp"),
        P("section", None, "mp"),
        P("section", "mp", None),
        P("section", "mp", None),
        P("section", ("dp", "mp"), None, None),
    )
    return jax.shard_map(
        per_device,
        mesh=mesh,
        in_specs=placed,
        out_specs=(
            P("section", ("dp", "mp"), None, None),
            P("section", ("dp", "mp"), None, None),
            P("section", None, ("dp", "mp")),
            P("section", None, "dp", "mp"),
            P("section", None, "mp", "dp"),
            P("section", "mp", "dp"),
            P("section", "mp", "dp"),
            P("section", None, "dp", "mp"),
            P("section", "dp", "mp"),
            P("section", "mp", "dp"),
            P("section", "mp", "dp"),
        ),
        check_vma=False,
    )
```

```python
import functools
import jax
import jax.numpy as jnp
from jax import lax
from jax.experimental import pallas as pl
from jax.experimental.pallas import tpu as pltpu
from jax.sharding import PartitionSpec as P

MESH = pl.DeviceIdType.MESH
ANY = pl.BlockSpec(memory_space=pl.ANY)
VM = pl.BlockSpec(memory_space=pltpu.VMEM)
BLOCKS = 4


def partners(dp_index, step):
    bit = lax.rem(dp_index // step, 2)
    return dp_index + step - 2 * step * bit


EPSILON = 1e-05
MASKED = -1e30
HEADS = 3
LANES = 128
PROJ = 640
CTX = 512
bf16, f32 = jnp.bfloat16, jnp.float32


def nn(a, b):
    return lax.dot_general(a, b, (((1,), (0,)), ((), ())), preferred_element_type=f32)


def nt(a, b):
    return lax.dot_general(a, b, (((1,), (1,)), ((), ())), preferred_element_type=f32)


def tn(a, b):
    return lax.dot_general(a, b, (((0,), (0,)), ((), ())), preferred_element_type=f32)


def norm_parts(x):
    centred = x - jnp.mean(x, axis=-1, keepdims=True)
    r = lax.rsqrt(jnp.mean(centred * centred, axis=-1, keepdims=True) + EPSILON)
    return centred * r, r


def norm(x, gain, shift):
    xh, _ = norm_parts(x)
    return xh * gain + shift


def row_loop(total, size, body):
    def step(i, carry):
        body(pl.ds(pl.multiple_of(i * size, size), size))
        return carry
    lax.fori_loop(0, total // size, step, 0)


def even_lanes(rows):
    return lax.broadcasted_iota(jnp.int32, (rows, LANES), 1) < LANES // 2


def half_mask(half):
    lane = lax.broadcasted_iota(jnp.int32, (1, LANES), 1)
    on = (lane < LANES // 2) if half == 0 else (lane >= LANES // 2)
    return on.astype(f32).astype(bf16)


def tile(ref, m, rows, t):
    return ref[m, rows, t * LANES:(t + 1) * LANES]


HEAD_TILES = (((3, 0), (0, 0), (1, 1), (0, 1)),
              ((3, 1), (0, 1), (2, 0), (1, 0)),
              ((4, 0), (1, 0), (2, 1), (1, 1)))


def attend(m, length, utts, qkv_ref, ctx_ref, p_ref, limits, ext_ref):
    key_at = lax.broadcasted_iota(jnp.int32, (length, length), 0)
    even = even_lanes(length)
    parts = {u: [None] * HEADS for u in utts}
    for r in range(HEADS):
        (qt, half), (kt, _), (vt, _), _ = HEAD_TILES[r]
        if ext_ref is not None:
            row = ext_ref[m, 3 + r:4 + r, :2 * length]
            bias = pltpu.roll(jnp.broadcast_to(row, (length, 2 * length)), 0, 1, stride=1, stride_axis=0)[:, :length].T
        for u in utts:
            rows = pl.ds(u * length, length)
            s = nt(tile(qkv_ref, m, rows, kt) * half_mask(half), tile(qkv_ref, m, rows, qt))
            if ext_ref is not None:
                s = s + bias
            s = jnp.where(key_at <= limits[u], s, MASKED)
            e = jnp.exp(s - jnp.max(s, axis=0, keepdims=True))
            p = (e * (1.0 / jnp.sum(e, axis=0, keepdims=True))).astype(bf16)
            p_ref[u, m, r] = p
            parts[u][r] = tn(p, tile(qkv_ref, m, rows, vt))
    for u in utts:
        rows = pl.ds(u * length, length)
        ctx_ref[m, rows, :LANES] = jnp.where(even, 0.0, parts[u][0]).astype(bf16)
        ctx_ref[m, rows, LANES:] = jnp.where(even, parts[u][1], parts[u][2]).astype(bf16)


def attend_back(m, length, utts, qkv_ref, p_ref, dctx_ref, out_ref, rel_ref, flip):
    even = even_lanes(length)
    got = {u: [None] * HEADS for u in utts}
    for r in range(HEADS):
        (qt, _), (kt, _), (vt, vhalf), (ot, _) = HEAD_TILES[r]
        total = None
        for u in utts:
            rows = pl.ds(u * length, length)
            p = p_ref[u, m, r]
            dctx = tile(dctx_ref, 0, rows, ot)
            dp = nt(tile(qkv_ref, m, rows, vt) * half_mask(vhalf), dctx)
            pf = p.astype(f32)
            t = pf * dp
            ds = (t - pf * jnp.sum(t, axis=0, keepdims=True)).astype(bf16)
            got[u][r] = (tn(ds, tile(qkv_ref, m, rows, kt)) * 0.125, nn(ds, tile(qkv_ref, m, rows, qt)), nn(p, dctx))
            if rel_ref is not None:
                turned = nn(ds, flip)
                total = turned if total is None else total + turned
        if rel_ref is not None:
            wide = jnp.concatenate([total, jnp.zeros_like(total)], axis=1)
            wide = pltpu.roll(wide, 0, 1, stride=1, stride_axis=0)
            rel_ref[m, 3 + r:4 + r, :2 * length] = jnp.sum(wide, axis=0, keepdims=True)
    for u in utts:
        rows = pl.ds(u * length, length)
        (q0, k0, v0), (q1, k1, v1), (q2, k2, v2) = got[u]
        for t, (left, right) in enumerate(((k0, k1), (k2, v0), (v1, v2), (q0, q1), (q2, 0.0))):
            out_ref[m, rows, t * LANES:(t + 1) * LANES] = jnp.where(even, left, right).astype(bf16)


def gelu_both(u):
    cdf = 0.5 + 0.5 * lax.erf(u * 0.7071067811865476)
    return u * cdf, cdf + u * (jnp.exp(-0.5 * u * u) * 0.3989422804014327)


def norm_back(total, x_ref, gain, dh_ref, add_into, vg_ref, gain_row, grad_out=None):
    width = gain.shape[-1]

    def step(i, carry):
        dgain, dshift = carry
        rows = pl.ds(pl.multiple_of(i * 128, 128), 128)
        dh = dh_ref[rows].astype(f32)
        xh, r = norm_parts(x_ref[rows].astype(f32))
        e = dh * gain
        dx = r * (e - jnp.mean(e, axis=-1, keepdims=True) - xh * jnp.mean(e * xh, axis=-1, keepdims=True))
        add_into[rows] = add_into[rows].astype(f32) + dx
        return dgain + jnp.sum(dh * xh, axis=0, keepdims=True), dshift + jnp.sum(dh, axis=0, keepdims=True)

    zero = jnp.zeros((1, width), f32)
    dgain, dshift = lax.fori_loop(0, total // 128, step, (zero, zero))
    vg_ref[gain_row:gain_row + 1, :] = dgain
    vg_ref[gain_row + 1:gain_row + 2, :] = dshift


def turn(dst_ref, src):
    dst_ref[...] = src.T


SMEM = pl.BlockSpec(memory_space=pltpu.SMEM)


SEQUENCE = ((0, 1), (1, 1), (2, 1), (0, 2), (1, 2), (3, 1), (0, 3), (1, 3), (2, 2), (3, 2), (2, 3), (3, 3))
HALVES = 2
RING = 5


def wide_dot(dot, a, b_cols, width, use, step=256):
    for start in range(0, width, step):
        size = min(step, width - start)
        use(slice(start, start + size), dot(a, b_cols(start, size)))


def ffn_shard(m, h, w1, w2, a, gp, bias, out):
    def keep(cols, u):
        act, slope = gelu_both(u + bias[:, cols])
        a[m, :, cols] = act.astype(bf16)
        gp[m, :, cols] = slope.astype(bf16)
    wide_dot(nn, h[...], lambda s, n: w1[m, :, s:s + n], w1.shape[2], keep)
    out[...] += nn(a[m], w2[m])


def ffn_start(total, x_ref, out_ref, h_ref, vec_ref):
    def prepare(rows):
        x = x_ref[rows]
        h_ref[rows] = norm(x, vec_ref[5:6], vec_ref[6:7]).astype(bf16)
        out_ref[rows] = x + vec_ref[7:8]
    row_loop(total, 256, prepare)


def ffn_dgrad_shard(m, gp, w1, w2, dy, dh, sg):
    def keep(cols, da):
        du = (da * gp[m, :, cols].astype(f32)).astype(bf16)
        gp[m, :, cols] = du
        sg[m, 2:3, cols] = jnp.sum(du.astype(f32), axis=0, keepdims=True)
    wide_dot(nt, dy[...], lambda s, n: w2[m, s:s + n], w2.shape[1], keep)
    dh[...] += nt(gp[m], w1[m])


def layers_kernel(mp, dp, utts, length,
                  lens_ref, x_ref, cot_ref, vec_ref, small_ref, in_ref, o_ref, cross_ref, w1_ref, w2_ref,
                  g, small_out, out_hbm, own_hbm, qkv_hbm, ctx_hbm, p_hbm,
                  wa, wc, w1, w2, smalls, peer_small, qkv, ctx, p, a, gp, x1, y2, out, h, hc, mem, dmem,
                  dy, dyt, ht, dctx, vg, sg, cb, from_core, from_side, from_line, sum_sg, got_vg, got_sg, got_line,
                  kv_grad,
                  l_sem, z_send, z_recv, p_send, p_recv, s_send, s_recv, x_send, x_recv, i_sem,
                  c_send, c_recv, y_send, y_recv, r_send, r_recv, credit, a_send, a_recv, b_send, b_recv):
    me = lax.axis_index("mp")
    dp_index = lax.axis_index("dp")
    section = lax.axis_index("section")
    decoding = section == 1
    encoding = section == 0
    near = dp // 4
    core = partners(dp_index, near)
    side = partners(dp_index, 2 * near)
    diag = partners(core, 2 * near)
    quarter = dp_index // near
    parity = lax.rem(quarter, 2)
    half = quarter // 2
    core_quarter = quarter + 1 - 2 * parity
    side_quarter = quarter + 2 - 4 * half
    diag_quarter = core_quarter + 2 - 4 * half
    part = wa.shape[1] // 4
    total = utts * length
    T = LANES
    KV, PROJ_END = 3 * T, PROJ
    bufs = (wa, wc, w1, w2)
    dh = out

    barrier = pltpu.get_barrier_semaphore()
    for hop in range(1, mp):
        pl.semaphore_signal(barrier, inc=1, device_id={"mp": lax.rem(me + hop, mp)}, device_id_type=MESH)
    for other in (core, side, diag):
        pl.semaphore_signal(barrier, inc=1, device_id={"dp": other}, device_id_type=MESH)
    pl.semaphore_signal(barrier, inc=1, device_id={"section": 1 - section}, device_id_type=MESH)

    def needed(b):
        return decoding if b == 1 else me >= 0

    def utt(u):
        return pl.ds(u * length, length)

    def own_rows(b, t, src):
        return pltpu.make_async_copy(src, bufs[b].at[me, t * part:(t + 1) * part], l_sem.at[b, t])

    own_a = [own_rows(0, 0, in_ref.at[1]), own_rows(0, 1, in_ref.at[2]), own_rows(0, 2, in_ref.at[0]),
             own_rows(0, 3, o_ref)]
    own_c = [own_rows(1, 2, cross_ref.at[0]), own_rows(1, 3, cross_ref.at[1])]
    own_w = [pltpu.make_async_copy(src, bufs[b].at[me], l_sem.at[b, 0]) for b, src in ((2, w1_ref), (3, w2_ref))]
    for copy in own_a:
        copy.start()

    @pl.when(decoding)
    def _():
        for copy in own_c:
            copy.start()
    for copy in own_w:
        copy.start()
    pl.semaphore_wait(barrier, mp + 3)
    for copy in own_a:
        copy.wait()

    def rows(which, hh=None):
        if hh is None:
            return pl.ds(pl.multiple_of(which * part, 16), part)
        size = part // HALVES
        return pl.ds(pl.multiple_of(which * part + hh * size, 16), size)

    def along(src, shard, b, hh, way, dist):
        return pltpu.make_async_remote_copy(
            src_ref=src, dst_ref=bufs[b].at[shard, rows(quarter, hh)],
            send_sem=z_send.at[way, dist - 1, b, hh], recv_sem=z_recv.at[way, dist - 1, b, hh],
            device_id={"mp": me + 1 - 2 * way}, device_id_type=MESH)

    def across(kind, shard, b, hh, which, way, dist, to):
        ref = bufs[b].at[shard, rows(which, hh)]
        return pltpu.make_async_remote_copy(
            src_ref=ref, dst_ref=ref,
            send_sem=p_send.at[kind, way, dist - 1, b, hh], recv_sem=p_recv.at[kind, way, dist - 1, b, hh],
            device_id={"dp": to}, device_id_type=MESH)

    def small_copy(hop, slot):
        return pltpu.make_async_remote_copy(
            src_ref=smalls.at[me], dst_ref=smalls.at[slot],
            send_sem=s_send.at[hop - 1], recv_sem=s_recv.at[hop - 1],
            device_id={"mp": lax.rem(me + hop, mp)}, device_id_type=MESH)

    def over(index, src, dst):
        return pltpu.make_async_remote_copy(
            src_ref=src, dst_ref=dst, send_sem=x_send.at[index], recv_sem=x_recv.at[index],
            device_id={"section": 1 - section}, device_id_type=MESH)

    def over_rows(i):
        return over(i, cross_ref.at[i], wc.at[me, i * part:(i + 1) * part])

    def over_mem(u):
        return over(3 + u, mem.at[utt(u)], mem.at[utt(u)])

    def over_dmem(u):
        return over(3 + utts + u, dmem.at[utt(u)], dmem.at[utt(u)])

    over_small = over(2, small_ref, peer_small)
    over_cb = over(3 + 2 * utts, cb, cb)
    over_kv = over(4 + 2 * utts, kv_grad.at[0], kv_grad.at[1])

    def has_next(way):
        return (me < mp - 1) if way == 0 else (me > 0)

    def has_shard(way, dist):
        return (me >= dist) if way == 0 else (me + dist <= mp - 1)

    def shard_at(way, dist):
        return me - dist if way == 0 else me + dist

    def own_src(b, hh):
        src = (wa.at[me], wc.at[me], w1_ref, w2_ref)[b]
        return src.at[rows(quarter, hh)]

    def own_send(b):
        for hh in range(HALVES):
            for way in (0, 1):
                @pl.when(needed(b) & has_next(way))
                def _():
                    along(own_src(b, hh), me, b, hh, way, 1).start()

    own_send(0)

    @pl.when(encoding)
    def _():
        for i in (0, 1):
            over_rows(i).start()
        over_small.start()
        smalls[me] = small_ref[...]
        own_send(2)

    @pl.when(decoding)
    def _():
        over_small.wait_recv()
        smalls[me] = small_ref[...]
        lane = lax.broadcasted_iota(jnp.int32, (1, small_ref.shape[1]), 1)
        smalls[me, 1:2] = jnp.where(lane < 2 * part, peer_small[1:2], small_ref[1:2])
        for copy in own_c:
            copy.wait()
        for i in (0, 1):
            over_rows(i).wait_recv()
        own_send(1)
        own_send(2)
    for hop in range(1, mp):
        small_copy(hop, me).start()

    steps = [(b, dist, hh) for b, dist in SEQUENCE for hh in range(HALVES)]

    def on_line(k):
        b, dist, hh = steps[k]
        for way in (0, 1):
            @pl.when(needed(b) & has_shard(way, dist))
            def _():
                shard = shard_at(way, dist)
                src = bufs[b].at[shard, rows(quarter, hh)]
                along(src, shard, b, hh, way, dist).wait_recv()
                if dist < mp - 1:
                    @pl.when(has_next(way))
                    def _():
                        along(src, shard, b, hh, way, dist + 1).start()
                across(1, shard, b, hh, quarter, way, dist, side).start()
                across(0, shard, b, hh, quarter, way, dist, core).start()
        if k == 0:
            own_send(3)

    def on_side(k):
        b, dist, hh = steps[k]
        for way in (0, 1):
            @pl.when(needed(b) & has_shard(way, dist))
            def _():
                shard = shard_at(way, dist)
                across(1, shard, b, hh, side_quarter, way, dist, side).wait_recv()
                across(2, shard, b, hh, side_quarter, way, dist, core).start()

    def complete(k):
        b, dist, hh = steps[k]
        for way in (0, 1):
            @pl.when(needed(b) & has_shard(way, dist))
            def _():
                shard = shard_at(way, dist)
                across(0, shard, b, hh, core_quarter, way, dist, core).wait_recv()
                across(2, shard, b, hh, diag_quarter, way, dist, core).wait_recv()

    done = [0, 0, 0]

    def service(lined, sided, completed):
        while done != [lined, sided, completed]:
            for which, (act, goal, ahead) in enumerate(((on_line, lined, 0), (on_side, sided, 2), (complete, completed, 4))):
                if done[which] < goal and (which == 0 or done[which] + ahead <= done[0] or done[0] == lined):
                    act(done[which])
                    done[which] += 1

    def drain():
        for hop in range(1, mp):
            small_copy(hop, me).wait_send()
        for b in range(BLOCKS):
            for hh in range(HALVES):
                for way in (0, 1):
                    @pl.when(needed(b) & has_next(way))
                    def _():
                        along(own_src(b, hh), me, b, hh, way, 1).wait_send()
        for b, dist, hh in steps:
            for way in (0, 1):
                @pl.when(needed(b) & has_shard(way, dist))
                def _():
                    shard = shard_at(way, dist)
                    across(0, shard, b, hh, quarter, way, dist, core).wait_send()
                    across(1, shard, b, hh, quarter, way, dist, side).wait_send()
                    across(2, shard, b, hh, side_quarter, way, dist, core).wait_send()
                    if dist < mp - 1:
                        @pl.when(has_next(way))
                        def _():
                            along(bufs[b].at[shard, rows(quarter, hh)], shard, b, hh, way, dist + 1).wait_send()

    def shard_of(i):
        return jnp.where(lax.rem(i, 2) == 0, mp - 1 - i // 2, i // 2)

    spots = 3 * mp + mp * section

    def place(b, i):
        return (spots - mp + i, 2 * mp + i, 2 * i + 1, 2 * i)[b]

    def piece(b, m, which):
        return bufs[b].at[m, rows(which)]

    def to_core(b, i, m, k):
        return pltpu.make_async_remote_copy(
            src_ref=piece(b, m, 2 * k + 1 - parity), dst_ref=from_core.at[lax.rem(place(b, i), RING), k],
            send_sem=c_send.at[b, m, k], recv_sem=c_recv.at[b, m, k],
            device_id={"dp": core}, device_id_type=MESH)

    def to_side(b, m):
        return pltpu.make_async_remote_copy(
            src_ref=piece(b, m, 2 * (1 - half) + parity), dst_ref=from_side.at[b, m],
            send_sem=y_send.at[b, m], recv_sem=y_recv.at[b, m],
            device_id={"dp": side}, device_id_type=MESH)

    def line_slot(way, m, at):
        return m if way == 0 else jnp.where(m == at, mp, m)

    def to_line(way, b, m):
        to = me + 1 - 2 * way
        return pltpu.make_async_remote_copy(
            src_ref=piece(b, m, quarter), dst_ref=from_line.at[line_slot(way, m, to), b],
            send_sem=r_send.at[way, b, m], recv_sem=r_recv.at[way, b, m],
            device_id={"mp": to}, device_id_type=MESH)

    def add(b, m, which, other):
        ref = piece(b, m, which)
        ref[...] = (ref[...].astype(f32) + other[...].astype(f32)).astype(bf16)

    def send_core(b, i):
        @pl.when(needed(b))
        def _():
            @pl.when(place(b, i) >= RING)
            def _():
                pl.semaphore_wait(credit, 1)
            for k in (0, 1):
                to_core(b, i, shard_of(i), k).start()

    def stage_core(b, i):
        m = shard_of(i)
        spot = place(b, i)

        @pl.when(needed(b))
        def _():
            for k in (0, 1):
                to_core(b, i, m, k).wait_recv()
                add(b, m, 2 * k + parity, from_core.at[lax.rem(spot, RING), k])
            to_side(b, m).start()

            @pl.when(spot + RING < spots)
            def _():
                pl.semaphore_signal(credit, inc=1, device_id={"dp": core}, device_id_type=MESH)

    def stage_side(b, i):
        m = shard_of(i)

        @pl.when(needed(b))
        def _():
            to_side(b, m).wait_recv()
            add(b, m, quarter, from_side.at[b, m])
            for way in (0, 1):
                first = (me == 0) if way == 0 else (me == mp - 1)

                @pl.when(first & (me != m))
                def _():
                    to_line(way, b, m).start()

    def stage_line(b, i):
        m = shard_of(i)
        for way in (0, 1):
            inner = ((me > 0) & (me < m)) if way == 0 else ((me < mp - 1) & (me > m))

            @pl.when(needed(b) & inner)
            def _():
                to_line(way, b, m).wait_recv()
                add(b, m, quarter, from_line.at[m, b])
                to_line(way, b, m).start()

    def prepare(rws):
        x = x_ref[rws].astype(f32)
        h[rws] = norm(x, vec_ref[0:1], vec_ref[1:2]).astype(bf16)
        x1[rws] = x + vec_ref[2:3]
    row_loop(total, 256, prepare)
    for hop in range(1, mp):
        small_copy(hop, lax.rem(me + mp - hop, mp)).wait_recv()

    query_at = lax.broadcasted_iota(jnp.int32, (1, length), 1)
    limits, frames = [], []
    for u in range(utts):
        last = lens_ref[u] - 1
        limits.append(jnp.where(decoding, jnp.minimum(query_at, last), last))
        frames.append(jnp.full((1, length), lens_ref[utts + u] - 1, jnp.int32))
    lane = lax.broadcasted_iota(jnp.int32, (1, PROJ), 1)
    scale = jnp.where((lane >= KV) & (lane < KV + part), 0.125, 1.0)

    def self_shard(m, carry):
        def keep(cols, value):
            qkv[m, :, cols] = ((value + smalls[m, 0:1, cols]) * scale[:, cols]).astype(bf16)
        wide_dot(nt, h[...], lambda s, n: wa[m, s:s + n], PROJ, keep)
        attend(m, length, range(utts), qkv, ctx, p, limits, smalls)
        x1[...] += nn(ctx[m], wa[m, CTX:])
        return carry

    def ffn_one(m):
        ffn_shard(m, h, w1, w2, a, gp, smalls[m, 2:3], out)

    def ffn_at(dist):
        @pl.when(encoding)
        def _():
            def step(way, carry):
                @pl.when(jnp.where(way == 0, me >= dist, me + dist <= mp - 1))
                def _():
                    ffn_one(jnp.where(way == 0, me - dist, me + dist))
                return carry
            lax.fori_loop(0, 2, step, 0)

    H = HALVES
    service(8 * H, 7 * H, 7 * H)
    lax.fori_loop(0, mp // 2, self_shard, 0)
    service(9 * H, 8 * H, 7 * H)
    lax.fori_loop(mp // 2, mp, self_shard, 0)
    for copy in own_w:
        copy.wait()
    spill = [pltpu.make_async_copy(src, dst, i_sem.at[j]) for j, (src, dst) in enumerate(
        ((qkv, qkv_hbm), (ctx, ctx_hbm), (p, p_hbm)))]
    fetch = [pltpu.make_async_copy(dst, src, i_sem.at[j]) for j, (src, dst) in enumerate(
        ((qkv, qkv_hbm), (ctx, ctx_hbm), (p, p_hbm)))]
    give = pltpu.make_async_copy(out, out_hbm, i_sem.at[3])

    @pl.when(decoding)
    def _():
        for copy in spill:
            copy.start()

        def start_cross(rws):
            y = x1[rws]
            hc[rws] = norm(y, vec_ref[3:4], vec_ref[4:5]).astype(bf16)
            y2[rws] = y
        row_loop(total, 256, start_cross)

    @pl.when(encoding)
    def _():
        ffn_start(total, x1, out, h, vec_ref)
        ffn_one(me)

    service(10 * H, 9 * H, 8 * H)
    ffn_at(1)

    @pl.when(decoding)
    def _():
        for copy in spill:
            copy.wait()

        def queries(m, carry):
            pq = nt(hc[...], wc[m, KV:PROJ])
            qkv[m, :, KV:] = ((pq + smalls[m, 1:2, KV:PROJ]) * scale[:, KV:]).astype(bf16)
            return carry
        lax.fori_loop(0, mp, queries, 0)

    service(11 * H, 10 * H, 10 * H)
    ffn_at(2)
    service(12 * H, 12 * H, 12 * H)
    ffn_at(3)

    @pl.when(encoding)
    def _():
        for u in range(utts):
            mem[utt(u)] = norm(out[utt(u)], vec_ref[3:4], vec_ref[4:5]).astype(bf16)
            over_mem(u).start()
        give.start()
        drain()
        g[...] = cot_ref[...].astype(f32)
        for u in range(utts):
            over_dmem(u).wait_recv()
        norm_back(total, out, vec_ref[3:4], dmem, g, vg, 3)
        give.wait()

        vg[7:8, :] = jnp.sum(g[...], axis=0, keepdims=True)
        dy[...] = g[...].astype(bf16)
        turn(dyt, dy[...])
        turn(ht, h[...])
        dh[...] = jnp.zeros_like(dh)

        def ffn_step(i, carry):
            m = shard_of(i)
            ffn_dgrad_shard(m, gp, w1, w2, dy, dh, sg)
            w2[m] = nn(dyt[...], a[m]).astype(bf16)
            send_core(3, i)
            w1[m] = nn(ht[...], gp[m]).astype(bf16)
            send_core(2, i)

            @pl.when(i > 0)
            def _():
                stage_core(3, i - 1)
                stage_core(2, i - 1)
            return carry
        lax.fori_loop(0, mp, ffn_step, 0)
        norm_back(total, x1, vec_ref[5:6], dh, g, vg, 5)
        stage_core(3, mp - 1)
        stage_core(2, mp - 1)
        over_cb.wait_recv()
        sg[:, 1:2, :PROJ] = cb[:, 0:1, :]

    @pl.when(decoding)
    def _():
        for u in range(utts):
            over_mem(u).wait_recv()
            rws = slice(u * length, (u + 1) * length)

            def cross_shard(m, carry):
                pk = nt(mem[rws], wc[m, :KV])
                qkv[m, rws, :KV] = (pk + smalls[m, 1:2, :KV]).astype(bf16)
                attend(m, length, (u,), qkv, ctx, p, frames, None)
                y2[rws] += nn(ctx[m, rws], wc[m, CTX:])
                return carry
            lax.fori_loop(0, mp, cross_shard, 0)

        ffn_start(total, y2, out, h, vec_ref)

        def one(m, carry):
            ffn_one(m)
            return carry
        lax.fori_loop(0, mp, one, 0)
        give.start()
        g[...] = cot_ref[...].astype(f32)
        vg[7:8, :] = jnp.sum(g[...], axis=0, keepdims=True)
        dy[...] = g[...].astype(bf16)
        turn(dyt, dy[...])
        turn(ht, h[...])
        drain()
        give.wait()
        dh[...] = jnp.zeros_like(dh)

        def dgrad(m, carry):
            ffn_dgrad_shard(m, gp, w1, w2, dy, dh, sg)
            return carry
        lax.fori_loop(0, mp, dgrad, 0)
        norm_back(total, y2, vec_ref[5:6], dh, g, vg, 5)

        def ffn_weights(i, carry):
            m = shard_of(i)
            w2[m] = nn(dyt[...], a[m]).astype(bf16)
            send_core(3, i)
            w1[m] = nn(ht[...], gp[m]).astype(bf16)
            send_core(2, i)

            @pl.when((i > 0) & (i != mp // 2))
            def _():
                stage_core(3, i - 1)
                stage_core(2, i - 1)
            return carry
        lax.fori_loop(0, mp // 2, ffn_weights, 0)

        dy[...] = g[...].astype(bf16)
        dh[...] = jnp.zeros_like(dh)
        for u in range(utts):
            rws = slice(u * length, (u + 1) * length)
            y2[rws] = jnp.zeros((length, y2.shape[1]), f32)

            def cross_back(m, carry):
                dctx[0, rws] = nt(dy[rws], wc[m, CTX:]).astype(bf16)
                attend_back(m, length, (u,), qkv, p, dctx, qkv, None, None)
                y2[rws] += nn(qkv[m, rws, :KV], wc[m, :KV])
                dh[rws] += nn(qkv[m, rws, KV:], wc[m, KV:PROJ])
                return carry
            lax.fori_loop(0, mp, cross_back, 0)
            dmem[utt(u)] = y2[rws].astype(bf16)
            over_dmem(u).start()
            if u == 0:
                stage_core(3, mp // 2 - 1)
                stage_core(2, mp // 2 - 1)
        lax.fori_loop(mp // 2, mp, ffn_weights, 0)

        def row_sums(m, carry):
            sums = jnp.sum(qkv[m].astype(f32), axis=0, keepdims=True)
            sg[m, 1:2, :PROJ] = sums
            cb[m, 0:1, :] = sums
            return carry
        lax.fori_loop(0, mp, row_sums, 0)
        over_cb.start()
        norm_back(total, x1, vec_ref[3:4], dh, g, vg, 3)
        turn(dyt, dy[...])
        turn(ht, hc[...])

        def cross_weights(i, carry):
            m = shard_of(i)
            wc[m, :, :KV] = tn(mem[...], qkv[m, :, :KV]).astype(bf16)
            gq = nn(ht[...], qkv[m, :, KV:])
            go = nn(dyt[...], ctx[m])
            wc[m, :, KV:CTX] = gq[:, :T].astype(bf16)
            wc[m, :, CTX:PROJ] = (gq[:, T:] + go[:, :T]).astype(bf16)
            wc[m, :, PROJ:] = go[:, T:].astype(bf16)

            @pl.when(i == 0)
            def _():
                stage_core(3, mp - 1)
                stage_core(2, mp - 1)
            send_core(1, i)

            @pl.when(i > 0)
            def _():
                stage_core(1, i - 1)
                stage_line(2, i - 1)
            stage_side(3, i)
            stage_side(2, i)
            stage_line(3, i)
            return carry
        lax.fori_loop(0, mp, cross_weights, 0)
        for copy in fetch:
            copy.start()
        stage_core(1, mp - 1)
        for copy in fetch:
            copy.wait()

    def prepare_self(rws):
        h[rws] = norm(x_ref[rws].astype(f32), vec_ref[0:1], vec_ref[1:2]).astype(bf16)
    row_loop(total, 256, prepare_self)
    vg[2:3, :] = jnp.sum(g[...], axis=0, keepdims=True)
    dy[...] = g[...].astype(bf16)
    turn(dyt, dy[...])
    turn(ht, h[...])
    dh[...] = jnp.zeros_like(dh)
    down = lax.broadcasted_iota(jnp.int32, (length, length), 0)
    right = lax.broadcasted_iota(jnp.int32, (length, length), 1)
    flip = (down + right == length - 1).astype(f32).astype(bf16)

    def self_step(i, carry):
        m = shard_of(i)
        dctx[0] = nt(dy[...], wa[m, CTX:]).astype(bf16)
        attend_back(m, length, range(utts), qkv, p, dctx, qkv, sg, flip)
        d = qkv[m]
        sg[m, 0:1, :PROJ] = jnp.sum(d.astype(f32), axis=0, keepdims=True)
        dh[...] += nn(d, wa[m, :PROJ])
        gd = nn(ht[...], d)
        go = nn(dyt[...], ctx[m])
        wa[m, :, :CTX] = gd[:, :CTX].astype(bf16)
        wa[m, :, CTX:PROJ] = (gd[:, CTX:] + go[:, :T]).astype(bf16)
        wa[m, :, PROJ:] = go[:, T:].astype(bf16)
        send_core(0, i)

        @pl.when(i > 0)
        def _():
            stage_core(0, i - 1)

        @pl.when(encoding)
        def _():
            @pl.when(i > 0)
            def _():
                stage_line(2, i - 1)
            stage_side(3, i)
            stage_side(2, i)
            stage_line(3, i)

        @pl.when(decoding)
        def _():
            @pl.when(i == 0)
            def _():
                stage_line(2, mp - 1)

            @pl.when(i > 0)
            def _():
                stage_line(1, i - 1)
            stage_side(1, i)
        return carry
    lax.fori_loop(0, mp, self_step, 0)
    stage_core(0, mp - 1)

    @pl.when(encoding)
    def _():
        stage_line(2, mp - 1)
    stage_line(1, mp - 1)
    norm_back(total, x_ref, vec_ref[0:1], dh, g, vg, 0)

    def group_small(hop, to, which):
        src, dst = ((vg, got_vg), (sg, got_sg))[which]
        return pltpu.make_async_remote_copy(
            src_ref=src, dst_ref=dst.at[hop], send_sem=a_send.at[hop, which], recv_sem=a_recv.at[hop, which],
            device_id={"dp": to}, device_id_type=MESH)

    mates = (core, side, diag)
    for hop, to in enumerate(mates):
        for which in (0, 1):
            group_small(hop, to, which).start()
    stage_side(0, 0)
    sum_sg[pl.ds(0, mp)] = sg[...]
    sum_sg[mp] = vg[...]
    for hop, to in enumerate(mates):
        for which in (0, 1):
            group_small(hop, to, which).wait_recv()
        sum_sg[pl.ds(0, mp)] += got_sg[hop]
        sum_sg[mp] += got_vg[hop]

    def line_small(hop, which):
        peer = lax.rem(me + hop, mp)
        src = sum_sg.at[peer] if which == 0 else sum_sg.at[mp]
        return pltpu.make_async_remote_copy(
            src_ref=src, dst_ref=got_line.at[hop - 1, which],
            send_sem=b_send.at[hop - 1, which], recv_sem=b_recv.at[hop - 1, which],
            device_id={"mp": peer}, device_id_type=MESH)

    for hop in range(1, mp):
        for which in (0, 1):
            line_small(hop, which).start()
    for i in range(1, mp):
        stage_side(0, i)
        stage_line(0, i - 1)
    stage_line(0, mp - 1)
    small_out[0] = sum_sg[me]
    small_out[1] = sum_sg[mp]
    for hop in range(1, mp):
        for which in (0, 1):
            line_small(hop, which).wait_recv()
            small_out[which] += got_line[hop - 1, which]

    stage = (x1.at[pl.ds(0, part)], x1.at[pl.ds(part, part)], y2.at[pl.ds(0, part)], y2.at[pl.ds(part, part)])

    def finish(b):
        stage[b][...] = bufs[b][me, rows(quarter)].astype(f32)

        @pl.when(me > 0)
        def _():
            to_line(0, b, me).wait_recv()
            stage[b][...] += from_line[me, b].astype(f32)

        @pl.when(me < mp - 1)
        def _():
            to_line(1, b, me).wait_recv()
            stage[b][...] += from_line[mp, b].astype(f32)

    def hand(b):
        return pltpu.make_async_copy(stage[b], own_hbm.at[b], l_sem.at[b, 0])

    @pl.when(decoding)
    def _():
        finish(1)
        kv_grad[0] = stage[1][:, :2 * part].astype(bf16)
        over_kv.start()
        hand(1).start()
    for b in (3, 2, 0):
        finish(b)
        hand(b).start()

    @pl.when(encoding)
    def _():
        over_kv.wait_recv()
        stage[1][:, :2 * part] = kv_grad[1].astype(f32)
        hand(1).start()

    @pl.when(encoding)
    def _():
        for i in (0, 1):
            over_rows(i).wait_send()
        over_small.wait_send()
        for u in range(utts):
            over_mem(u).wait_send()

    @pl.when(decoding)
    def _():
        for u in range(utts):
            over_dmem(u).wait_send()
        over_cb.wait_send()
        over_kv.wait_send()
    for hop, to in enumerate(mates):
        for which in (0, 1):
            group_small(hop, to, which).wait_send()
    for hop in range(1, mp):
        for which in (0, 1):
            line_small(hop, which).wait_send()

    def left(i, carry):
        m = shard_of(i)
        for b in range(BLOCKS):
            @pl.when(needed(b))
            def _():
                for k in (0, 1):
                    to_core(b, i, m, k).wait_send()
                to_side(b, m).wait_send()
                for way in (0, 1):
                    @pl.when((me < m) if way == 0 else (me > m))
                    def _():
                        to_line(way, b, m).wait_send()
        return carry
    lax.fori_loop(0, mp, left, 0)
    for b in range(BLOCKS):
        hand(b).wait()


def layers(mp, dp, utts, length, lens, x, cot, vec, small, w_in, w_o, w_cross, w_one, w_two):
    total, width = x.shape
    hidden = w_one.shape[1]
    sds = jax.ShapeDtypeStruct
    v = pltpu.VMEM
    sem = pltpu.SemaphoreType.DMA
    shard = v((mp, width, hidden), bf16)
    part = width // 4
    wide_b, wide_f = v((total, width), bf16), v((total, width), f32)
    turned = v((width, total), bf16)
    heads = (utts, mp, HEADS, length, length)
    proj, context = (mp, total, PROJ), (mp, total, 2 * LANES)
    rows = small.shape
    gather = (2, mp - 1, BLOCKS, HALVES)
    return pl.pallas_call(
        functools.partial(layers_kernel, mp, dp, utts, length),
        out_shape=(sds((total, width), f32), sds((2,) + rows, f32), sds((total, width), f32),
                   sds((BLOCKS, part, hidden), f32), sds(proj, bf16), sds(context, bf16), sds(heads, bf16)),
        in_specs=[SMEM] + [VM] * 4 + [ANY] * 5,
        out_specs=(VM,) * 2 + (ANY,) * 5,
        scratch_shapes=[shard] * 4 + [
            v((mp,) + rows, f32), v(rows, f32), v(proj, bf16), v(context, bf16), v(heads, bf16),
            v((mp, total, hidden), bf16), v((mp, total, hidden), bf16),
            wide_f, wide_f, wide_f, wide_b, wide_b, wide_b, wide_b,
            wide_b, turned, turned, v((1,) + context[1:], bf16), v(vec.shape, f32), v((mp,) + rows, f32),
            v((mp, 8, PROJ), f32),
            v((RING, 2, part, hidden), bf16), v((BLOCKS, mp, part, hidden), bf16), v((mp + 1, BLOCKS, part, hidden), bf16),
            v((mp + 1,) + rows, f32), v((3,) + rows, f32), v((3, mp) + rows, f32), v((mp - 1, 2) + rows, f32),
            v((2, part, 2 * part), bf16),
            sem((BLOCKS, 4)), sem(gather), sem(gather), sem((3,) + gather), sem((3,) + gather),
            sem((mp - 1,)), sem((mp - 1,)), sem((5 + 2 * utts,)), sem((5 + 2 * utts,)), sem((4,)),
            sem((BLOCKS, mp, 2)), sem((BLOCKS, mp, 2)), sem((BLOCKS, mp)), sem((BLOCKS, mp)),
            sem((2, BLOCKS, mp)), sem((2, BLOCKS, mp)), pltpu.SemaphoreType.REGULAR,
            sem((3, 2)), sem((3, 2)), sem((mp - 1, 2)), sem((mp - 1, 2))],
        compiler_params=pltpu.CompilerParams(collective_id=0, has_side_effects=True, vmem_limit_bytes=63 * 2**20),
        name="both_layers",
    )(lens, x, cot, vec, small, w_in, w_o, w_cross, w_one, w_two)


def finish_kernel(mp, dp, length, rel, own, small, out_in, dx_in,
                  out, dx, vectors, in_grad, bias, o_grad, rel_grad, cross, one, b1, two):
    me = lax.axis_index("mp")
    dp_index = lax.axis_index("dp")
    decoding = lax.axis_index("section") == 1
    out[...] = out_in[...]
    dx[...] = dx_in[...]
    part = own.shape[1]
    k, v, q, o = (slice(t * part, (t + 1) * part) for t in range(4))
    mine = own[0]
    in_grad[0], in_grad[1], in_grad[2] = mine[:, q], mine[:, k], mine[:, v]
    o_grad[...] = mine[:, o].T
    mine = own[1]
    cross[0] = jnp.where(decoding, mine[:, q], mine[:, k])
    cross[1] = jnp.where(decoding, mine[:, o], mine[:, v])
    one[...] = own[2]
    two[...] = own[3]

    width = small.shape[2]

    def back(value, by):
        return pltpu.roll(value, lax.rem(width - by, width), 1)

    vectors[...] = back(small[1], (dp_index * mp + me) * vectors.shape[1])[:, :vectors.shape[1]]
    size = bias.shape[2]
    turned = back(small[0], dp_index * size)
    cross_row = jnp.where(decoding, turned[1:2, q], turned[1:2, v])
    for t, row in enumerate((turned[0:1, q], turned[0:1, v], cross_row)):
        for r in range(HEADS):
            bias[t, r:r + 1, :] = row[:, 64 * r:64 * r + size]
    size = b1.shape[1]
    turned = back(small[0], dp_index * size)
    for r in range(b1.shape[0]):
        b1[r:r + 1, :] = turned[2:3, 128 * r:128 * r + size]
    lines = small[0]
    low, high = length - rel // 2, length + rel // 2 - 2
    lane = lax.broadcasted_iota(jnp.int32, lines.shape, 1)
    first = jnp.sum(jnp.where(lane < low, lines, 0.0), axis=1, keepdims=True)
    last = jnp.sum(jnp.where((lane >= high) & (lane < 2 * length), lines, 0.0), axis=1, keepdims=True)
    moved = pltpu.roll(lines, width - (low - 1), 1)
    moved = jnp.where(lane == 0, first, jnp.where(lane == rel - 1, last, moved))
    rel_grad[...] = back(moved, dp_index * rel_grad.shape[1])[3:3 + HEADS, :rel_grad.shape[1]]


def finish(mp, dp, length, rel, own, small, out, dx):
    sds = jax.ShapeDtypeStruct
    part, hidden = own.shape[1:]
    width = small.shape[2]
    shard = width // mp
    return pl.pallas_call(
        functools.partial(finish_kernel, mp, dp, length, rel),
        out_shape=(sds(out.shape, f32), sds(dx.shape, f32), sds((8, width // (dp * mp)), f32),
                   sds((3, part, shard), f32), sds((3, HEADS, 64 // dp), f32), sds((shard, part), f32),
                   sds((HEADS, rel // dp), f32), sds((2, part, shard), f32), sds((part, hidden), f32),
                   sds((hidden // 128, 128 // dp), f32), sds((part, hidden), f32)),
        in_specs=[VM] * 4, out_specs=(VM,) * 11,
        compiler_params=pltpu.CompilerParams(vmem_limit_bytes=32 * 2**20), name="finish",
    )(own, small, out, dx)


def rel_line(table, length):
    half = table.shape[1] // 2
    heads = table.shape[0]
    first = jnp.broadcast_to(table[:, :1], (heads, length - half))
    last = jnp.broadcast_to(table[:, -1:], (heads, length - half))
    return jnp.concatenate([table[:, half:], last, first, table[:, :half]], axis=1)


def per_device(streams, lengths, vectors, attn_in, attn_bias, attn_out, rel_table, cross, ffn_in, ffn_bias, ffn_out,
               cotangent):
    decoding = lax.axis_index("section") == 1
    mp = lax.axis_size("mp")
    dp = lax.axis_size("dp")
    me = lax.axis_index("mp")
    utts, length, width = streams.shape[1:]
    total = utts * length
    x = streams[0].reshape(total, width)
    cot = cotangent[0].reshape(total, width)
    vec = vectors[0]

    lens = lax.dynamic_slice_in_dim(lengths, me * utts, utts, 1)
    lens = jnp.concatenate([jnp.where(decoding, lens[1], lens[0]), lens[0]])
    ext = rel_line(rel_table[0], length)
    biases = attn_bias[0].reshape(3, -1)
    none = jnp.zeros_like(biases[0])
    small = jnp.concatenate([jnp.concatenate([none, biases[1], biases[0], none])[None],
                             jnp.concatenate([none, biases[2], biases[2], none])[None],
                             ffn_bias[0].reshape(1, -1), jnp.pad(ext, ((0, 2), (0, width - ext.shape[1])))], axis=0)

    g, small_sum, out, own, _, _, _ = layers(
        mp, dp, utts, length, lens, x, cot, vec, small, jnp.swapaxes(attn_in[0], 1, 2), attn_out[0],
        jnp.swapaxes(cross[0], 1, 2), ffn_in[0], ffn_out[0])
    if dp > 4:
        near = [[q * (dp // 4) + i for i in range(dp // 4)] for q in range(4)]
        small_sum = lax.psum(small_sum, "dp", axis_index_groups=near)
    out, dx, vectors_grad, in_grad, bias_grad, o_grad, rel_grad, cross_grad, one_grad, b1_grad, two_grad = finish(
        mp, dp, length, rel_table.shape[2], own, small_sum, out, g)
    two_grad = two_grad.T
    if dp > 4:
        per = dp // 4
        groups = [[q * per + i for i in range(per)] for q in range(4)]

        def rest(value, axis):
            return lax.psum_scatter(value.astype(bf16), "dp", scatter_dimension=axis, axis_index_groups=groups,
                                    tiled=True).astype(f32)

        in_grad, o_grad, cross_grad = rest(in_grad, 1), rest(o_grad, 1), rest(cross_grad, 1)
        one_grad, two_grad = rest(one_grad, 0), rest(two_grad, 1)
    shape = (1, utts, length, width)
    return (out.reshape(shape), dx.reshape(shape), vectors_grad[None], in_grad[None], bias_grad[None], o_grad[None],
            rel_grad[None], cross_grad[None], one_grad[None], b1_grad[None], two_grad[None])


def solution(mesh):
    placed = (
        P("section", ("dp", "mp"), None, None),
        P(None, "dp"),
        P("section", None, None),
        P("section", None, None, "mp"),
        P("section", None, "mp", None),
        P("section", "mp", None),
        P("section", "mp", None),
        P("section", None, None, "mp"),
        P("section", None, "mp"),
        P("section", "mp", None),
        P("section", "mp", None),
        P("section", ("dp", "mp"), None, None),
    )
    return jax.shard_map(
        per_device,
        mesh=mesh,
        in_specs=placed,
        out_specs=(
            P("section", ("dp", "mp"), None, None),
            P("section", ("dp", "mp"), None, None),
            P("section", None, ("dp", "mp")),
            P("section", None, "dp", "mp"),
            P("section", None, "mp", "dp"),
            P("section", "mp", "dp"),
            P("section", "mp", "dp"),
            P("section", None, "dp", "mp"),
            P("section", "dp", "mp"),
            P("section", "mp", "dp"),
            P("section", "mp", "dp"),
        ),
        check_vma=False,
    )
```

```python
import functools
import jax
import jax.numpy as jnp
from jax import lax
from jax.experimental import pallas as pl
from jax.experimental.pallas import tpu as pltpu
from jax.sharding import PartitionSpec as P

MESH = pl.DeviceIdType.MESH
ANY = pl.BlockSpec(memory_space=pl.ANY)
VM = pl.BlockSpec(memory_space=pltpu.VMEM)
BLOCKS = 4


def partners(dp_index, step):
    bit = lax.rem(dp_index // step, 2)
    return dp_index + step - 2 * step * bit


EPSILON = 1e-05
MASKED = -1e30
HEADS = 3
LANES = 128
PROJ = 640
CTX = 512
bf16, f32 = jnp.bfloat16, jnp.float32


def nn(a, b):
    return lax.dot_general(a, b, (((1,), (0,)), ((), ())), preferred_element_type=f32)


def nt(a, b):
    return lax.dot_general(a, b, (((1,), (1,)), ((), ())), preferred_element_type=f32)


def tn(a, b):
    return lax.dot_general(a, b, (((0,), (0,)), ((), ())), preferred_element_type=f32)


def norm_parts(x):
    centred = x - jnp.mean(x, axis=-1, keepdims=True)
    r = lax.rsqrt(jnp.mean(centred * centred, axis=-1, keepdims=True) + EPSILON)
    return centred * r, r


def norm(x, gain, shift):
    xh, _ = norm_parts(x)
    return xh * gain + shift


def row_loop(total, size, body):
    def step(i, carry):
        body(pl.ds(pl.multiple_of(i * size, size), size))
        return carry
    lax.fori_loop(0, total // size, step, 0)


def even_lanes(rows):
    return lax.broadcasted_iota(jnp.int32, (rows, LANES), 1) < LANES // 2


def half_mask(half):
    lane = lax.broadcasted_iota(jnp.int32, (1, LANES), 1)
    on = (lane < LANES // 2) if half == 0 else (lane >= LANES // 2)
    return on.astype(f32).astype(bf16)


def tile(ref, m, rows, t):
    return ref[m, rows, t * LANES:(t + 1) * LANES]


HEAD_TILES = (((3, 0), (0, 0), (1, 1), (0, 1)),
              ((3, 1), (0, 1), (2, 0), (1, 0)),
              ((4, 0), (1, 0), (2, 1), (1, 1)))


def utt_rows(u, length):
    return pl.ds(u * length, length) if isinstance(u, int) else pl.ds(pl.multiple_of(u * length, length), length)


def attend(pairs, length, qkv_ref, ctx_ref, p_ref, limits, ext_ref):
    key_at = lax.broadcasted_iota(jnp.int32, (length, length), 0)
    even = even_lanes(length)
    parts, probs, biases = {}, {}, {}
    for r in range(HEADS):
        (qt, half), (kt, _), (vt, _), _ = HEAD_TILES[r]
        for n, (m, u) in enumerate(pairs):
            rows = utt_rows(u, length)
            s = nt(tile(qkv_ref, m, rows, kt) * half_mask(half), tile(qkv_ref, m, rows, qt))
            if ext_ref is not None:
                if (id(m), r) not in biases:
                    row = ext_ref[m, 3 + r:4 + r, :2 * length]
                    biases[id(m), r] = pltpu.roll(jnp.broadcast_to(row, (length, 2 * length)), 0, 1, stride=1,
                                                  stride_axis=0)[:, :length].T
                s = s + biases[id(m), r]
            s = jnp.where(key_at <= limits(u), s, MASKED)
            e = jnp.exp(s - jnp.max(s, axis=0, keepdims=True))
            p = (e * (1.0 / jnp.sum(e, axis=0, keepdims=True))).astype(bf16)
            probs[n, r] = p
            parts[n, r] = tn(p, tile(qkv_ref, m, rows, vt))
    for n, (m, u) in enumerate(pairs):
        rows = utt_rows(u, length)
        for r in range(HEADS):
            p_ref[u, m, r] = probs[n, r]
        ctx_ref[m, rows, :LANES] = jnp.where(even, 0.0, parts[n, 0]).astype(bf16)
        ctx_ref[m, rows, LANES:] = jnp.where(even, parts[n, 1], parts[n, 2]).astype(bf16)


def attend_back(pairs, length, qkv_ref, p_ref, dctx_of, out_ref, rel_ref, flip):
    even = even_lanes(length)
    got, total = {}, {}
    for r in range(HEADS):
        (qt, _), (kt, _), (vt, vhalf), (ot, _) = HEAD_TILES[r]
        for n, (m, u) in enumerate(pairs):
            rows = utt_rows(u, length)
            p = p_ref[u, m, r]
            dctx = dctx_of(m, rows, ot)
            dp = nt(tile(qkv_ref, m, rows, vt) * half_mask(vhalf), dctx)
            pf = p.astype(f32)
            t = pf * dp
            ds = (t - pf * jnp.sum(t, axis=0, keepdims=True)).astype(bf16)
            got[n, r] = (tn(ds, tile(qkv_ref, m, rows, kt)) * 0.125, nn(ds, tile(qkv_ref, m, rows, qt)), nn(p, dctx))
            if rel_ref is not None:
                turned = nn(ds, flip)
                total[r] = total[r] + turned if r in total else turned
    for r in total:
        m = pairs[0][0]
        wide = jnp.concatenate([total[r], jnp.zeros_like(total[r])], axis=1)
        wide = pltpu.roll(wide, 0, 1, stride=1, stride_axis=0)
        rel_ref[m, 3 + r:4 + r, :2 * length] = jnp.sum(wide, axis=0, keepdims=True)
    for n, (m, u) in enumerate(pairs):
        rows = utt_rows(u, length)
        (q0, k0, v0), (q1, k1, v1), (q2, k2, v2) = got[n, 0], got[n, 1], got[n, 2]
        for t, (left, right) in enumerate(((k0, k1), (k2, v0), (v1, v2), (q0, q1), (q2, 0.0))):
            out_ref[m, rows, t * LANES:(t + 1) * LANES] = jnp.where(even, left, right).astype(bf16)


def gelu_both(u):
    cdf = 0.5 + 0.5 * lax.erf(u * 0.7071067811865476)
    return u * cdf, cdf + u * (jnp.exp(-0.5 * u * u) * 0.3989422804014327)


def norm_back(total, x_ref, gain, dh_ref, add_into, vg_ref, gain_row, grad_out=None):
    width = gain.shape[-1]

    def step(i, carry):
        dgain, dshift = carry
        rows = pl.ds(pl.multiple_of(i * 256, 256), 256)
        dh = dh_ref[rows].astype(f32)
        xh, r = norm_parts(x_ref[rows].astype(f32))
        e = dh * gain
        dx = r * (e - jnp.mean(e, axis=-1, keepdims=True) - xh * jnp.mean(e * xh, axis=-1, keepdims=True))
        add_into[rows] = add_into[rows].astype(f32) + dx
        return dgain + jnp.sum(dh * xh, axis=0, keepdims=True), dshift + jnp.sum(dh, axis=0, keepdims=True)

    zero = jnp.zeros((1, width), f32)
    dgain, dshift = lax.fori_loop(0, total // 256, step, (zero, zero))
    vg_ref[gain_row:gain_row + 1, :] = dgain
    vg_ref[gain_row + 1:gain_row + 2, :] = dshift


def turn(dst_ref, src):
    dst_ref[...] = src.T


SMEM = pl.BlockSpec(memory_space=pltpu.SMEM)


SEQUENCE = ((0, 1), (2, 1), (0, 2), (3, 1), (0, 3), (1, 1), (2, 2), (1, 2), (3, 2), (1, 3), (2, 3), (3, 3))
HALVES = 2
RING = 4


def wide_dot(dot, a, b_cols, width, use, step=256):
    for start in range(0, width, step):
        size = min(step, width - start)
        use(slice(start, start + size), dot(a, b_cols(start, size)))


def ffn_shard(m, h, w1, w2, a, gp, bias, out):
    def keep(cols, u):
        act, slope = gelu_both(u + bias[:, cols])
        a[m, :, cols] = act.astype(bf16)
        gp[m, :, cols] = slope.astype(bf16)
    wide_dot(nn, h[...], lambda s, n: w1[m, :, s:s + n], w1.shape[2], keep)
    out[...] += nn(a[m], w2[m])


def ffn_start(total, x_ref, out_ref, h_ref, vec_ref):
    def prepare(rows):
        x = x_ref[rows]
        h_ref[rows] = norm(x, vec_ref[5:6], vec_ref[6:7]).astype(bf16)
        out_ref[rows] = x + vec_ref[7:8]
    row_loop(total, 256, prepare)


def hidden_grad(m, gp, w2, dy, sg):
    def keep(cols, da):
        du = (da * gp[m, :, cols].astype(f32)).astype(bf16)
        gp[m, :, cols] = du
        sg[m, 2:3, cols] = jnp.sum(du.astype(f32), axis=0, keepdims=True)
    wide_dot(nt, dy[...], lambda s, n: w2[m, s:s + n], w2.shape[1], keep)


def layers_kernel(mp, dp, utts, length,
                  lens_ref, x_ref, cot_ref, vec_ref, small_ref, in_ref, o_ref, cross_ref, w1_ref, w2_ref,
                  g, small_out, out_hbm, own_hbm, qkv_hbm, ctx_hbm, p_hbm,
                  wa, wc, w1, w2, smalls, peer_small, qkv, ctx, p, a, gp, x1, y2, out, h, hc, mem, dmem,
                  dy, dyt, ht, dctx, sg, cb, from_core, from_side, from_line, pair_sg, got_small, got_line,
                  kv_grad,
                  l_sem, z_send, z_recv, p_send, p_recv, s_send, s_recv, x_send, x_recv, i_sem,
                  c_send, c_recv, y_send, y_recv, r_send, r_recv, credit, a_send, a_recv, b_send, b_recv):
    me = lax.axis_index("mp")
    dp_index = lax.axis_index("dp")
    section = lax.axis_index("section")
    decoding = section == 1
    encoding = section == 0
    near = dp // 4
    core = partners(dp_index, near)
    side = partners(dp_index, 2 * near)
    quarter = dp_index // near
    parity = lax.rem(quarter, 2)
    half = quarter // 2
    core_quarter = quarter + 1 - 2 * parity
    side_quarter = quarter + 2 - 4 * half
    diag_quarter = core_quarter + 2 - 4 * half
    part = wa.shape[1] // 4
    total = utts * length
    T = LANES
    KV, PROJ_END = 3 * T, PROJ
    bufs = (wa, wc, w1, w2)
    dh = out
    vg = sg.at[mp]

    barrier = pltpu.get_barrier_semaphore()
    for hop in range(1, mp):
        pl.semaphore_signal(barrier, inc=1, device_id={"mp": lax.rem(me + hop, mp)}, device_id_type=MESH)
    for other in (core, side):
        pl.semaphore_signal(barrier, inc=1, device_id={"dp": other}, device_id_type=MESH)
    pl.semaphore_signal(barrier, inc=1, device_id={"section": 1 - section}, device_id_type=MESH)

    def needed(b):
        return decoding if b == 1 else me >= 0

    def utt(u):
        return utt_rows(u, length)

    def own_rows(b, t, src):
        return pltpu.make_async_copy(src, bufs[b].at[me, t * part:(t + 1) * part], l_sem.at[b, t])

    own_a = [own_rows(0, 0, in_ref.at[1]), own_rows(0, 1, in_ref.at[2]), own_rows(0, 2, in_ref.at[0]),
             own_rows(0, 3, o_ref)]
    own_c = [own_rows(1, 2, cross_ref.at[0]), own_rows(1, 3, cross_ref.at[1])]
    own_w = [pltpu.make_async_copy(src, bufs[b].at[me], l_sem.at[b, 0]) for b, src in ((2, w1_ref), (3, w2_ref))]
    for copy in own_a:
        copy.start()

    @pl.when(decoding)
    def _():
        for copy in own_c:
            copy.start()
    for copy in own_w:
        copy.start()
    cotangent = pltpu.make_async_copy(cot_ref, dy, l_sem.at[1, 0])
    cotangent.start()
    pl.semaphore_wait(barrier, mp + 2)
    for copy in own_a:
        copy.wait()

    def rows(which, hh=None):
        if hh is None:
            return pl.ds(pl.multiple_of(which * part, 16), part)
        size = part // HALVES
        return pl.ds(pl.multiple_of(which * part + hh * size, 16), size)

    def along(src, shard, b, hh, way, dist):
        return pltpu.make_async_remote_copy(
            src_ref=src, dst_ref=bufs[b].at[shard, rows(quarter, hh)],
            send_sem=z_send.at[way, dist - 1, b, hh], recv_sem=z_recv.at[way, dist - 1, b, hh],
            device_id={"mp": me + 1 - 2 * way}, device_id_type=MESH)

    def across(kind, shard, b, hh, which, way, dist, to):
        ref = bufs[b].at[shard, rows(which, hh)]
        return pltpu.make_async_remote_copy(
            src_ref=ref, dst_ref=ref,
            send_sem=p_send.at[kind, way, dist - 1, b, hh], recv_sem=p_recv.at[kind, way, dist - 1, b, hh],
            device_id={"dp": to}, device_id_type=MESH)

    def small_copy(hop, slot):
        return pltpu.make_async_remote_copy(
            src_ref=smalls.at[me], dst_ref=smalls.at[slot],
            send_sem=s_send.at[hop - 1], recv_sem=s_recv.at[hop - 1],
            device_id={"mp": lax.rem(me + hop, mp)}, device_id_type=MESH)

    def over(index, src, dst):
        return pltpu.make_async_remote_copy(
            src_ref=src, dst_ref=dst, send_sem=x_send.at[index], recv_sem=x_recv.at[index],
            device_id={"section": 1 - section}, device_id_type=MESH)

    def over_rows(i):
        return over(i, cross_ref.at[i], wc.at[me, i * part:(i + 1) * part])

    def over_mem(u):
        return over(3 + u, mem.at[utt(u)], mem.at[utt(u)])

    def over_dmem(u):
        return over(3 + utts + u, dmem.at[utt(u)], dmem.at[utt(u)])

    over_small = over(2, small_ref, peer_small)
    over_cb = over(3 + 2 * utts, cb, cb)
    over_kv = over(4 + 2 * utts, kv_grad.at[0], kv_grad.at[1])

    def has_next(way):
        return (me < mp - 1) if way == 0 else (me > 0)

    def has_shard(way, dist):
        return (me >= dist) if way == 0 else (me + dist <= mp - 1)

    def shard_at(way, dist):
        return me - dist if way == 0 else me + dist

    def own_src(b, hh):
        src = (wa.at[me], wc.at[me], w1_ref, w2_ref)[b]
        return src.at[rows(quarter, hh)]

    def own_send(b):
        for hh in range(HALVES):
            for way in (0, 1):
                @pl.when(needed(b) & has_next(way))
                def _():
                    along(own_src(b, hh), me, b, hh, way, 1).start()

    own_send(0)

    @pl.when(encoding)
    def _():
        for i in (0, 1):
            over_rows(i).start()
        over_small.start()
        smalls[me] = small_ref[...]
    own_send(2)

    @pl.when(decoding)
    def _():
        over_small.wait_recv()
        smalls[me] = small_ref[...]
        lane = lax.broadcasted_iota(jnp.int32, (1, small_ref.shape[1]), 1)
        smalls[me, 1:2] = jnp.where(lane < 2 * part, peer_small[1:2], small_ref[1:2])
    for hop in range(1, mp):
        small_copy(hop, me).start()

    steps = [(b, dist, hh) for b, dist in SEQUENCE for hh in range(HALVES)]

    def on_line(k):
        b, dist, hh = steps[k]
        for way in (0, 1):
            @pl.when(needed(b) & has_shard(way, dist))
            def _():
                shard = shard_at(way, dist)
                src = bufs[b].at[shard, rows(quarter, hh)]
                along(src, shard, b, hh, way, dist).wait_recv()
                if dist < mp - 1:
                    @pl.when(has_next(way))
                    def _():
                        along(src, shard, b, hh, way, dist + 1).start()
                across(1, shard, b, hh, quarter, way, dist, side).start()
                across(0, shard, b, hh, quarter, way, dist, core).start()
        if k == 0:
            own_send(3)
        if k == 2 * HALVES:
            @pl.when(decoding)
            def _():
                for copy in own_c:
                    copy.wait()
                for i in (0, 1):
                    over_rows(i).wait_recv()
            own_send(1)

    def on_side(k):
        b, dist, hh = steps[k]
        for way in (0, 1):
            @pl.when(needed(b) & has_shard(way, dist))
            def _():
                shard = shard_at(way, dist)
                across(1, shard, b, hh, side_quarter, way, dist, side).wait_recv()
                across(2, shard, b, hh, side_quarter, way, dist, core).start()

    def complete(k):
        b, dist, hh = steps[k]
        for way in (0, 1):
            @pl.when(needed(b) & has_shard(way, dist))
            def _():
                shard = shard_at(way, dist)
                across(0, shard, b, hh, core_quarter, way, dist, core).wait_recv()
                across(2, shard, b, hh, diag_quarter, way, dist, core).wait_recv()

    def run(*events):
        for event in events:
            act = {"L": on_line, "S": on_side, "P": complete}[event[0]]
            for hh in range(HALVES):
                act(int(event[1:]) * HALVES + hh)

    def drain():
        for hop in range(1, mp):
            small_copy(hop, me).wait_send()
        for b in range(BLOCKS):
            for hh in range(HALVES):
                for way in (0, 1):
                    @pl.when(needed(b) & has_next(way))
                    def _():
                        along(own_src(b, hh), me, b, hh, way, 1).wait_send()
        for b, dist, hh in steps:
            for way in (0, 1):
                @pl.when(needed(b) & has_shard(way, dist))
                def _():
                    shard = shard_at(way, dist)
                    across(0, shard, b, hh, quarter, way, dist, core).wait_send()
                    across(1, shard, b, hh, quarter, way, dist, side).wait_send()
                    across(2, shard, b, hh, side_quarter, way, dist, core).wait_send()
                    if dist < mp - 1:
                        @pl.when(has_next(way))
                        def _():
                            along(bufs[b].at[shard, rows(quarter, hh)], shard, b, hh, way, dist + 1).wait_send()

    def shard_of(i):
        return jnp.where(lax.rem(i, 2) == 0, mp - 1 - i // 2, i // 2)

    spots = 3 * mp + mp * section

    def place(b, i):
        return (spots - mp + i, 2 * mp + i, 2 * i + 1, 2 * i)[b]

    def piece(b, m, which, hh=None):
        return bufs[b].at[m, rows(which, hh)]

    cut = part // HALVES

    def to_core(b, i, m, k):
        return pltpu.make_async_remote_copy(
            src_ref=piece(b, m, 2 * k + 1 - parity), dst_ref=from_core.at[lax.rem(place(b, i), RING), k],
            send_sem=c_send.at[b, m, k], recv_sem=c_recv.at[b, m, k],
            device_id={"dp": core}, device_id_type=MESH)

    def to_side(b, m, hh):
        return pltpu.make_async_remote_copy(
            src_ref=piece(b, m, 2 * (1 - half) + parity, hh), dst_ref=from_side.at[b, m, pl.ds(hh * cut, cut)],
            send_sem=y_send.at[b, m, hh], recv_sem=y_recv.at[b, m, hh],
            device_id={"dp": side}, device_id_type=MESH)

    def line_slot(way, m, at):
        return m if way == 0 else jnp.where(m == at, mp, m)

    def to_line(way, b, m, hh):
        to = me + 1 - 2 * way
        return pltpu.make_async_remote_copy(
            src_ref=piece(b, m, quarter, hh), dst_ref=from_line.at[line_slot(way, m, to), b, pl.ds(hh * cut, cut)],
            send_sem=r_send.at[way, b, m, hh], recv_sem=r_recv.at[way, b, m, hh],
            device_id={"mp": to}, device_id_type=MESH)

    def add(b, m, which, other, hh=None):
        ref = piece(b, m, which, hh)
        ref[...] = (ref[...].astype(f32) + other[...].astype(f32)).astype(bf16)

    def send_core(b, i):
        @pl.when(needed(b))
        def _():
            @pl.when(place(b, i) >= RING)
            def _():
                pl.semaphore_wait(credit, 1)
            for k in (0, 1):
                to_core(b, i, shard_of(i), k).start()

    def stage_core(b, i):
        m = shard_of(i)
        spot = place(b, i)

        @pl.when(needed(b))
        def _():
            for k in (0, 1):
                to_core(b, i, m, k).wait_recv()
                add(b, m, 2 * k + parity, from_core.at[lax.rem(spot, RING), k])
            for hh in range(HALVES):
                to_side(b, m, hh).start()

            @pl.when(spot + RING < spots)
            def _():
                pl.semaphore_signal(credit, inc=1, device_id={"dp": core}, device_id_type=MESH)

    def stage_side(b, i):
        m = shard_of(i)

        @pl.when(needed(b))
        def _():
            for hh in range(HALVES):
                to_side(b, m, hh).wait_recv()
                add(b, m, quarter, from_side.at[b, m, pl.ds(hh * cut, cut)], hh)
                for way in (0, 1):
                    first = (me == 0) if way == 0 else (me == mp - 1)

                    @pl.when(first & (me != m))
                    def _():
                        to_line(way, b, m, hh).start()

    def stage_line(b, i, hop):
        m = shard_of(i)
        for way in (0, 1):
            inner = ((me == hop) & (me < m)) if way == 0 else ((me == mp - 1 - hop) & (me > m))

            @pl.when(needed(b) & inner)
            def _():
                for hh in range(HALVES):
                    to_line(way, b, m, hh).wait_recv()
                    add(b, m, quarter, from_line.at[m, b, pl.ds(hh * cut, cut)], hh)
                    to_line(way, b, m, hh).start()

    def ffn_ticks(i):
        stage_side(3, i)

        @pl.when(i > 0)
        def _():
            stage_line(2, i - 1, 1)
            stage_line(3, i - 1, 2)
        stage_side(2, i)
        stage_line(3, i, 1)

        @pl.when(i > 0)
        def _():
            stage_line(2, i - 1, 2)

    def cross_tick(i):
        stage_side(1, i)

        @pl.when(i == 0)
        def _():
            stage_line(2, mp - 1, 1)
            stage_line(3, mp - 1, 2)

        @pl.when(i > 0)
        def _():
            stage_line(1, i - 1, 1)

        @pl.when(i == 1)
        def _():
            stage_line(2, mp - 1, 2)

        @pl.when(i > 1)
        def _():
            stage_line(1, i - 2, 2)

    def self_tick(i):
        stage_side(0, i)
        if i == 0:
            @pl.when(encoding)
            def _():
                stage_line(2, mp - 1, 1)
                stage_line(3, mp - 1, 2)
            stage_line(1, mp - 1, 1)
            stage_line(1, mp - 2, 2)
        else:
            stage_line(0, i - 1, 1)
        if i == 1:
            @pl.when(encoding)
            def _():
                stage_line(2, mp - 1, 2)
            stage_line(1, mp - 1, 2)
        if i > 1:
            stage_line(0, i - 2, 2)

    def prepare(rws):
        x = x_ref[rws].astype(f32)
        h[rws] = norm(x, vec_ref[0:1], vec_ref[1:2]).astype(bf16)
        x1[rws] = x + vec_ref[2:3]
    row_loop(total, 256, prepare)

    query_at = lax.broadcasted_iota(jnp.int32, (1, length), 1)

    def limits(u):
        last = lens_ref[section, me * utts + u] - 1
        return jnp.where(decoding, jnp.minimum(query_at, last), last)

    def frames(u):
        return jnp.full((1, length), lens_ref[0, me * utts + u] - 1, jnp.int32)

    lane = lax.broadcasted_iota(jnp.int32, (1, PROJ), 1)
    scale = jnp.where((lane >= KV) & (lane < KV + part), 0.125, 1.0)

    def self_shards(g, carry):
        shards = (2 * g, 2 * g + 1)
        for m in shards:
            def keep(cols, value):
                qkv[m, :, cols] = ((value + smalls[m, 0:1, cols]) * scale[:, cols]).astype(bf16)
            wide_dot(nt, h[...], lambda s, n: wa[m, s:s + n], PROJ, keep)
        attend([(m, u) for m in shards for u in range(utts)], length, qkv, ctx, p, limits, smalls)
        x1[...] += nn(ctx[shards[0]], wa[shards[0], CTX:]) + nn(ctx[shards[1]], wa[shards[1], CTX:])
        return carry

    def ffn_one(m):
        ffn_shard(m, h, w1, w2, a, gp, smalls[m, 2:3], out)

    def ffn_at(dist):
        @pl.when(encoding)
        def _():
            def step(way, carry):
                @pl.when(jnp.where(way == 0, me >= dist, me + dist <= mp - 1))
                def _():
                    ffn_one(jnp.where(way == 0, me - dist, me + dist))
                return carry
            lax.fori_loop(0, 2, step, 0)

    run("L0", "L1", "S0", "L2", "P0", "L3", "S1", "S2", "L4", "P1", "P2", "S4", "L5", "L6", "P4")
    for hop in range(1, mp):
        small_copy(hop, lax.rem(me + mp - hop, mp)).wait_recv()
    lax.fori_loop(0, mp // 4, self_shards, 0)
    run("L7", "L8", "S3")
    lax.fori_loop(mp // 4, mp // 2, self_shards, 0)
    for copy in own_w:
        copy.wait()
    spill = [pltpu.make_async_copy(src, dst, i_sem.at[j]) for j, (src, dst) in enumerate(
        ((qkv, qkv_hbm), (ctx, ctx_hbm), (p, p_hbm)))]
    fetch = [pltpu.make_async_copy(dst, src, i_sem.at[j]) for j, (src, dst) in enumerate(
        ((qkv, qkv_hbm), (ctx, ctx_hbm), (p, p_hbm)))]
    give = pltpu.make_async_copy(out, out_hbm, i_sem.at[3])

    @pl.when(decoding)
    def _():
        for copy in spill:
            copy.start()

        def start_cross(rws):
            y = x1[rws]
            hc[rws] = norm(y, vec_ref[3:4], vec_ref[4:5]).astype(bf16)
            y2[rws] = y
        row_loop(total, 256, start_cross)

    @pl.when(encoding)
    def _():
        ffn_start(total, x1, out, h, vec_ref)
        ffn_one(me)

    run("L9", "L10", "S5", "P3")
    ffn_at(1)

    run("S6", "L11", "S7", "S8", "P5", "P6", "P8")
    ffn_at(2)
    run("S9", "S10", "S11", "P7", "P9", "P10", "P11")
    ffn_at(3)

    @pl.when(decoding)
    def _():
        for copy in spill:
            copy.wait()

        def queries(m, carry):
            pq = nt(hc[...], wc[m, KV:PROJ])
            qkv[m, :, KV:] = ((pq + smalls[m, 1:2, KV:PROJ]) * scale[:, KV:]).astype(bf16)
            return carry
        lax.fori_loop(0, mp, queries, 0)

    @pl.when(encoding)
    def _():
        for u in range(utts):
            mem[utt(u)] = norm(out[utt(u)], vec_ref[3:4], vec_ref[4:5]).astype(bf16)
            over_mem(u).start()
        give.start()
        drain()
        cotangent.wait()
        g[...] = dy[...].astype(f32)
        turn(ht, h[...])
        give.wait()
        for u in range(utts):
            over_dmem(u).wait_recv()
        norm_back(total, out, vec_ref[3:4], dmem, g, vg, 3)

        dy[...] = g[...].astype(bf16)
        turn(dyt, dy[...])
        vg[7:8, :] = jnp.sum(g[...], axis=0, keepdims=True)
        dh[...] = jnp.zeros_like(dh)

        def ffn_step(i, carry):
            m = shard_of(i)
            hidden_grad(m, gp, w2, dy, sg)
            w2[m] = nn(dyt[...], a[m]).astype(bf16)
            send_core(3, i)

            @pl.when(i > 0)
            def _():
                stage_core(2, i - 1)
            dh[...] += nt(gp[m], w1[m])
            w1[m] = nn(ht[...], gp[m]).astype(bf16)
            send_core(2, i)
            stage_core(3, i)

            @pl.when(i >= mp // 2)
            def _():
                ffn_ticks(i - mp // 2)
            return carry
        lax.fori_loop(0, mp, ffn_step, 0)
        norm_back(total, x1, vec_ref[5:6], dh, g, vg, 5)
        stage_core(2, mp - 1)
        over_cb.wait_recv()
        sg[pl.ds(0, mp), 1:2, :PROJ] = cb[:, 0:1, :]

    @pl.when(decoding)
    def _():
        def cross_utt(u, carry):
            over_mem(u).wait_recv()
            rws = utt(u)
            for m in range(mp):
                qkv[m, rws, :KV] = (nt(mem[rws], wc[m, :KV]) + smalls[m, 1:2, :KV]).astype(bf16)
            attend([(m, u) for m in range(mp)], length, qkv, ctx, p, frames, None)
            y2[rws] += sum(nn(ctx[m, rws], wc[m, CTX:]) for m in range(mp))
            return carry
        lax.fori_loop(0, utts, cross_utt, 0)

        ffn_start(total, y2, out, h, vec_ref)

        def one(m, carry):
            ffn_one(m)
            return carry
        lax.fori_loop(0, mp, one, 0)
        give.start()
        cotangent.wait()
        g[...] = dy[...].astype(f32)
        vg[7:8, :] = jnp.sum(g[...], axis=0, keepdims=True)
        dy[...] = g[...].astype(bf16)
        turn(dyt, dy[...])
        turn(ht, h[...])
        drain()
        give.wait()
        dh[...] = jnp.zeros_like(dh)

        def dgrad(m, carry):
            hidden_grad(m, gp, w2, dy, sg)
            dh[...] += nt(gp[m], w1[m])
            return carry
        lax.fori_loop(0, mp, dgrad, 0)
        norm_back(total, y2, vec_ref[5:6], dh, g, vg, 5)

        early = 1

        def ffn_weights(i, carry):
            m = shard_of(i)
            w2[m] = nn(dyt[...], a[m]).astype(bf16)
            send_core(3, i)

            @pl.when((i > 0) & (i != early))
            def _():
                stage_core(2, i - 1)
            w1[m] = nn(ht[...], gp[m]).astype(bf16)
            send_core(2, i)
            stage_core(3, i)

            @pl.when(i >= mp // 2)
            def _():
                ffn_ticks(i - mp // 2)
            return carry
        lax.fori_loop(0, early, ffn_weights, 0)

        dy[...] = g[...].astype(bf16)

        def cross_back(u, carry):
            rws = utt(u)
            for pair in range(0, mp, 2):
                shards = (pair, pair + 1)
                for m in shards:
                    dctx[m - pair] = nt(dy[rws], wc[m, CTX:]).astype(bf16)
                attend_back([(m, u) for m in shards], length, qkv, p,
                            lambda m, rows, t: tile(dctx, m - pair, slice(None), t), qkv, None, None)
            dmem[rws] = sum(nn(qkv[m, rws, :KV], wc[m, :KV]) for m in range(mp)).astype(bf16)
            over_dmem(u).start()
            dh[rws] = sum(nn(qkv[m, rws, KV:], wc[m, KV:PROJ]) for m in range(mp))

            @pl.when(u == 0)
            def _():
                stage_core(2, early - 1)
            return carry
        lax.fori_loop(0, utts, cross_back, 0)
        lax.fori_loop(early, mp, ffn_weights, 0)

        def row_sums(m, carry):
            sums = jnp.sum(qkv[m].astype(f32), axis=0, keepdims=True)
            sg[m, 1:2, :PROJ] = sums
            cb[m, 0:1, :] = sums
            return carry
        lax.fori_loop(0, mp, row_sums, 0)
        over_cb.start()
        norm_back(total, x1, vec_ref[3:4], dh, g, vg, 3)
        turn(dyt, dy[...])
        turn(ht, hc[...])

        def cross_weights(i, carry):
            m = shard_of(i)
            wc[m, :, :KV] = tn(mem[...], qkv[m, :, :KV]).astype(bf16)
            gq = nn(ht[...], qkv[m, :, KV:])
            go = nn(dyt[...], ctx[m])
            wc[m, :, KV:CTX] = gq[:, :T].astype(bf16)
            wc[m, :, CTX:PROJ] = (gq[:, T:] + go[:, :T]).astype(bf16)
            wc[m, :, PROJ:] = go[:, T:].astype(bf16)

            @pl.when(i == 0)
            def _():
                stage_core(2, mp - 1)
            send_core(1, i)

            @pl.when(i > 0)
            def _():
                stage_core(1, i - 1)

            @pl.when(i < mp // 2)
            def _():
                ffn_ticks(i + mp // 2)
            return carry
        lax.fori_loop(0, mp, cross_weights, 0)
        for copy in fetch:
            copy.start()
        stage_core(1, mp - 1)
        for copy in fetch:
            copy.wait()

    def prepare_self(rws):
        h[rws] = norm(x_ref[rws].astype(f32), vec_ref[0:1], vec_ref[1:2]).astype(bf16)
    row_loop(total, 256, prepare_self)
    vg[2:3, :] = jnp.sum(g[...], axis=0, keepdims=True)
    dy[...] = g[...].astype(bf16)
    turn(dyt, dy[...])
    turn(ht, h[...])
    dh[...] = jnp.zeros_like(dh)
    down = lax.broadcasted_iota(jnp.int32, (length, length), 0)
    right = lax.broadcasted_iota(jnp.int32, (length, length), 1)
    flip = (down + right == length - 1).astype(f32).astype(bf16)

    def dctx_at(rows, t):
        return tile(dctx, rows.start // length, slice(None), t)

    def self_step(i, carry):
        m = shard_of(i)
        for u in range(utts):
            dctx[u] = nt(dy[utt(u)], wa[m, CTX:]).astype(bf16)
        attend_back([(m, u) for u in range(utts)], length, qkv, p, lambda m, rows, t: dctx_at(rows, t), qkv, sg, flip)
        d = qkv[m]
        sg[m, 0:1, :PROJ] = jnp.sum(d.astype(f32), axis=0, keepdims=True)
        dh[...] += nn(d, wa[m, :PROJ])
        gd = nn(ht[...], d)
        go = nn(dyt[...], ctx[m])
        wa[m, :, :CTX] = gd[:, :CTX].astype(bf16)
        wa[m, :, CTX:PROJ] = (gd[:, CTX:] + go[:, :T]).astype(bf16)
        wa[m, :, PROJ:] = go[:, T:].astype(bf16)
        send_core(0, i)

        @pl.when(i > 0)
        def _():
            stage_core(0, i - 1)

        @pl.when(encoding & (i < mp // 2))
        def _():
            ffn_ticks(i + mp // 2)

        @pl.when(decoding)
        def _():
            cross_tick(i)
        return carry
    lax.fori_loop(0, mp, self_step, 0)
    norm_back(total, x_ref, vec_ref[0:1], dh, g, vg, 0)

    def small_sum(hop, src, to):
        return pltpu.make_async_remote_copy(
            src_ref=src, dst_ref=got_small.at[hop], send_sem=a_send.at[hop], recv_sem=a_recv.at[hop],
            device_id={"dp": to}, device_id_type=MESH)

    with_core, with_side = small_sum(0, sg, core), small_sum(1, pair_sg, side)
    with_core.start()
    with_core.wait_recv()
    pair_sg[...] = sg[...] + got_small[0]
    with_side.start()
    stage_core(0, mp - 1)
    self_tick(0)
    self_tick(1)
    with_side.wait_recv()
    with_core.wait_send()
    sg[...] = pair_sg[...] + got_small[1]

    def line_small(hop, which):
        peer = lax.rem(me + hop, mp)
        src = sg.at[peer] if which == 0 else sg.at[mp]
        return pltpu.make_async_remote_copy(
            src_ref=src, dst_ref=got_line.at[hop - 1, which],
            send_sem=b_send.at[hop - 1, which], recv_sem=b_recv.at[hop - 1, which],
            device_id={"mp": peer}, device_id_type=MESH)

    for hop in range(1, mp):
        for which in (0, 1):
            line_small(hop, which).start()
    for i in range(2, mp):
        self_tick(i)
    stage_line(0, mp - 1, 1)
    stage_line(0, mp - 2, 2)
    stage_line(0, mp - 1, 2)
    small_out[0] = sg[me]
    small_out[1] = sg[mp]
    for hop in range(1, mp):
        for which in (0, 1):
            line_small(hop, which).wait_recv()
            small_out[which] += got_line[hop - 1, which]

    stage = (x1.at[pl.ds(0, part)], x1.at[pl.ds(part, part)], y2.at[pl.ds(0, part)], y2.at[pl.ds(part, part)])

    def finish(b):
        stage[b][...] = bufs[b][me, rows(quarter)].astype(f32)

        @pl.when(me > 0)
        def _():
            for hh in range(HALVES):
                to_line(0, b, me, hh).wait_recv()
            stage[b][...] += from_line[me, b].astype(f32)

        @pl.when(me < mp - 1)
        def _():
            for hh in range(HALVES):
                to_line(1, b, me, hh).wait_recv()
            stage[b][...] += from_line[mp, b].astype(f32)

    def hand(b):
        return pltpu.make_async_copy(stage[b], own_hbm.at[b], l_sem.at[b, 0])

    @pl.when(decoding)
    def _():
        finish(1)
        kv_grad[0] = stage[1][:, :2 * part].astype(bf16)
        over_kv.start()
        hand(1).start()
    for b in (3, 2, 0):
        finish(b)
        hand(b).start()

    @pl.when(encoding)
    def _():
        over_kv.wait_recv()
        stage[1][:, :2 * part] = kv_grad[1].astype(f32)
        hand(1).start()

    @pl.when(encoding)
    def _():
        for i in (0, 1):
            over_rows(i).wait_send()
        over_small.wait_send()
        for u in range(utts):
            over_mem(u).wait_send()

    @pl.when(decoding)
    def _():
        for u in range(utts):
            over_dmem(u).wait_send()
        over_cb.wait_send()
        over_kv.wait_send()
    with_side.wait_send()
    for hop in range(1, mp):
        for which in (0, 1):
            line_small(hop, which).wait_send()

    def left(i, carry):
        m = shard_of(i)
        for b in range(BLOCKS):
            @pl.when(needed(b))
            def _():
                for k in (0, 1):
                    to_core(b, i, m, k).wait_send()
                for hh in range(HALVES):
                    to_side(b, m, hh).wait_send()
                    for way in (0, 1):
                        @pl.when((me < m) if way == 0 else (me > m))
                        def _():
                            to_line(way, b, m, hh).wait_send()
        return carry
    lax.fori_loop(0, mp, left, 0)
    for b in range(BLOCKS):
        hand(b).wait()


def layers(mp, dp, utts, length, lens, x, cot, vec, small, w_in, w_o, w_cross, w_one, w_two):
    total, width = x.shape
    hidden = w_one.shape[1]
    sds = jax.ShapeDtypeStruct
    v = pltpu.VMEM
    sem = pltpu.SemaphoreType.DMA
    shard = v((mp, width, hidden), bf16)
    part = width // 4
    wide_b, wide_f = v((total, width), bf16), v((total, width), f32)
    turned = v((width, total), bf16)
    heads = (utts, mp, HEADS, length, length)
    proj, context = (mp, total, PROJ), (mp, total, 2 * LANES)
    rows = small.shape
    gather = (2, mp - 1, BLOCKS, HALVES)
    return pl.pallas_call(
        functools.partial(layers_kernel, mp, dp, utts, length),
        out_shape=(sds((total, width), f32), sds((2,) + rows, f32), sds((total, width), f32),
                   sds((BLOCKS, part, hidden), f32), sds(proj, bf16), sds(context, bf16), sds(heads, bf16)),
        in_specs=[SMEM, VM, ANY, VM, VM] + [ANY] * 5,
        out_specs=(VM,) * 2 + (ANY,) * 5,
        scratch_shapes=[shard] * 4 + [
            v((mp,) + rows, f32), v(rows, f32), v(proj, bf16), v(context, bf16), v(heads, bf16),
            v((mp, total, hidden), bf16), v((mp, total, hidden), bf16),
            wide_f, wide_f, wide_f, wide_b, wide_b, wide_b, wide_b,
            wide_b, turned, turned, v((max(utts, 2), length, 2 * LANES), bf16), v((mp + 1,) + rows, f32),
            v((mp, 8, PROJ), f32),
            v((RING, 2, part, hidden), bf16), v((BLOCKS, mp, part, hidden), bf16), v((mp + 1, BLOCKS, part, hidden), bf16),
            v((mp + 1,) + rows, f32), v((2, mp + 1) + rows, f32), v((mp - 1, 2) + rows, f32),
            v((2, part, 2 * part), bf16),
            sem((BLOCKS, 4)), sem(gather), sem(gather), sem((3,) + gather), sem((3,) + gather),
            sem((mp - 1,)), sem((mp - 1,)), sem((5 + 2 * utts,)), sem((5 + 2 * utts,)), sem((4,)),
            sem((BLOCKS, mp, 2)), sem((BLOCKS, mp, 2)), sem((BLOCKS, mp, HALVES)), sem((BLOCKS, mp, HALVES)),
            sem((2, BLOCKS, mp, HALVES)), sem((2, BLOCKS, mp, HALVES)), pltpu.SemaphoreType.REGULAR,
            sem((2,)), sem((2,)), sem((mp - 1, 2)), sem((mp - 1, 2))],
        compiler_params=pltpu.CompilerParams(collective_id=0, has_side_effects=True, vmem_limit_bytes=63 * 2**20),
        name="both_layers",
    )(lens, x, cot, vec, small, w_in, w_o, w_cross, w_one, w_two)


def finish_kernel(mp, dp, length, rel, own_in, small, out_in, dx_in,
                  out, dx, vectors, in_grad, bias, o_grad, rel_grad, cross, one, b1, two,
                  own, out_held, dx_held, in_sem, out_sem):
    me = lax.axis_index("mp")
    dp_index = lax.axis_index("dp")
    decoding = lax.axis_index("section") == 1
    loads = [pltpu.make_async_copy(src, dst, in_sem.at[j]) for j, (src, dst) in enumerate(
        ((own_in.at[0], own.at[0]), (own_in.at[1], own.at[1]), (out_in, out_held), (dx_in, dx_held),
         (own_in.at[2], own.at[2]), (own_in.at[3], own.at[3])))]
    stores = [pltpu.make_async_copy(src, dst, out_sem.at[j]) for j, (src, dst) in enumerate(
        ((out_held, out), (dx_held, dx), (own.at[2], one), (own.at[3], two)))]
    for copy in loads:
        copy.start()
    for copy in loads[:2]:
        copy.wait()
    part = own.shape[1]
    k, v, q, o = (slice(t * part, (t + 1) * part) for t in range(4))
    mine = own[0]
    in_grad[0], in_grad[1], in_grad[2] = mine[:, q], mine[:, k], mine[:, v]
    o_grad[...] = mine[:, o].T
    mine = own[1]
    cross[0] = jnp.where(decoding, mine[:, q], mine[:, k])
    cross[1] = jnp.where(decoding, mine[:, o], mine[:, v])
    for load, store in zip(loads[2:], stores):
        load.wait()
        store.start()

    width = small.shape[2]

    def back(value, by):
        return pltpu.roll(value, lax.rem(width - by, width), 1)

    vectors[...] = back(small[1], (dp_index * mp + me) * vectors.shape[1])[:, :vectors.shape[1]]
    size = bias.shape[2]
    turned = back(small[0], dp_index * size)
    cross_row = jnp.where(decoding, turned[1:2, q], turned[1:2, v])
    for t, row in enumerate((turned[0:1, q], turned[0:1, v], cross_row)):
        for r in range(HEADS):
            bias[t, r:r + 1, :] = row[:, 64 * r:64 * r + size]
    size = b1.shape[1]
    turned = back(small[0], dp_index * size)
    for r in range(b1.shape[0]):
        b1[r:r + 1, :] = turned[2:3, 128 * r:128 * r + size]
    lines = small[0]
    low, high = length - rel // 2, length + rel // 2 - 2
    lane = lax.broadcasted_iota(jnp.int32, lines.shape, 1)
    first = jnp.sum(jnp.where(lane < low, lines, 0.0), axis=1, keepdims=True)
    last = jnp.sum(jnp.where((lane >= high) & (lane < 2 * length), lines, 0.0), axis=1, keepdims=True)
    moved = pltpu.roll(lines, width - (low - 1), 1)
    moved = jnp.where(lane == 0, first, jnp.where(lane == rel - 1, last, moved))
    rel_grad[...] = back(moved, dp_index * rel_grad.shape[1])[3:3 + HEADS, :rel_grad.shape[1]]
    for store in stores:
        store.wait()


def finish(mp, dp, length, rel, own, small, out, dx):
    sds = jax.ShapeDtypeStruct
    part, hidden = own.shape[1:]
    width = small.shape[2]
    shard = width // mp
    return pl.pallas_call(
        functools.partial(finish_kernel, mp, dp, length, rel),
        out_shape=(sds(out.shape, f32), sds(dx.shape, f32), sds((8, width // (dp * mp)), f32),
                   sds((3, part, shard), f32), sds((3, HEADS, 64 // dp), f32), sds((shard, part), f32),
                   sds((HEADS, rel // dp), f32), sds((2, part, shard), f32), sds((part, hidden), f32),
                   sds((hidden // 128, 128 // dp), f32), sds((part, hidden), f32)),
        in_specs=[ANY, VM, ANY, ANY], out_specs=(ANY,) * 2 + (VM,) * 6 + (ANY, VM, ANY),
        scratch_shapes=[pltpu.VMEM(own.shape, f32), pltpu.VMEM(out.shape, f32), pltpu.VMEM(dx.shape, f32),
                        pltpu.SemaphoreType.DMA((6,)), pltpu.SemaphoreType.DMA((4,))],
        compiler_params=pltpu.CompilerParams(vmem_limit_bytes=60 * 2**20), name="finish",
    )(own, small, out, dx)


def rel_line(table, length):
    half = table.shape[1] // 2
    heads = table.shape[0]
    first = jnp.broadcast_to(table[:, :1], (heads, length - half))
    last = jnp.broadcast_to(table[:, -1:], (heads, length - half))
    return jnp.concatenate([table[:, half:], last, first, table[:, :half]], axis=1)


def per_device(streams, lengths, vectors, attn_in, attn_bias, attn_out, rel_table, cross, ffn_in, ffn_bias, ffn_out,
               cotangent):
    mp = lax.axis_size("mp")
    dp = lax.axis_size("dp")
    utts, length, width = streams.shape[1:]
    total = utts * length
    x = streams[0].reshape(total, width)
    cot = cotangent[0].reshape(total, width)
    vec = vectors[0]

    ext = rel_line(rel_table[0], length)
    biases = attn_bias[0].reshape(3, -1)
    none = jnp.zeros_like(biases[0])
    small = jnp.concatenate([jnp.concatenate([none, biases[1], biases[0], none])[None],
                             jnp.concatenate([none, biases[2], biases[2], none])[None],
                             ffn_bias[0].reshape(1, -1), jnp.pad(ext, ((0, 2), (0, width - ext.shape[1])))], axis=0)

    g, small_sum, out, own, _, _, _ = layers(
        mp, dp, utts, length, lengths, x, cot, vec, small, jnp.swapaxes(attn_in[0], 1, 2), attn_out[0],
        jnp.swapaxes(cross[0], 1, 2), ffn_in[0], ffn_out[0])
    if dp > 4:
        near = [[q * (dp // 4) + i for i in range(dp // 4)] for q in range(4)]
        small_sum = lax.psum(small_sum, "dp", axis_index_groups=near)
    out, dx, vectors_grad, in_grad, bias_grad, o_grad, rel_grad, cross_grad, one_grad, b1_grad, two_grad = finish(
        mp, dp, length, rel_table.shape[2], own, small_sum, out, g)
    two_grad = two_grad.T
    if dp > 4:
        per = dp // 4
        groups = [[q * per + i for i in range(per)] for q in range(4)]

        def rest(value, axis):
            return lax.psum_scatter(value.astype(bf16), "dp", scatter_dimension=axis, axis_index_groups=groups,
                                    tiled=True).astype(f32)

        in_grad, o_grad, cross_grad = rest(in_grad, 1), rest(o_grad, 1), rest(cross_grad, 1)
        one_grad, two_grad = rest(one_grad, 0), rest(two_grad, 1)
    shape = (1, utts, length, width)
    return (out.reshape(shape), dx.reshape(shape), vectors_grad[None], in_grad[None], bias_grad[None], o_grad[None],
            rel_grad[None], cross_grad[None], one_grad[None], b1_grad[None], two_grad[None])


def solution(mesh):
    placed = (
        P("section", ("dp", "mp"), None, None),
        P(None, "dp"),
        P("section", None, None),
        P("section", None, None, "mp"),
        P("section", None, "mp", None),
        P("section", "mp", None),
        P("section", "mp", None),
        P("section", None, None, "mp"),
        P("section", None, "mp"),
        P("section", "mp", None),
        P("section", "mp", None),
        P("section", ("dp", "mp"), None, None),
    )
    return jax.shard_map(
        per_device,
        mesh=mesh,
        in_specs=placed,
        out_specs=(
            P("section", ("dp", "mp"), None, None),
            P("section", ("dp", "mp"), None, None),
            P("section", None, ("dp", "mp")),
            P("section", None, "dp", "mp"),
            P("section", None, "mp", "dp"),
            P("section", "mp", "dp"),
            P("section", "mp", "dp"),
            P("section", None, "dp", "mp"),
            P("section", "dp", "mp"),
            P("section", "mp", "dp"),
            P("section", "mp", "dp"),
        ),
        check_vma=False,
    )
```

```python
import functools
import jax
import jax.numpy as jnp
from jax import lax
from jax.experimental import pallas as pl
from jax.experimental.pallas import tpu as pltpu
from jax.sharding import PartitionSpec as P

MESH = pl.DeviceIdType.MESH
ANY = pl.BlockSpec(memory_space=pl.ANY)
VM = pl.BlockSpec(memory_space=pltpu.VMEM)
BLOCKS = 4


def partners(dp_index, step):
    bit = lax.rem(dp_index // step, 2)
    return dp_index + step - 2 * step * bit


EPSILON = 1e-05
MASKED = -1e30
HEADS = 3
LANES = 128
PROJ = 640
CTX = 512
bf16, f32 = jnp.bfloat16, jnp.float32


def nn(a, b):
    return lax.dot_general(a, b, (((1,), (0,)), ((), ())), preferred_element_type=f32)


def nt(a, b):
    return lax.dot_general(a, b, (((1,), (1,)), ((), ())), preferred_element_type=f32)


def tn(a, b):
    return lax.dot_general(a, b, (((0,), (0,)), ((), ())), preferred_element_type=f32)


def norm_parts(x):
    centred = x - jnp.mean(x, axis=-1, keepdims=True)
    r = lax.rsqrt(jnp.mean(centred * centred, axis=-1, keepdims=True) + EPSILON)
    return centred * r, r


def norm(x, gain, shift):
    xh, _ = norm_parts(x)
    return xh * gain + shift


def row_loop(total, size, body):
    def step(i, carry):
        body(pl.ds(pl.multiple_of(i * size, size), size))
        return carry
    lax.fori_loop(0, total // size, step, 0)


def even_lanes(rows):
    return lax.broadcasted_iota(jnp.int32, (rows, LANES), 1) < LANES // 2


def half_mask(half):
    lane = lax.broadcasted_iota(jnp.int32, (1, LANES), 1)
    on = (lane < LANES // 2) if half == 0 else (lane >= LANES // 2)
    return on.astype(f32).astype(bf16)


def tile(ref, m, rows, t):
    return ref[m, rows, t * LANES:(t + 1) * LANES]


HEAD_TILES = (((3, 0), (0, 0), (1, 1), (0, 1)),
              ((3, 1), (0, 1), (2, 0), (1, 0)),
              ((4, 0), (1, 0), (2, 1), (1, 1)))


def utt_rows(u, length):
    return pl.ds(u * length, length) if isinstance(u, int) else pl.ds(pl.multiple_of(u * length, length), length)


def attend(pairs, length, qkv_ref, ctx_ref, p_ref, limits, ext_ref):
    key_at = lax.broadcasted_iota(jnp.int32, (length, length), 0)
    even = even_lanes(length)
    parts, probs, biases = {}, {}, {}
    for r in range(HEADS):
        (qt, half), (kt, _), (vt, _), _ = HEAD_TILES[r]
        for n, (m, u) in enumerate(pairs):
            rows = utt_rows(u, length)
            s = nt(tile(qkv_ref, m, rows, kt) * half_mask(half), tile(qkv_ref, m, rows, qt))
            if ext_ref is not None:
                if (id(m), r) not in biases:
                    row = ext_ref[m, 3 + r:4 + r, :2 * length]
                    biases[id(m), r] = pltpu.roll(jnp.broadcast_to(row, (length, 2 * length)), 0, 1, stride=1,
                                                  stride_axis=0)[:, :length].T
                s = s + biases[id(m), r]
            s = jnp.where(key_at <= limits(u), s, MASKED)
            e = jnp.exp(s - jnp.max(s, axis=0, keepdims=True))
            p = (e * (1.0 / jnp.sum(e, axis=0, keepdims=True))).astype(bf16)
            probs[n, r] = p
            parts[n, r] = tn(p, tile(qkv_ref, m, rows, vt))
    for n, (m, u) in enumerate(pairs):
        rows = utt_rows(u, length)
        for r in range(HEADS):
            p_ref[u, m, r] = probs[n, r]
        ctx_ref[m, rows, :LANES] = jnp.where(even, 0.0, parts[n, 0]).astype(bf16)
        ctx_ref[m, rows, LANES:] = jnp.where(even, parts[n, 1], parts[n, 2]).astype(bf16)


def attend_back(pairs, length, qkv_ref, p_ref, dctx_of, out_ref, rel_ref, flip):
    even = even_lanes(length)
    got, total = {}, {}
    for r in range(HEADS):
        (qt, _), (kt, _), (vt, vhalf), (ot, _) = HEAD_TILES[r]
        for n, (m, u) in enumerate(pairs):
            rows = utt_rows(u, length)
            p = p_ref[u, m, r]
            dctx = dctx_of(m, rows, ot)
            dp = nt(tile(qkv_ref, m, rows, vt) * half_mask(vhalf), dctx)
            pf = p.astype(f32)
            t = pf * dp
            ds = (t - pf * jnp.sum(t, axis=0, keepdims=True)).astype(bf16)
            got[n, r] = (tn(ds, tile(qkv_ref, m, rows, kt)) * 0.125, nn(ds, tile(qkv_ref, m, rows, qt)), nn(p, dctx))
            if rel_ref is not None:
                turned = nn(ds, flip)
                total[r] = total[r] + turned if r in total else turned
    for r in total:
        m = pairs[0][0]
        wide = jnp.concatenate([total[r], jnp.zeros_like(total[r])], axis=1)
        wide = pltpu.roll(wide, 0, 1, stride=1, stride_axis=0)
        rel_ref[m, 3 + r:4 + r, :2 * length] = jnp.sum(wide, axis=0, keepdims=True)
    for n, (m, u) in enumerate(pairs):
        rows = utt_rows(u, length)
        (q0, k0, v0), (q1, k1, v1), (q2, k2, v2) = got[n, 0], got[n, 1], got[n, 2]
        for t, (left, right) in enumerate(((k0, k1), (k2, v0), (v1, v2), (q0, q1), (q2, 0.0))):
            out_ref[m, rows, t * LANES:(t + 1) * LANES] = jnp.where(even, left, right).astype(bf16)


def gelu_both(u):
    cdf = 0.5 + 0.5 * lax.erf(u * 0.7071067811865476)
    return u * cdf, cdf + u * (jnp.exp(-0.5 * u * u) * 0.3989422804014327)


def norm_back(total, x_ref, gain, dh_ref, add_into, vg_ref, gain_row, grad_out=None):
    width = gain.shape[-1]

    def step(i, carry):
        dgain, dshift = carry
        rows = pl.ds(pl.multiple_of(i * 256, 256), 256)
        dh = dh_ref[rows].astype(f32)
        xh, r = norm_parts(x_ref[rows].astype(f32))
        e = dh * gain
        dx = r * (e - jnp.mean(e, axis=-1, keepdims=True) - xh * jnp.mean(e * xh, axis=-1, keepdims=True))
        add_into[rows] = add_into[rows].astype(f32) + dx
        return dgain + jnp.sum(dh * xh, axis=0, keepdims=True), dshift + jnp.sum(dh, axis=0, keepdims=True)

    zero = jnp.zeros((1, width), f32)
    dgain, dshift = lax.fori_loop(0, total // 256, step, (zero, zero))
    vg_ref[gain_row:gain_row + 1, :] = dgain
    vg_ref[gain_row + 1:gain_row + 2, :] = dshift


def turn(dst_ref, src):
    dst_ref[...] = src.T


SMEM = pl.BlockSpec(memory_space=pltpu.SMEM)


SEQUENCE = ((0, 1), (2, 1), (0, 2), (3, 1), (0, 3), (1, 1), (2, 2), (1, 2), (3, 2), (1, 3), (2, 3), (3, 3))
HALVES = 2
RING = 4


def wide_dot(dot, a, b_cols, width, use, step=256):
    for start in range(0, width, step):
        size = min(step, width - start)
        use(slice(start, start + size), dot(a, b_cols(start, size)))


def ffn_shard(m, rows, h, w1, w2, a, gp, bias, out):
    def keep(cols, u):
        act, slope = gelu_both(u + bias[:, cols])
        a[m, rows, cols] = act.astype(bf16)
        gp[m, rows, cols] = slope.astype(bf16)
    wide_dot(nn, h[rows], lambda s, n: w1[m, :, s:s + n], w1.shape[2], keep)
    out[rows] += nn(a[m, rows], w2[m])


def ffn_start(rows, x_ref, out_ref, h_ref, vec_ref):
    x = x_ref[rows]
    h_ref[rows] = norm(x, vec_ref[5:6], vec_ref[6:7]).astype(bf16)
    out_ref[rows] = x + vec_ref[7:8]


def hidden_grad(m, gp, w2, dy, sg):
    def keep(cols, da):
        du = (da * gp[m, :, cols].astype(f32)).astype(bf16)
        gp[m, :, cols] = du
        sg[m, 2:3, cols] = jnp.sum(du.astype(f32), axis=0, keepdims=True)
    wide_dot(nt, dy[...], lambda s, n: w2[m, s:s + n], w2.shape[1], keep)


def layers_kernel(mp, dp, utts, length,
                  lens_ref, x_ref, cot_ref, vec_ref, bias_ref, b1_ref, rel_ref, in_ref, o_ref, cross_ref, w1_ref, w2_ref,
                  small_out, dx_hbm, out_hbm, own_hbm, qkv_hbm, ctx_hbm, p_hbm,
                  g, wa, wc, w1, w2, smalls, small_ref, peer_small, qkv, ctx, p, a, gp, x1, y2, out, h, hc, mem, dmem,
                  dy, dyt, ht, dctx, sg, cb, from_core, from_side, from_line, pair_sg, got_small, got_line,
                  kv_grad,
                  l_sem, z_send, z_recv, p_send, p_recv, s_send, s_recv, x_send, x_recv, i_sem,
                  c_send, c_recv, y_send, y_recv, r_send, r_recv, credit, a_send, a_recv, b_send, b_recv):
    me = lax.axis_index("mp")
    dp_index = lax.axis_index("dp")
    section = lax.axis_index("section")
    decoding = section == 1
    encoding = section == 0
    near = dp // 4
    core = partners(dp_index, near)
    side = partners(dp_index, 2 * near)
    quarter = dp_index // near
    parity = lax.rem(quarter, 2)
    half = quarter // 2
    core_quarter = quarter + 1 - 2 * parity
    side_quarter = quarter + 2 - 4 * half
    diag_quarter = core_quarter + 2 - 4 * half
    part = wa.shape[1] // 4
    total = utts * length
    T = LANES
    KV, PROJ_END = 3 * T, PROJ
    bufs = (wa, wc, w1, w2)
    dh = out
    vg = sg.at[mp]

    barrier = pltpu.get_barrier_semaphore()
    for hop in range(1, mp):
        pl.semaphore_signal(barrier, inc=1, device_id={"mp": lax.rem(me + hop, mp)}, device_id_type=MESH)
    for other in (core, side):
        pl.semaphore_signal(barrier, inc=1, device_id={"dp": other}, device_id_type=MESH)
    pl.semaphore_signal(barrier, inc=1, device_id={"section": 1 - section}, device_id_type=MESH)

    def needed(b):
        return decoding if b == 1 else me >= 0

    def utt(u):
        return utt_rows(u, length)

    def own_rows(b, t, src):
        return pltpu.make_async_copy(src, bufs[b].at[me, t * part:(t + 1) * part], l_sem.at[b, t])

    own_a = [own_rows(0, 0, in_ref.at[1]), own_rows(0, 1, in_ref.at[2]), own_rows(0, 2, in_ref.at[0]),
             own_rows(0, 3, o_ref)]
    own_c = [own_rows(1, 2, cross_ref.at[0]), own_rows(1, 3, cross_ref.at[1])]
    own_w = [pltpu.make_async_copy(src, bufs[b].at[me], l_sem.at[b, 0]) for b, src in ((2, w1_ref), (3, w2_ref))]
    for copy in own_a:
        copy.start()

    @pl.when(decoding)
    def _():
        for copy in own_c:
            copy.start()
    for copy in own_w:
        copy.start()
    cotangent = pltpu.make_async_copy(cot_ref, dy, l_sem.at[1, 0])
    cotangent.start()
    stream = pltpu.make_async_copy(x_ref, hc, l_sem.at[1, 1])
    stream.start()

    small_ref[...] = jnp.zeros_like(small_ref)
    for row, value, query in ((0, 1, 0), (1, 2, 2)):
        for r in range(HEADS):
            small_ref[row:row + 1, part + 64 * r:part + 64 * (r + 1)] = bias_ref[HEADS * value + r]
            small_ref[row:row + 1, 2 * part + 64 * r:2 * part + 64 * (r + 1)] = bias_ref[HEADS * query + r]
    for r in range(b1_ref.shape[0]):
        small_ref[2:3, 128 * r:128 * (r + 1)] = b1_ref[r]
    rel = rel_ref.shape[2]
    for r in range(HEADS):
        small_ref[3 + r:4 + r, 0:rel] = rel_ref[r]
    wide = small_ref.shape[1]
    table = small_ref[...]
    lane = lax.broadcasted_iota(jnp.int32, table.shape, 1)
    line = lax.broadcasted_iota(jnp.int32, table.shape, 0)
    low, high = pltpu.roll(table, wide - rel // 2, 1), pltpu.roll(table, 2 * length - rel // 2, 1)
    around = jnp.where(lane < rel // 2, low, jnp.where(lane < length, table[:, rel - 1:rel],
                       jnp.where(lane < 2 * length - rel // 2, table[:, 0:1], high)))
    small_ref[...] = jnp.where((line >= 3) & (line < 3 + HEADS) & (lane < 2 * length), around, table)
    pl.semaphore_wait(barrier, mp + 2)
    for copy in own_a:
        copy.wait()

    def rows(which, hh=None):
        if hh is None:
            return pl.ds(pl.multiple_of(which * part, 16), part)
        size = part // HALVES
        return pl.ds(pl.multiple_of(which * part + hh * size, 16), size)

    def along(src, shard, b, hh, way, dist):
        return pltpu.make_async_remote_copy(
            src_ref=src, dst_ref=bufs[b].at[shard, rows(quarter, hh)],
            send_sem=z_send.at[way, dist - 1, b, hh], recv_sem=z_recv.at[way, dist - 1, b, hh],
            device_id={"mp": me + 1 - 2 * way}, device_id_type=MESH)

    def across(kind, shard, b, hh, which, way, dist, to):
        ref = bufs[b].at[shard, rows(which, hh)]
        return pltpu.make_async_remote_copy(
            src_ref=ref, dst_ref=ref,
            send_sem=p_send.at[kind, way, dist - 1, b, hh], recv_sem=p_recv.at[kind, way, dist - 1, b, hh],
            device_id={"dp": to}, device_id_type=MESH)

    def small_copy(hop, slot):
        return pltpu.make_async_remote_copy(
            src_ref=smalls.at[me], dst_ref=smalls.at[slot],
            send_sem=s_send.at[hop - 1], recv_sem=s_recv.at[hop - 1],
            device_id={"mp": lax.rem(me + hop, mp)}, device_id_type=MESH)

    def over(index, src, dst):
        return pltpu.make_async_remote_copy(
            src_ref=src, dst_ref=dst, send_sem=x_send.at[index], recv_sem=x_recv.at[index],
            device_id={"section": 1 - section}, device_id_type=MESH)

    def over_rows(i):
        return over(i, cross_ref.at[i], wc.at[me, i * part:(i + 1) * part])

    def over_mem(u):
        return over(3 + u, mem.at[utt(u)], mem.at[utt(u)])

    def over_dmem(u):
        return over(3 + utts + u, dmem.at[utt(u)], dmem.at[utt(u)])

    over_small = over(2, small_ref, peer_small)
    over_cb = over(3 + 2 * utts, cb, cb)
    over_kv = over(4 + 2 * utts, kv_grad.at[0], kv_grad.at[1])

    def has_next(way):
        return (me < mp - 1) if way == 0 else (me > 0)

    def has_shard(way, dist):
        return (me >= dist) if way == 0 else (me + dist <= mp - 1)

    def shard_at(way, dist):
        return me - dist if way == 0 else me + dist

    def own_src(b, hh):
        src = (wa.at[me], wc.at[me], w1_ref, w2_ref)[b]
        return src.at[rows(quarter, hh)]

    def own_send(b):
        for hh in range(HALVES):
            for way in (0, 1):
                @pl.when(needed(b) & has_next(way))
                def _():
                    along(own_src(b, hh), me, b, hh, way, 1).start()

    own_send(0)

    @pl.when(encoding)
    def _():
        for i in (0, 1):
            over_rows(i).start()
        over_small.start()
        smalls[me] = small_ref[...]
    own_send(2)

    @pl.when(decoding)
    def _():
        over_small.wait_recv()
        smalls[me] = small_ref[...]
        lane = lax.broadcasted_iota(jnp.int32, (1, small_ref.shape[1]), 1)
        smalls[me, 1:2] = jnp.where(lane < 2 * part, peer_small[1:2], small_ref[1:2])
    for hop in range(1, mp):
        small_copy(hop, me).start()

    steps = [(b, dist, hh) for b, dist in SEQUENCE for hh in range(HALVES)]

    def on_line(k):
        b, dist, hh = steps[k]
        for way in (0, 1):
            @pl.when(needed(b) & has_shard(way, dist))
            def _():
                shard = shard_at(way, dist)
                src = bufs[b].at[shard, rows(quarter, hh)]
                along(src, shard, b, hh, way, dist).wait_recv()
                if dist < mp - 1:
                    @pl.when(has_next(way))
                    def _():
                        along(src, shard, b, hh, way, dist + 1).start()
                across(1, shard, b, hh, quarter, way, dist, side).start()
                across(0, shard, b, hh, quarter, way, dist, core).start()
        if k == 0:
            own_send(3)
        if k == 2 * HALVES:
            @pl.when(decoding)
            def _():
                for copy in own_c:
                    copy.wait()
                for i in (0, 1):
                    over_rows(i).wait_recv()
            own_send(1)

    def on_side(k):
        b, dist, hh = steps[k]
        for way in (0, 1):
            @pl.when(needed(b) & has_shard(way, dist))
            def _():
                shard = shard_at(way, dist)
                across(1, shard, b, hh, side_quarter, way, dist, side).wait_recv()
                across(2, shard, b, hh, side_quarter, way, dist, core).start()

    def complete(k):
        b, dist, hh = steps[k]
        for way in (0, 1):
            @pl.when(needed(b) & has_shard(way, dist))
            def _():
                shard = shard_at(way, dist)
                across(0, shard, b, hh, core_quarter, way, dist, core).wait_recv()
                across(2, shard, b, hh, diag_quarter, way, dist, core).wait_recv()

    def run(*events):
        for event in events:
            act = {"L": on_line, "S": on_side, "P": complete}[event[0]]
            for hh in range(HALVES):
                act(int(event[1:]) * HALVES + hh)

    def drain():
        for hop in range(1, mp):
            small_copy(hop, me).wait_send()
        for b in range(BLOCKS):
            for hh in range(HALVES):
                for way in (0, 1):
                    @pl.when(needed(b) & has_next(way))
                    def _():
                        along(own_src(b, hh), me, b, hh, way, 1).wait_send()
        for b, dist, hh in steps:
            for way in (0, 1):
                @pl.when(needed(b) & has_shard(way, dist))
                def _():
                    shard = shard_at(way, dist)
                    across(0, shard, b, hh, quarter, way, dist, core).wait_send()
                    across(1, shard, b, hh, quarter, way, dist, side).wait_send()
                    across(2, shard, b, hh, side_quarter, way, dist, core).wait_send()
                    if dist < mp - 1:
                        @pl.when(has_next(way))
                        def _():
                            along(bufs[b].at[shard, rows(quarter, hh)], shard, b, hh, way, dist + 1).wait_send()

    def shard_of(i):
        return jnp.where(lax.rem(i, 2) == 0, mp - 1 - i // 2, i // 2)

    spots = 3 * mp + mp * section

    def place(b, i):
        return (spots - mp + i, 2 * mp + i, 2 * i + 1, 2 * i)[b]

    def piece(b, m, which, hh=None):
        return bufs[b].at[m, rows(which, hh)]

    cut = part // HALVES

    def to_core(b, i, m, k):
        return pltpu.make_async_remote_copy(
            src_ref=piece(b, m, 2 * k + 1 - parity), dst_ref=from_core.at[lax.rem(place(b, i), RING), k],
            send_sem=c_send.at[b, m, k], recv_sem=c_recv.at[b, m, k],
            device_id={"dp": core}, device_id_type=MESH)

    def to_side(b, m, hh):
        return pltpu.make_async_remote_copy(
            src_ref=piece(b, m, 2 * (1 - half) + parity, hh), dst_ref=from_side.at[b, m, pl.ds(hh * cut, cut)],
            send_sem=y_send.at[b, m, hh], recv_sem=y_recv.at[b, m, hh],
            device_id={"dp": side}, device_id_type=MESH)

    def line_slot(way, m, at):
        return m if way == 0 else jnp.where(m == at, mp, m)

    def to_line(way, b, m, hh):
        to = me + 1 - 2 * way
        return pltpu.make_async_remote_copy(
            src_ref=piece(b, m, quarter, hh), dst_ref=from_line.at[line_slot(way, m, to), b, pl.ds(hh * cut, cut)],
            send_sem=r_send.at[way, b, m, hh], recv_sem=r_recv.at[way, b, m, hh],
            device_id={"mp": to}, device_id_type=MESH)

    def add(b, m, which, other, hh=None):
        ref = piece(b, m, which, hh)
        ref[...] = (ref[...].astype(f32) + other[...].astype(f32)).astype(bf16)

    def send_core(b, i):
        @pl.when(needed(b))
        def _():
            @pl.when(place(b, i) >= RING)
            def _():
                pl.semaphore_wait(credit, 1)
            for k in (0, 1):
                to_core(b, i, shard_of(i), k).start()

    def stage_core(b, i):
        m = shard_of(i)
        spot = place(b, i)

        @pl.when(needed(b))
        def _():
            for k in (0, 1):
                to_core(b, i, m, k).wait_recv()
                add(b, m, 2 * k + parity, from_core.at[lax.rem(spot, RING), k])
            for hh in range(HALVES):
                to_side(b, m, hh).start()

            @pl.when(spot + RING < spots)
            def _():
                pl.semaphore_signal(credit, inc=1, device_id={"dp": core}, device_id_type=MESH)

    def stage_side(b, i):
        m = shard_of(i)

        @pl.when(needed(b))
        def _():
            for hh in range(HALVES):
                to_side(b, m, hh).wait_recv()
                add(b, m, quarter, from_side.at[b, m, pl.ds(hh * cut, cut)], hh)
                for way in (0, 1):
                    first = (me == 0) if way == 0 else (me == mp - 1)

                    @pl.when(first & (me != m))
                    def _():
                        to_line(way, b, m, hh).start()

    def stage_line(b, i, hop):
        m = shard_of(i)
        for way in (0, 1):
            inner = ((me == hop) & (me < m)) if way == 0 else ((me == mp - 1 - hop) & (me > m))

            @pl.when(needed(b) & inner)
            def _():
                for hh in range(HALVES):
                    to_line(way, b, m, hh).wait_recv()
                    add(b, m, quarter, from_line.at[m, b, pl.ds(hh * cut, cut)], hh)
                    to_line(way, b, m, hh).start()

    def ffn_ticks(i):
        stage_side(3, i)

        @pl.when(i > 0)
        def _():
            stage_line(2, i - 1, 1)
            stage_line(3, i - 1, 2)
        stage_side(2, i)
        stage_line(3, i, 1)

        @pl.when(i > 0)
        def _():
            stage_line(2, i - 1, 2)

    def cross_tick(i):
        stage_side(1, i)

        @pl.when(i == 0)
        def _():
            stage_line(2, mp - 1, 1)
            stage_line(3, mp - 1, 2)

        @pl.when(i > 0)
        def _():
            stage_line(1, i - 1, 1)

        @pl.when(i == 1)
        def _():
            stage_line(2, mp - 1, 2)

        @pl.when(i > 1)
        def _():
            stage_line(1, i - 2, 2)

    def self_tick(i):
        stage_side(0, i)
        if i == 0:
            @pl.when(encoding)
            def _():
                stage_line(2, mp - 1, 1)
                stage_line(3, mp - 1, 2)
            stage_line(1, mp - 1, 1)
            stage_line(1, mp - 2, 2)
        else:
            stage_line(0, i - 1, 1)
        if i == 1:
            @pl.when(encoding)
            def _():
                stage_line(2, mp - 1, 2)
            stage_line(1, mp - 1, 2)
        if i > 1:
            stage_line(0, i - 2, 2)

    stream.wait()

    def prepare(rws):
        x = hc[rws].astype(f32)
        h[rws] = norm(x, vec_ref[0:1], vec_ref[1:2]).astype(bf16)
        x1[rws] = x + vec_ref[2:3]
    row_loop(total, 256, prepare)

    query_at = lax.broadcasted_iota(jnp.int32, (1, length), 1)

    def limits(u):
        last = lens_ref[section, me * utts + u] - 1
        return jnp.where(decoding, jnp.minimum(query_at, last), last)

    def frames(u):
        return jnp.full((1, length), lens_ref[0, me * utts + u] - 1, jnp.int32)

    lane = lax.broadcasted_iota(jnp.int32, (1, PROJ), 1)
    scale = jnp.where((lane >= KV) & (lane < KV + part), 0.125, 1.0)

    def self_shards(g, carry):
        shards = (2 * g, 2 * g + 1)
        for m in shards:
            def keep(cols, value):
                qkv[m, :, cols] = ((value + smalls[m, 0:1, cols]) * scale[:, cols]).astype(bf16)
            wide_dot(nt, h[...], lambda s, n: wa[m, s:s + n], PROJ, keep)
        attend([(m, u) for m in shards for u in range(utts)], length, qkv, ctx, p, limits, smalls)
        x1[...] += nn(ctx[shards[0]], wa[shards[0], CTX:]) + nn(ctx[shards[1]], wa[shards[1], CTX:])
        return carry

    def ffn_one(m):
        ffn_shard(m, slice(0, total), h, w1, w2, a, gp, smalls[m, 2:3], out)

    def ffn_at(dist):
        @pl.when(encoding)
        def _():
            def step(way, carry):
                @pl.when(jnp.where(way == 0, me >= dist, me + dist <= mp - 1))
                def _():
                    ffn_one(jnp.where(way == 0, me - dist, me + dist))
                return carry
            lax.fori_loop(0, 2, step, 0)

    run("L0", "L1", "S0", "L2", "P0", "L3", "S1", "S2", "L4", "P1", "P2", "S4", "L5", "L6", "P4")
    for hop in range(1, mp):
        small_copy(hop, lax.rem(me + mp - hop, mp)).wait_recv()
    lax.fori_loop(0, mp // 4, self_shards, 0)
    run("L7", "L8", "S3")
    lax.fori_loop(mp // 4, mp // 2, self_shards, 0)
    for copy in own_w:
        copy.wait()
    spill = [pltpu.make_async_copy(src, dst, i_sem.at[j]) for j, (src, dst) in enumerate(
        ((qkv, qkv_hbm), (ctx, ctx_hbm), (p, p_hbm)))]
    fetch = [pltpu.make_async_copy(dst, src, i_sem.at[j]) for j, (src, dst) in enumerate(
        ((qkv, qkv_hbm), (ctx, ctx_hbm), (p, p_hbm)))]
    give = pltpu.make_async_copy(out, out_hbm, i_sem.at[3])

    @pl.when(decoding)
    def _():
        for copy in spill:
            copy.start()

        def start_cross(rws):
            y = x1[rws]
            hc[rws] = norm(y, vec_ref[3:4], vec_ref[4:5]).astype(bf16)
            y2[rws] = y
        row_loop(total, 256, start_cross)

    @pl.when(encoding)
    def _():
        row_loop(total, length, lambda rws: ffn_start(rws, x1, out, h, vec_ref))
        ffn_one(me)

    run("L9", "L10", "S5", "P3")
    ffn_at(1)

    run("S6", "L11", "S7", "S8", "P5", "P6", "P8")
    ffn_at(2)
    run("S9", "S10", "S11", "P7", "P9", "P10", "P11")
    ffn_at(3)

    @pl.when(decoding)
    def _():
        for copy in spill:
            copy.wait()

        def queries(m, carry):
            pq = nt(hc[...], wc[m, KV:PROJ])
            qkv[m, :, KV:] = ((pq + smalls[m, 1:2, KV:PROJ]) * scale[:, KV:]).astype(bf16)
            return carry
        lax.fori_loop(0, mp, queries, 0)

    @pl.when(encoding)
    def _():
        for u in range(utts):
            mem[utt(u)] = norm(out[utt(u)], vec_ref[3:4], vec_ref[4:5]).astype(bf16)
            over_mem(u).start()
        give.start()
        drain()
        cotangent.wait()
        g[...] = dy[...].astype(f32)
        turn(ht, h[...])
        give.wait()
        for u in range(utts):
            over_dmem(u).wait_recv()
        norm_back(total, out, vec_ref[3:4], dmem, g, vg, 3)

        dy[...] = g[...].astype(bf16)
        turn(dyt, dy[...])
        vg[7:8, :] = jnp.sum(g[...], axis=0, keepdims=True)
        dh[...] = jnp.zeros_like(dh)

        def ffn_step(i, carry):
            m = shard_of(i)
            hidden_grad(m, gp, w2, dy, sg)
            w2[m] = nn(dyt[...], a[m]).astype(bf16)
            send_core(3, i)

            @pl.when(i > 0)
            def _():
                stage_core(2, i - 1)
            dh[...] += nt(gp[m], w1[m])
            w1[m] = nn(ht[...], gp[m]).astype(bf16)
            send_core(2, i)
            stage_core(3, i)

            @pl.when(i >= mp // 2)
            def _():
                ffn_ticks(i - mp // 2)
            return carry
        lax.fori_loop(0, mp, ffn_step, 0)
        norm_back(total, x1, vec_ref[5:6], dh, g, vg, 5)
        stage_core(2, mp - 1)
        over_cb.wait_recv()
        sg[pl.ds(0, mp), 1:2, :PROJ] = cb[:, 0:1, :]

    @pl.when(decoding)
    def _():
        def cross_utt(u, carry):
            over_mem(u).wait_recv()
            rws = utt(u)
            for m in range(mp):
                qkv[m, rws, :KV] = (nt(mem[rws], wc[m, :KV]) + smalls[m, 1:2, :KV]).astype(bf16)
            attend([(m, u) for m in range(mp)], length, qkv, ctx, p, frames, None)
            y2[rws] += sum(nn(ctx[m, rws], wc[m, CTX:]) for m in range(mp))
            ffn_start(rws, y2, out, h, vec_ref)

            def one(m, carry):
                ffn_shard(m, rws, h, w1, w2, a, gp, smalls[m, 2:3], out)
                return carry
            return lax.fori_loop(0, mp, one, carry)
        lax.fori_loop(0, utts, cross_utt, 0)
        give.start()
        cotangent.wait()
        g[...] = dy[...].astype(f32)
        vg[7:8, :] = jnp.sum(g[...], axis=0, keepdims=True)
        dy[...] = g[...].astype(bf16)
        turn(dyt, dy[...])
        turn(ht, h[...])
        drain()
        give.wait()
        dh[...] = jnp.zeros_like(dh)

        def dgrad(m, carry):
            hidden_grad(m, gp, w2, dy, sg)
            dh[...] += nt(gp[m], w1[m])
            return carry
        lax.fori_loop(0, mp, dgrad, 0)
        norm_back(total, y2, vec_ref[5:6], dh, g, vg, 5)

        early = 1

        def ffn_weights(i, carry):
            m = shard_of(i)
            w2[m] = nn(dyt[...], a[m]).astype(bf16)
            send_core(3, i)

            @pl.when((i > 0) & (i != early))
            def _():
                stage_core(2, i - 1)
            w1[m] = nn(ht[...], gp[m]).astype(bf16)
            send_core(2, i)
            stage_core(3, i)

            @pl.when(i >= mp // 2)
            def _():
                ffn_ticks(i - mp // 2)
            return carry
        lax.fori_loop(0, early, ffn_weights, 0)

        dy[...] = g[...].astype(bf16)

        def cross_back(u, carry):
            rws = utt(u)
            for pair in range(0, mp, 2):
                shards = (pair, pair + 1)
                for m in shards:
                    dctx[m - pair] = nt(dy[rws], wc[m, CTX:]).astype(bf16)
                attend_back([(m, u) for m in shards], length, qkv, p,
                            lambda m, rows, t: tile(dctx, m - pair, slice(None), t), qkv, None, None)
            dmem[rws] = sum(nn(qkv[m, rws, :KV], wc[m, :KV]) for m in range(mp)).astype(bf16)
            over_dmem(u).start()
            dh[rws] = sum(nn(qkv[m, rws, KV:], wc[m, KV:PROJ]) for m in range(mp))

            @pl.when(u == 0)
            def _():
                stage_core(2, early - 1)
            return carry
        lax.fori_loop(0, utts, cross_back, 0)
        lax.fori_loop(early, mp, ffn_weights, 0)

        def row_sums(m, carry):
            sums = jnp.sum(qkv[m].astype(f32), axis=0, keepdims=True)
            sg[m, 1:2, :PROJ] = sums
            cb[m, 0:1, :] = sums
            return carry
        lax.fori_loop(0, mp, row_sums, 0)
        over_cb.start()
        norm_back(total, x1, vec_ref[3:4], dh, g, vg, 3)
        turn(dyt, dy[...])
        turn(ht, hc[...])
        stream.start()

        def cross_weights(i, carry):
            m = shard_of(i)
            wc[m, :, :KV] = tn(mem[...], qkv[m, :, :KV]).astype(bf16)
            gq = nn(ht[...], qkv[m, :, KV:])
            go = nn(dyt[...], ctx[m])
            wc[m, :, KV:CTX] = gq[:, :T].astype(bf16)
            wc[m, :, CTX:PROJ] = (gq[:, T:] + go[:, :T]).astype(bf16)
            wc[m, :, PROJ:] = go[:, T:].astype(bf16)

            @pl.when(i == 0)
            def _():
                stage_core(2, mp - 1)
            send_core(1, i)

            @pl.when(i > 0)
            def _():
                stage_core(1, i - 1)

            @pl.when(i < mp // 2)
            def _():
                ffn_ticks(i + mp // 2)
            return carry
        lax.fori_loop(0, mp, cross_weights, 0)
        for copy in fetch:
            copy.start()
        stage_core(1, mp - 1)
        for copy in fetch:
            copy.wait()
        stream.wait()

    def prepare_self(rws):
        h[rws] = norm(hc[rws].astype(f32), vec_ref[0:1], vec_ref[1:2]).astype(bf16)
    row_loop(total, 256, prepare_self)
    vg[2:3, :] = jnp.sum(g[...], axis=0, keepdims=True)
    dy[...] = g[...].astype(bf16)
    turn(dyt, dy[...])
    turn(ht, h[...])
    dh[...] = jnp.zeros_like(dh)
    down = lax.broadcasted_iota(jnp.int32, (length, length), 0)
    right = lax.broadcasted_iota(jnp.int32, (length, length), 1)
    flip = (down + right == length - 1).astype(f32).astype(bf16)

    def dctx_at(rows, t):
        return tile(dctx, rows.start // length, slice(None), t)

    def self_step(i, carry):
        m = shard_of(i)
        for u in range(utts):
            dctx[u] = nt(dy[utt(u)], wa[m, CTX:]).astype(bf16)
        attend_back([(m, u) for u in range(utts)], length, qkv, p, lambda m, rows, t: dctx_at(rows, t), qkv, sg, flip)
        d = qkv[m]
        sg[m, 0:1, :PROJ] = jnp.sum(d.astype(f32), axis=0, keepdims=True)
        dh[...] += nn(d, wa[m, :PROJ])
        gd = nn(ht[...], d)
        go = nn(dyt[...], ctx[m])
        wa[m, :, :CTX] = gd[:, :CTX].astype(bf16)
        wa[m, :, CTX:PROJ] = (gd[:, CTX:] + go[:, :T]).astype(bf16)
        wa[m, :, PROJ:] = go[:, T:].astype(bf16)
        send_core(0, i)

        @pl.when(i > 0)
        def _():
            stage_core(0, i - 1)

        @pl.when(encoding & (i < mp // 2))
        def _():
            ffn_ticks(i + mp // 2)

        @pl.when(decoding)
        def _():
            cross_tick(i)
        return carry
    lax.fori_loop(0, mp, self_step, 0)
    norm_back(total, hc, vec_ref[0:1], dh, g, vg, 0)
    give_dx = pltpu.make_async_copy(g, dx_hbm, i_sem.at[3])
    give_dx.start()

    def small_sum(hop, src, to):
        return pltpu.make_async_remote_copy(
            src_ref=src, dst_ref=got_small.at[hop], send_sem=a_send.at[hop], recv_sem=a_recv.at[hop],
            device_id={"dp": to}, device_id_type=MESH)

    with_core, with_side = small_sum(0, sg, core), small_sum(1, pair_sg, side)
    with_core.start()
    with_core.wait_recv()
    pair_sg[...] = sg[...] + got_small[0]
    with_side.start()
    stage_core(0, mp - 1)
    self_tick(0)
    self_tick(1)
    with_side.wait_recv()
    with_core.wait_send()
    sg[...] = pair_sg[...] + got_small[1]

    def line_small(hop, which):
        peer = lax.rem(me + hop, mp)
        src = sg.at[peer] if which == 0 else sg.at[mp]
        return pltpu.make_async_remote_copy(
            src_ref=src, dst_ref=got_line.at[hop - 1, which],
            send_sem=b_send.at[hop - 1, which], recv_sem=b_recv.at[hop - 1, which],
            device_id={"mp": peer}, device_id_type=MESH)

    for hop in range(1, mp):
        for which in (0, 1):
            line_small(hop, which).start()
    stage = (x1.at[pl.ds(0, part)], x1.at[pl.ds(part, part)], y2.at[pl.ds(0, part)], y2.at[pl.ds(part, part)])

    def finish(b):
        stage[b][...] = bufs[b][me, rows(quarter)].astype(f32)

        @pl.when(me > 0)
        def _():
            for hh in range(HALVES):
                to_line(0, b, me, hh).wait_recv()
            stage[b][...] += from_line[me, b].astype(f32)

        @pl.when(me < mp - 1)
        def _():
            for hh in range(HALVES):
                to_line(1, b, me, hh).wait_recv()
            stage[b][...] += from_line[mp, b].astype(f32)

    def hand(b):
        return pltpu.make_async_copy(stage[b], own_hbm.at[b], l_sem.at[b, 0])

    self_tick(2)
    @pl.when(decoding)
    def _():
        finish(1)
        kv_grad[0] = stage[1][:, :2 * part].astype(bf16)
        over_kv.start()
        hand(1).start()
    for b in (3, 2):
        finish(b)
        hand(b).start()
    self_tick(3)
    stage_line(0, mp - 1, 1)
    stage_line(0, mp - 2, 2)
    stage_line(0, mp - 1, 2)
    small_out[0] = sg[me]
    small_out[1] = sg[mp]
    for hop in range(1, mp):
        for which in (0, 1):
            line_small(hop, which).wait_recv()
            small_out[which] += got_line[hop - 1, which]

    finish(0)
    hand(0).start()

    @pl.when(encoding)
    def _():
        over_kv.wait_recv()
        stage[1][:, :2 * part] = kv_grad[1].astype(f32)
        hand(1).start()

    @pl.when(encoding)
    def _():
        for i in (0, 1):
            over_rows(i).wait_send()
        over_small.wait_send()
        for u in range(utts):
            over_mem(u).wait_send()

    @pl.when(decoding)
    def _():
        for u in range(utts):
            over_dmem(u).wait_send()
        over_cb.wait_send()
        over_kv.wait_send()
    with_side.wait_send()
    for hop in range(1, mp):
        for which in (0, 1):
            line_small(hop, which).wait_send()

    def left(i, carry):
        m = shard_of(i)
        for b in range(BLOCKS):
            @pl.when(needed(b))
            def _():
                for k in (0, 1):
                    to_core(b, i, m, k).wait_send()
                for hh in range(HALVES):
                    to_side(b, m, hh).wait_send()
                    for way in (0, 1):
                        @pl.when((me < m) if way == 0 else (me > m))
                        def _():
                            to_line(way, b, m, hh).wait_send()
        return carry
    lax.fori_loop(0, mp, left, 0)
    for b in range(BLOCKS):
        hand(b).wait()
    give_dx.wait()


def layers(mp, dp, utts, length, lens, x, cot, vec, biases, b_one, rel, w_in, w_o, w_cross, w_one, w_two):
    total, width = x.shape
    hidden = w_one.shape[1]
    sds = jax.ShapeDtypeStruct
    v = pltpu.VMEM
    sem = pltpu.SemaphoreType.DMA
    shard = v((mp, width, hidden), bf16)
    part = width // 4
    wide_b, wide_f = v((total, width), bf16), v((total, width), f32)
    turned = v((width, total), bf16)
    heads = (utts, mp, HEADS, length, length)
    proj, context = (mp, total, PROJ), (mp, total, 2 * LANES)
    rows = (8, width)
    gather = (2, mp - 1, BLOCKS, HALVES)
    return pl.pallas_call(
        functools.partial(layers_kernel, mp, dp, utts, length),
        out_shape=(sds((2,) + rows, f32), sds((total, width), f32), sds((total, width), f32),
                   sds((BLOCKS, part, hidden), f32), sds(proj, bf16), sds(context, bf16), sds(heads, bf16)),
        in_specs=[SMEM, ANY, ANY, VM, VM, VM, VM] + [ANY] * 5,
        out_specs=(VM,) + (ANY,) * 6,
        scratch_shapes=[wide_f] + [shard] * 4 + [
            v((mp,) + rows, f32), v(rows, f32), v(rows, f32), v(proj, bf16), v(context, bf16), v(heads, bf16),
            v((mp, total, hidden), bf16), v((mp, total, hidden), bf16),
            wide_f, wide_f, wide_f, wide_b, wide_b, wide_b, wide_b,
            wide_b, turned, turned, v((max(utts, 2), length, 2 * LANES), bf16), v((mp + 1,) + rows, f32),
            v((mp, 8, PROJ), f32),
            v((RING, 2, part, hidden), bf16), v((BLOCKS, mp, part, hidden), bf16), v((mp + 1, BLOCKS, part, hidden), bf16),
            v((mp + 1,) + rows, f32), v((2, mp + 1) + rows, f32), v((mp - 1, 2) + rows, f32),
            v((2, part, 2 * part), bf16),
            sem((BLOCKS, 4)), sem(gather), sem(gather), sem((3,) + gather), sem((3,) + gather),
            sem((mp - 1,)), sem((mp - 1,)), sem((5 + 2 * utts,)), sem((5 + 2 * utts,)), sem((4,)),
            sem((BLOCKS, mp, 2)), sem((BLOCKS, mp, 2)), sem((BLOCKS, mp, HALVES)), sem((BLOCKS, mp, HALVES)),
            sem((2, BLOCKS, mp, HALVES)), sem((2, BLOCKS, mp, HALVES)), pltpu.SemaphoreType.REGULAR,
            sem((2,)), sem((2,)), sem((mp - 1, 2)), sem((mp - 1, 2))],
        compiler_params=pltpu.CompilerParams(collective_id=0, has_side_effects=True, vmem_limit_bytes=63 * 2**20),
        name="both_layers",
    )(lens, x, cot, vec, biases, b_one, rel, w_in, w_o, w_cross, w_one, w_two)


def finish_kernel(mp, dp, length, rel, own_in, small, out_in, dx_in,
                  out, dx, vectors, in_grad, bias, o_grad, rel_grad, cross, one, b1, two,
                  own, out_held, dx_held, in_sem, out_sem):
    me = lax.axis_index("mp")
    dp_index = lax.axis_index("dp")
    decoding = lax.axis_index("section") == 1
    loads = [pltpu.make_async_copy(src, dst, in_sem.at[j]) for j, (src, dst) in enumerate(
        ((own_in.at[0], own.at[0]), (own_in.at[1], own.at[1]), (out_in, out_held), (dx_in, dx_held),
         (own_in.at[2], own.at[2]), (own_in.at[3], own.at[3])))]
    stores = [pltpu.make_async_copy(src, dst, out_sem.at[j]) for j, (src, dst) in enumerate(
        ((out_held, out), (dx_held, dx), (own.at[2], one), (own.at[3], two)))]
    for copy in loads:
        copy.start()
    for copy in loads[:2]:
        copy.wait()
    part = own.shape[1]
    k, v, q, o = (slice(t * part, (t + 1) * part) for t in range(4))
    mine = own[0]
    in_grad[0], in_grad[1], in_grad[2] = mine[:, q], mine[:, k], mine[:, v]
    o_grad[...] = mine[:, o].T
    mine = own[1]
    cross[0] = jnp.where(decoding, mine[:, q], mine[:, k])
    cross[1] = jnp.where(decoding, mine[:, o], mine[:, v])
    for load, store in zip(loads[2:], stores):
        load.wait()
        store.start()

    width = small.shape[2]

    def back(value, by):
        return pltpu.roll(value, lax.rem(width - by, width), 1)

    vectors[...] = back(small[1], (dp_index * mp + me) * vectors.shape[1])[:, :vectors.shape[1]]
    size = bias.shape[2]
    turned = back(small[0], dp_index * size)
    cross_row = jnp.where(decoding, turned[1:2, q], turned[1:2, v])
    for t, row in enumerate((turned[0:1, q], turned[0:1, v], cross_row)):
        for r in range(HEADS):
            bias[3 * t + r] = row[:, 64 * r:64 * r + size]
    size = b1.shape[2]
    turned = back(small[0], dp_index * size)
    for r in range(b1.shape[0]):
        b1[r] = turned[2:3, 128 * r:128 * r + size]
    lines = small[0]
    low, high = length - rel // 2, length + rel // 2 - 2
    lane = lax.broadcasted_iota(jnp.int32, lines.shape, 1)
    first = jnp.sum(jnp.where(lane < low, lines, 0.0), axis=1, keepdims=True)
    last = jnp.sum(jnp.where((lane >= high) & (lane < 2 * length), lines, 0.0), axis=1, keepdims=True)
    moved = pltpu.roll(lines, width - (low - 1), 1)
    moved = jnp.where(lane == 0, first, jnp.where(lane == rel - 1, last, moved))
    moved = back(moved, dp_index * rel_grad.shape[2])
    for r in range(HEADS):
        rel_grad[r] = moved[3 + r:4 + r, :rel_grad.shape[2]]
    for store in stores:
        store.wait()


def finish(mp, dp, length, rel, own, small, out, dx):
    sds = jax.ShapeDtypeStruct
    part, hidden = own.shape[1:]
    width = small.shape[2]
    shard = width // mp
    return pl.pallas_call(
        functools.partial(finish_kernel, mp, dp, length, rel),
        out_shape=(sds(out.shape, f32), sds(dx.shape, f32), sds((8, width // (dp * mp)), f32),
                   sds((3, part, shard), f32), sds((3 * HEADS, 1, 64 // dp), f32), sds((shard, part), f32),
                   sds((HEADS, 1, rel // dp), f32), sds((2, part, shard), f32), sds((part, hidden), f32),
                   sds((hidden // 128, 1, 128 // dp), f32), sds((part, hidden), f32)),
        in_specs=[ANY, VM, ANY, ANY], out_specs=(ANY,) * 2 + (VM,) * 6 + (ANY, VM, ANY),
        scratch_shapes=[pltpu.VMEM(own.shape, f32), pltpu.VMEM(out.shape, f32), pltpu.VMEM(dx.shape, f32),
                        pltpu.SemaphoreType.DMA((6,)), pltpu.SemaphoreType.DMA((4,))],
        compiler_params=pltpu.CompilerParams(vmem_limit_bytes=60 * 2**20), name="finish",
    )(own, small, out, dx)


def per_device(streams, lengths, vectors, attn_in, attn_bias, attn_out, rel_table, cross, ffn_in, ffn_bias, ffn_out,
               cotangent):
    mp = lax.axis_size("mp")
    dp = lax.axis_size("dp")
    utts, length, width = streams.shape[1:]
    total = utts * length
    x = streams[0].reshape(total, width)
    cot = cotangent[0].reshape(total, width)
    vec = vectors[0]

    small_sum, g, out, own, _, _, _ = layers(
        mp, dp, utts, length, lengths, x, cot, vec, jnp.transpose(attn_bias, (1, 2, 0, 3)).reshape(3 * HEADS, 1, -1),
        jnp.swapaxes(ffn_bias, 0, 1), jnp.swapaxes(rel_table, 0, 1), jnp.swapaxes(attn_in[0], 1, 2), attn_out[0],
        jnp.swapaxes(cross[0], 1, 2), ffn_in[0], ffn_out[0])
    if dp > 4:
        near = [[q * (dp // 4) + i for i in range(dp // 4)] for q in range(4)]
        small_sum = lax.psum(small_sum, "dp", axis_index_groups=near)
    out, dx, vectors_grad, in_grad, bias_grad, o_grad, rel_grad, cross_grad, one_grad, b1_grad, two_grad = finish(
        mp, dp, length, rel_table.shape[2], own, small_sum, out, g)
    two_grad = two_grad.T
    if dp > 4:
        per = dp // 4
        groups = [[q * per + i for i in range(per)] for q in range(4)]

        def rest(value, axis):
            return lax.psum_scatter(value.astype(bf16), "dp", scatter_dimension=axis, axis_index_groups=groups,
                                    tiled=True).astype(f32)

        in_grad, o_grad, cross_grad = rest(in_grad, 1), rest(o_grad, 1), rest(cross_grad, 1)
        one_grad, two_grad = rest(one_grad, 0), rest(two_grad, 1)
    shape = (1, utts, length, width)
    bias_grad = bias_grad.reshape(3, HEADS, 1, -1)
    return (out.reshape(shape), dx.reshape(shape), vectors_grad[None], in_grad[None],
            jnp.transpose(bias_grad, (2, 0, 1, 3)), o_grad[None], jnp.swapaxes(rel_grad, 0, 1), cross_grad[None],
            one_grad[None], jnp.swapaxes(b1_grad, 0, 1), two_grad[None])


def solution(mesh):
    placed = (
        P("section", ("dp", "mp"), None, None),
        P(None, "dp"),
        P("section", None, None),
        P("section", None, None, "mp"),
        P("section", None, "mp", None),
        P("section", "mp", None),
        P("section", "mp", None),
        P("section", None, None, "mp"),
        P("section", None, "mp"),
        P("section", "mp", None),
        P("section", "mp", None),
        P("section", ("dp", "mp"), None, None),
    )
    return jax.shard_map(
        per_device,
        mesh=mesh,
        in_specs=placed,
        out_specs=(
            P("section", ("dp", "mp"), None, None),
            P("section", ("dp", "mp"), None, None),
            P("section", None, ("dp", "mp")),
            P("section", None, "dp", "mp"),
            P("section", None, "mp", "dp"),
            P("section", "mp", "dp"),
            P("section", "mp", "dp"),
            P("section", None, "dp", "mp"),
            P("section", "dp", "mp"),
            P("section", "mp", "dp"),
            P("section", "mp", "dp"),
        ),
        check_vma=False,
    )
```

```python
import functools
import jax
import jax.numpy as jnp
from jax import lax
from jax.experimental import pallas as pl
from jax.experimental.pallas import tpu as pltpu
from jax.sharding import PartitionSpec as P

MESH = pl.DeviceIdType.MESH
ANY = pl.BlockSpec(memory_space=pl.ANY)
VM = pl.BlockSpec(memory_space=pltpu.VMEM)
BLOCKS = 4


def partners(dp_index, step):
    bit = lax.rem(dp_index // step, 2)
    return dp_index + step - 2 * step * bit


EPSILON = 1e-05
MASKED = -1e30
HEADS = 3
LANES = 128
PROJ = 640
CTX = 512
bf16, f32 = jnp.bfloat16, jnp.float32


def nn(a, b):
    return lax.dot_general(a, b, (((1,), (0,)), ((), ())), preferred_element_type=f32)


def nt(a, b):
    return lax.dot_general(a, b, (((1,), (1,)), ((), ())), preferred_element_type=f32)


def tn(a, b):
    return lax.dot_general(a, b, (((0,), (0,)), ((), ())), preferred_element_type=f32)


def norm_parts(x):
    centred = x - jnp.mean(x, axis=-1, keepdims=True)
    r = lax.rsqrt(jnp.mean(centred * centred, axis=-1, keepdims=True) + EPSILON)
    return centred * r, r


def norm(x, gain, shift):
    xh, _ = norm_parts(x)
    return xh * gain + shift


def row_loop(total, size, body):
    def step(i, carry):
        body(pl.ds(pl.multiple_of(i * size, size), size))
        return carry
    lax.fori_loop(0, total // size, step, 0)


def even_lanes(rows):
    return lax.broadcasted_iota(jnp.int32, (rows, LANES), 1) < LANES // 2


def half_mask(half):
    lane = lax.broadcasted_iota(jnp.int32, (1, LANES), 1)
    on = (lane < LANES // 2) if half == 0 else (lane >= LANES // 2)
    return on.astype(f32).astype(bf16)


def tile(ref, m, rows, t):
    return ref[m, rows, t * LANES:(t + 1) * LANES]


HEAD_TILES = (((3, 0), (0, 0), (1, 1), (0, 1)),
              ((3, 1), (0, 1), (2, 0), (1, 0)),
              ((4, 0), (1, 0), (2, 1), (1, 1)))


def utt_rows(u, length):
    return pl.ds(u * length, length) if isinstance(u, int) else pl.ds(pl.multiple_of(u * length, length), length)


def attend(pairs, length, qkv_ref, ctx_ref, p_ref, limits, ext_ref):
    key_at = lax.broadcasted_iota(jnp.int32, (length, length), 0)
    even = even_lanes(length)
    parts, probs, biases = {}, {}, {}
    for r in range(HEADS):
        (qt, half), (kt, _), (vt, _), _ = HEAD_TILES[r]
        for n, (m, u) in enumerate(pairs):
            rows = utt_rows(u, length)
            s = nt(tile(qkv_ref, m, rows, kt) * half_mask(half), tile(qkv_ref, m, rows, qt))
            if ext_ref is not None:
                if (id(m), r) not in biases:
                    row = ext_ref[m, 3 + r:4 + r, :2 * length]
                    biases[id(m), r] = pltpu.roll(jnp.broadcast_to(row, (length, 2 * length)), 0, 1, stride=1,
                                                  stride_axis=0)[:, :length].T
                s = s + biases[id(m), r]
            s = jnp.where(key_at <= limits(u), s, MASKED)
            e = jnp.exp(s - jnp.max(s, axis=0, keepdims=True))
            p = (e * (1.0 / jnp.sum(e, axis=0, keepdims=True))).astype(bf16)
            probs[n, r] = p
            parts[n, r] = tn(p, tile(qkv_ref, m, rows, vt))
    for n, (m, u) in enumerate(pairs):
        rows = utt_rows(u, length)
        for r in range(HEADS):
            p_ref[u, m, r] = probs[n, r]
        ctx_ref[m, rows, :LANES] = jnp.where(even, 0.0, parts[n, 0]).astype(bf16)
        ctx_ref[m, rows, LANES:] = jnp.where(even, parts[n, 1], parts[n, 2]).astype(bf16)


def attend_back(pairs, length, qkv_ref, p_ref, dctx_of, out_ref, rel_ref, flip):
    even = even_lanes(length)
    got, total = {}, {}
    for r in range(HEADS):
        (qt, _), (kt, _), (vt, vhalf), (ot, _) = HEAD_TILES[r]
        for n, (m, u) in enumerate(pairs):
            rows = utt_rows(u, length)
            p = p_ref[u, m, r]
            dctx = dctx_of(m, rows, ot)
            dp = nt(tile(qkv_ref, m, rows, vt) * half_mask(vhalf), dctx)
            pf = p.astype(f32)
            t = pf * dp
            ds = (t - pf * jnp.sum(t, axis=0, keepdims=True)).astype(bf16)
            got[n, r] = (tn(ds, tile(qkv_ref, m, rows, kt)) * 0.125, nn(ds, tile(qkv_ref, m, rows, qt)), nn(p, dctx))
            if rel_ref is not None:
                turned = nn(ds, flip)
                total[r] = total[r] + turned if r in total else turned
    for r in total:
        m = pairs[0][0]
        wide = jnp.concatenate([total[r], jnp.zeros_like(total[r])], axis=1)
        wide = pltpu.roll(wide, 0, 1, stride=1, stride_axis=0)
        rel_ref[m, 3 + r:4 + r, :2 * length] = jnp.sum(wide, axis=0, keepdims=True)
    for n, (m, u) in enumerate(pairs):
        rows = utt_rows(u, length)
        (q0, k0, v0), (q1, k1, v1), (q2, k2, v2) = got[n, 0], got[n, 1], got[n, 2]
        for t, (left, right) in enumerate(((k0, k1), (k2, v0), (v1, v2), (q0, q1), (q2, 0.0))):
            out_ref[m, rows, t * LANES:(t + 1) * LANES] = jnp.where(even, left, right).astype(bf16)


def gelu_both(u):
    cdf = 0.5 + 0.5 * lax.erf(u * 0.7071067811865476)
    return u * cdf, cdf + u * (jnp.exp(-0.5 * u * u) * 0.3989422804014327)


def norm_back(total, x_ref, gain, dh_ref, add_into, vg_ref, gain_row, grad_out=None):
    width = gain.shape[-1]

    def step(i, carry):
        dgain, dshift = carry
        rows = pl.ds(pl.multiple_of(i * 256, 256), 256)
        dh = dh_ref[rows].astype(f32)
        xh, r = norm_parts(x_ref[rows].astype(f32))
        e = dh * gain
        dx = r * (e - jnp.mean(e, axis=-1, keepdims=True) - xh * jnp.mean(e * xh, axis=-1, keepdims=True))
        add_into[rows] = add_into[rows].astype(f32) + dx
        return dgain + jnp.sum(dh * xh, axis=0, keepdims=True), dshift + jnp.sum(dh, axis=0, keepdims=True)

    zero = jnp.zeros((1, width), f32)
    dgain, dshift = lax.fori_loop(0, total // 256, step, (zero, zero))
    vg_ref[gain_row:gain_row + 1, :] = dgain
    vg_ref[gain_row + 1:gain_row + 2, :] = dshift


def turn(dst_ref, src):
    dst_ref[...] = src.T


SMEM = pl.BlockSpec(memory_space=pltpu.SMEM)


SEQUENCE = ((0, 1), (2, 1), (0, 2), (3, 1), (0, 3), (1, 1), (2, 2), (1, 2), (3, 2), (1, 3), (2, 3), (3, 3))
HALVES = 2
RING = 4


def wide_dot(dot, a, b_cols, width, use, step=256):
    for start in range(0, width, step):
        size = min(step, width - start)
        use(slice(start, start + size), dot(a, b_cols(start, size)))


def ffn_shard(m, rows, h, w1, w2, a, gp, bias, out):
    def keep(cols, u):
        act, slope = gelu_both(u + bias[:, cols])
        a[m, rows, cols] = act.astype(bf16)
        gp[m, rows, cols] = slope.astype(bf16)
    wide_dot(nn, h[rows], lambda s, n: w1[m, :, s:s + n], w1.shape[2], keep)
    out[rows] += nn(a[m, rows], w2[m])


def ffn_start(rows, x_ref, out_ref, h_ref, vec_ref):
    x = x_ref[rows]
    h_ref[rows] = norm(x, vec_ref[5:6], vec_ref[6:7]).astype(bf16)
    out_ref[rows] = x + vec_ref[7:8]


def hidden_grad(m, gp, w2, dy, sg):
    def keep(cols, da):
        du = (da * gp[m, :, cols].astype(f32)).astype(bf16)
        gp[m, :, cols] = du
        sg[m, 2:3, cols] = jnp.sum(du.astype(f32), axis=0, keepdims=True)
    wide_dot(nt, dy[...], lambda s, n: w2[m, s:s + n], w2.shape[1], keep)


def layers_kernel(mp, dp, utts, length,
                  lens_ref, x_ref, cot_ref, vec_ref, bias_ref, b1_ref, rel_ref, in_ref, o_ref, cross_ref, w1_ref, w2_ref,
                  small_out, dx_hbm, out_hbm, own_hbm, qkv_hbm, ctx_hbm, p_hbm,
                  g, wa, wc, w1, w2, smalls, small_ref, peer_small, qkv, ctx, p, a, gp, x1, y2, out, h, hc, mem, dmem,
                  dy, dyt, ht, dctx, sg, cb, from_core, from_side, from_line, pair_sg, got_small, got_line,
                  kv_grad,
                  l_sem, z_send, z_recv, p_send, p_recv, s_send, s_recv, x_send, x_recv, i_sem,
                  c_send, c_recv, y_send, y_recv, r_send, r_recv, credit, a_send, a_recv, b_send, b_recv):
    me = lax.axis_index("mp")
    dp_index = lax.axis_index("dp")
    section = lax.axis_index("section")
    decoding = section == 1
    encoding = section == 0
    near = dp // 4
    core = partners(dp_index, near)
    side = partners(dp_index, 2 * near)
    quarter = dp_index // near
    parity = lax.rem(quarter, 2)
    half = quarter // 2
    core_quarter = quarter + 1 - 2 * parity
    side_quarter = quarter + 2 - 4 * half
    diag_quarter = core_quarter + 2 - 4 * half
    part = wa.shape[1] // 4
    total = utts * length
    T = LANES
    KV, PROJ_END = 3 * T, PROJ
    bufs = (wa, wc, w1, w2)
    dh = out
    vg = sg.at[mp]

    barrier = pltpu.get_barrier_semaphore()
    for hop in range(1, mp):
        pl.semaphore_signal(barrier, inc=1, device_id={"mp": lax.rem(me + hop, mp)}, device_id_type=MESH)
    for other in (core, side):
        pl.semaphore_signal(barrier, inc=1, device_id={"dp": other}, device_id_type=MESH)
    pl.semaphore_signal(barrier, inc=1, device_id={"section": 1 - section}, device_id_type=MESH)

    def needed(b):
        return decoding if b == 1 else me >= 0

    def utt(u):
        return utt_rows(u, length)

    def own_rows(b, t, src):
        return pltpu.make_async_copy(src, bufs[b].at[me, t * part:(t + 1) * part], l_sem.at[b, t])

    own_a = [own_rows(0, 0, in_ref.at[1]), own_rows(0, 1, in_ref.at[2]), own_rows(0, 2, in_ref.at[0]),
             own_rows(0, 3, o_ref)]
    own_c = [own_rows(1, 2, cross_ref.at[0]), own_rows(1, 3, cross_ref.at[1])]
    own_w = [pltpu.make_async_copy(src, bufs[b].at[me], l_sem.at[b, 0]) for b, src in ((2, w1_ref), (3, w2_ref))]
    for copy in own_a:
        copy.start()

    @pl.when(decoding)
    def _():
        for copy in own_c:
            copy.start()
    for copy in own_w:
        copy.start()
    cotangent = pltpu.make_async_copy(cot_ref, dy, l_sem.at[1, 0])
    cotangent.start()
    stream = pltpu.make_async_copy(x_ref, hc, l_sem.at[1, 1])
    stream.start()

    small_ref[...] = jnp.zeros_like(small_ref)
    for row, value, query in ((0, 1, 0), (1, 2, 2)):
        for r in range(HEADS):
            small_ref[row:row + 1, part + 64 * r:part + 64 * (r + 1)] = bias_ref[HEADS * value + r]
            small_ref[row:row + 1, 2 * part + 64 * r:2 * part + 64 * (r + 1)] = bias_ref[HEADS * query + r]
    for r in range(b1_ref.shape[0]):
        small_ref[2:3, 128 * r:128 * (r + 1)] = b1_ref[r]
    rel = rel_ref.shape[2]
    for r in range(HEADS):
        small_ref[3 + r:4 + r, 0:rel] = rel_ref[r]
    wide = small_ref.shape[1]
    table = small_ref[...]
    lane = lax.broadcasted_iota(jnp.int32, table.shape, 1)
    line = lax.broadcasted_iota(jnp.int32, table.shape, 0)
    low, high = pltpu.roll(table, wide - rel // 2, 1), pltpu.roll(table, 2 * length - rel // 2, 1)
    around = jnp.where(lane < rel // 2, low, jnp.where(lane < length, table[:, rel - 1:rel],
                       jnp.where(lane < 2 * length - rel // 2, table[:, 0:1], high)))
    small_ref[...] = jnp.where((line >= 3) & (line < 3 + HEADS) & (lane < 2 * length), around, table)
    pl.semaphore_wait(barrier, mp + 2)
    for copy in own_a:
        copy.wait()

    def rows(which, hh=None):
        if hh is None:
            return pl.ds(pl.multiple_of(which * part, 16), part)
        size = part // HALVES
        return pl.ds(pl.multiple_of(which * part + hh * size, 16), size)

    def along(src, shard, b, hh, way, dist):
        return pltpu.make_async_remote_copy(
            src_ref=src, dst_ref=bufs[b].at[shard, rows(quarter, hh)],
            send_sem=z_send.at[way, dist - 1, b, hh], recv_sem=z_recv.at[way, dist - 1, b, hh],
            device_id={"mp": me + 1 - 2 * way}, device_id_type=MESH)

    def across(kind, shard, b, hh, which, way, dist, to):
        ref = bufs[b].at[shard, rows(which, hh)]
        return pltpu.make_async_remote_copy(
            src_ref=ref, dst_ref=ref,
            send_sem=p_send.at[kind, way, dist - 1, b, hh], recv_sem=p_recv.at[kind, way, dist - 1, b, hh],
            device_id={"dp": to}, device_id_type=MESH)

    def small_copy(hop, slot):
        return pltpu.make_async_remote_copy(
            src_ref=smalls.at[me], dst_ref=smalls.at[slot],
            send_sem=s_send.at[hop - 1], recv_sem=s_recv.at[hop - 1],
            device_id={"mp": lax.rem(me + hop, mp)}, device_id_type=MESH)

    def over(index, src, dst):
        return pltpu.make_async_remote_copy(
            src_ref=src, dst_ref=dst, send_sem=x_send.at[index], recv_sem=x_recv.at[index],
            device_id={"section": 1 - section}, device_id_type=MESH)

    def over_rows(i):
        return over(i, cross_ref.at[i], wc.at[me, i * part:(i + 1) * part])

    def over_mem(u):
        return over(3 + u, mem.at[utt(u)], mem.at[utt(u)])

    def over_dmem(u):
        return over(3 + utts + u, dmem.at[utt(u)], dmem.at[utt(u)])

    over_small = over(2, small_ref, peer_small)
    over_cb = over(3 + 2 * utts, cb, cb)
    over_kv = over(4 + 2 * utts, kv_grad.at[0], kv_grad.at[1])

    def has_next(way):
        return (me < mp - 1) if way == 0 else (me > 0)

    def has_shard(way, dist):
        return (me >= dist) if way == 0 else (me + dist <= mp - 1)

    def shard_at(way, dist):
        return me - dist if way == 0 else me + dist

    def own_src(b, hh):
        src = (wa.at[me], wc.at[me], w1_ref, w2_ref)[b]
        return src.at[rows(quarter, hh)]

    def own_send(b):
        for hh in range(HALVES):
            for way in (0, 1):
                @pl.when(needed(b) & has_next(way))
                def _():
                    along(own_src(b, hh), me, b, hh, way, 1).start()

    own_send(0)

    @pl.when(encoding)
    def _():
        for i in (0, 1):
            over_rows(i).start()
        over_small.start()
        smalls[me] = small_ref[...]
    own_send(2)

    @pl.when(decoding)
    def _():
        over_small.wait_recv()
        smalls[me] = small_ref[...]
        lane = lax.broadcasted_iota(jnp.int32, (1, small_ref.shape[1]), 1)
        smalls[me, 1:2] = jnp.where(lane < 2 * part, peer_small[1:2], small_ref[1:2])
    for hop in range(1, mp):
        small_copy(hop, me).start()

    steps = [(b, dist, hh) for b, dist in SEQUENCE for hh in range(HALVES)]

    def on_line(k):
        b, dist, hh = steps[k]
        for way in (0, 1):
            @pl.when(needed(b) & has_shard(way, dist))
            def _():
                shard = shard_at(way, dist)
                src = bufs[b].at[shard, rows(quarter, hh)]
                along(src, shard, b, hh, way, dist).wait_recv()
                if dist < mp - 1:
                    @pl.when(has_next(way))
                    def _():
                        along(src, shard, b, hh, way, dist + 1).start()
                across(1, shard, b, hh, quarter, way, dist, side).start()
                across(0, shard, b, hh, quarter, way, dist, core).start()
        if k == 0:
            own_send(3)
        if k == 2 * HALVES:
            @pl.when(decoding)
            def _():
                for copy in own_c:
                    copy.wait()
                for i in (0, 1):
                    over_rows(i).wait_recv()
            own_send(1)

    def on_side(k):
        b, dist, hh = steps[k]
        for way in (0, 1):
            @pl.when(needed(b) & has_shard(way, dist))
            def _():
                shard = shard_at(way, dist)
                across(1, shard, b, hh, side_quarter, way, dist, side).wait_recv()
                across(2, shard, b, hh, side_quarter, way, dist, core).start()

    def complete(k):
        b, dist, hh = steps[k]
        for way in (0, 1):
            @pl.when(needed(b) & has_shard(way, dist))
            def _():
                shard = shard_at(way, dist)
                across(0, shard, b, hh, core_quarter, way, dist, core).wait_recv()
                across(2, shard, b, hh, diag_quarter, way, dist, core).wait_recv()

    def run(*events):
        for event in events:
            act = {"L": on_line, "S": on_side, "P": complete}[event[0]]
            for hh in range(HALVES):
                act(int(event[1:]) * HALVES + hh)

    def drain():
        for hop in range(1, mp):
            small_copy(hop, me).wait_send()
        for b in range(BLOCKS):
            for hh in range(HALVES):
                for way in (0, 1):
                    @pl.when(needed(b) & has_next(way))
                    def _():
                        along(own_src(b, hh), me, b, hh, way, 1).wait_send()
        for b, dist, hh in steps:
            for way in (0, 1):
                @pl.when(needed(b) & has_shard(way, dist))
                def _():
                    shard = shard_at(way, dist)
                    across(0, shard, b, hh, quarter, way, dist, core).wait_send()
                    across(1, shard, b, hh, quarter, way, dist, side).wait_send()
                    across(2, shard, b, hh, side_quarter, way, dist, core).wait_send()
                    if dist < mp - 1:
                        @pl.when(has_next(way))
                        def _():
                            along(bufs[b].at[shard, rows(quarter, hh)], shard, b, hh, way, dist + 1).wait_send()

    def shard_of(i):
        return jnp.where(lax.rem(i, 2) == 0, mp - 1 - i // 2, i // 2)

    spots = 3 * mp + mp * section

    def place(b, i):
        return (spots - mp + i, 2 * mp + i, 2 * i + 1, 2 * i)[b]

    def piece(b, m, which, hh=None):
        return bufs[b].at[m, rows(which, hh)]

    cut = part // HALVES

    def to_core(b, i, m, k):
        return pltpu.make_async_remote_copy(
            src_ref=piece(b, m, 2 * k + 1 - parity), dst_ref=from_core.at[lax.rem(place(b, i), RING), k],
            send_sem=c_send.at[b, m, k], recv_sem=c_recv.at[b, m, k],
            device_id={"dp": core}, device_id_type=MESH)

    def to_side(b, m, hh):
        return pltpu.make_async_remote_copy(
            src_ref=piece(b, m, 2 * (1 - half) + parity, hh), dst_ref=from_side.at[b, m, pl.ds(hh * cut, cut)],
            send_sem=y_send.at[b, m, hh], recv_sem=y_recv.at[b, m, hh],
            device_id={"dp": side}, device_id_type=MESH)

    def line_slot(way, m, at):
        return m if way == 0 else jnp.where(m == at, mp, m)

    def to_line(way, b, m, hh):
        to = me + 1 - 2 * way
        return pltpu.make_async_remote_copy(
            src_ref=piece(b, m, quarter, hh), dst_ref=from_line.at[line_slot(way, m, to), b, pl.ds(hh * cut, cut)],
            send_sem=r_send.at[way, b, m, hh], recv_sem=r_recv.at[way, b, m, hh],
            device_id={"mp": to}, device_id_type=MESH)

    def add(b, m, which, other, hh=None):
        ref = piece(b, m, which, hh)
        ref[...] = (ref[...].astype(f32) + other[...].astype(f32)).astype(bf16)

    def send_core(b, i):
        @pl.when(needed(b))
        def _():
            @pl.when(place(b, i) >= RING)
            def _():
                pl.semaphore_wait(credit, 1)
            for k in (0, 1):
                to_core(b, i, shard_of(i), k).start()

    def stage_core(b, i):
        m = shard_of(i)
        spot = place(b, i)

        @pl.when(needed(b))
        def _():
            for k in (0, 1):
                to_core(b, i, m, k).wait_recv()
                add(b, m, 2 * k + parity, from_core.at[lax.rem(spot, RING), k])
            for hh in range(HALVES):
                to_side(b, m, hh).start()

            @pl.when(spot + RING < spots)
            def _():
                pl.semaphore_signal(credit, inc=1, device_id={"dp": core}, device_id_type=MESH)

    def stage_side(b, i):
        m = shard_of(i)

        @pl.when(needed(b))
        def _():
            for hh in range(HALVES):
                to_side(b, m, hh).wait_recv()
                add(b, m, quarter, from_side.at[b, m, pl.ds(hh * cut, cut)], hh)
                for way in (0, 1):
                    first = (me == 0) if way == 0 else (me == mp - 1)

                    @pl.when(first & (me != m))
                    def _():
                        to_line(way, b, m, hh).start()

    def stage_line(b, i, hop):
        m = shard_of(i)
        for way in (0, 1):
            inner = ((me == hop) & (me < m)) if way == 0 else ((me == mp - 1 - hop) & (me > m))

            @pl.when(needed(b) & inner)
            def _():
                for hh in range(HALVES):
                    to_line(way, b, m, hh).wait_recv()
                    add(b, m, quarter, from_line.at[m, b, pl.ds(hh * cut, cut)], hh)
                    to_line(way, b, m, hh).start()

    def ffn_ticks(i):
        stage_side(3, i)

        @pl.when(i > 0)
        def _():
            stage_line(2, i - 1, 1)
            stage_line(3, i - 1, 2)
        stage_side(2, i)
        stage_line(3, i, 1)

        @pl.when(i > 0)
        def _():
            stage_line(2, i - 1, 2)

    def cross_tick(i):
        stage_side(1, i)

        @pl.when(i == 0)
        def _():
            stage_line(2, mp - 1, 1)
            stage_line(3, mp - 1, 2)

        @pl.when(i > 0)
        def _():
            stage_line(1, i - 1, 1)

        @pl.when(i == 1)
        def _():
            stage_line(2, mp - 1, 2)

        @pl.when(i > 1)
        def _():
            stage_line(1, i - 2, 2)

    def self_tick(i):
        stage_side(0, i)
        if i == 0:
            @pl.when(encoding)
            def _():
                stage_line(2, mp - 1, 1)
                stage_line(3, mp - 1, 2)
            stage_line(1, mp - 1, 1)
            stage_line(1, mp - 2, 2)
        else:
            stage_line(0, i - 1, 1)
        if i == 1:
            @pl.when(encoding)
            def _():
                stage_line(2, mp - 1, 2)
            stage_line(1, mp - 1, 2)
        if i > 1:
            stage_line(0, i - 2, 2)

    stream.wait()

    def prepare(rws):
        x = hc[rws].astype(f32)
        h[rws] = norm(x, vec_ref[0:1], vec_ref[1:2]).astype(bf16)
        x1[rws] = x + vec_ref[2:3]
    row_loop(total, 256, prepare)

    query_at = lax.broadcasted_iota(jnp.int32, (1, length), 1)

    def limits(u):
        last = lens_ref[section, me * utts + u] - 1
        return jnp.where(decoding, jnp.minimum(query_at, last), last)

    def frames(u):
        return jnp.full((1, length), lens_ref[0, me * utts + u] - 1, jnp.int32)

    lane = lax.broadcasted_iota(jnp.int32, (1, PROJ), 1)
    scale = jnp.where((lane >= KV) & (lane < KV + part), 0.125, 1.0)

    def self_shards(g, carry):
        shards = (2 * g, 2 * g + 1)
        for m in shards:
            def keep(cols, value):
                qkv[m, :, cols] = ((value + smalls[m, 0:1, cols]) * scale[:, cols]).astype(bf16)
            wide_dot(nt, h[...], lambda s, n: wa[m, s:s + n], PROJ, keep)
        attend([(m, u) for m in shards for u in range(utts)], length, qkv, ctx, p, limits, smalls)
        x1[...] += nn(ctx[shards[0]], wa[shards[0], CTX:]) + nn(ctx[shards[1]], wa[shards[1], CTX:])
        return carry

    def ffn_one(m):
        ffn_shard(m, slice(0, total), h, w1, w2, a, gp, smalls[m, 2:3], out)

    def ffn_at(dist):
        @pl.when(encoding)
        def _():
            def step(way, carry):
                @pl.when(jnp.where(way == 0, me >= dist, me + dist <= mp - 1))
                def _():
                    ffn_one(jnp.where(way == 0, me - dist, me + dist))
                return carry
            lax.fori_loop(0, 2, step, 0)

    run("L0", "L1", "S0", "L2", "P0", "L3", "S1", "S2", "L4", "P1", "P2", "S4", "L5", "L6", "P4")
    for hop in range(1, mp):
        small_copy(hop, lax.rem(me + mp - hop, mp)).wait_recv()
    lax.fori_loop(0, mp // 4, self_shards, 0)
    run("L7", "L8", "S3")
    lax.fori_loop(mp // 4, mp // 2, self_shards, 0)
    for copy in own_w:
        copy.wait()
    spill = [pltpu.make_async_copy(src, dst, i_sem.at[j]) for j, (src, dst) in enumerate(
        ((qkv, qkv_hbm), (ctx, ctx_hbm), (p, p_hbm)))]
    fetch = [pltpu.make_async_copy(dst, src, i_sem.at[j]) for j, (src, dst) in enumerate(
        ((qkv, qkv_hbm), (ctx, ctx_hbm), (p, p_hbm)))]
    give = pltpu.make_async_copy(out, out_hbm, i_sem.at[3])

    @pl.when(decoding)
    def _():
        for copy in spill:
            copy.start()

        def start_cross(rws):
            y = x1[rws]
            hc[rws] = norm(y, vec_ref[3:4], vec_ref[4:5]).astype(bf16)
            y2[rws] = y
        row_loop(total, 256, start_cross)

    @pl.when(encoding)
    def _():
        row_loop(total, length, lambda rws: ffn_start(rws, x1, out, h, vec_ref))
        ffn_one(me)

    run("L9", "L10", "S5", "P3")
    ffn_at(1)

    run("S6", "L11", "S7", "S8", "P5", "P6", "P8")
    ffn_at(2)
    run("S9", "S10", "S11", "P7", "P9", "P10", "P11")
    ffn_at(3)

    @pl.when(decoding)
    def _():
        for copy in spill:
            copy.wait()

        def queries(m, carry):
            pq = nt(hc[...], wc[m, KV:PROJ])
            qkv[m, :, KV:] = ((pq + smalls[m, 1:2, KV:PROJ]) * scale[:, KV:]).astype(bf16)
            return carry
        lax.fori_loop(0, mp, queries, 0)

    @pl.when(encoding)
    def _():
        for u in range(utts):
            mem[utt(u)] = norm(out[utt(u)], vec_ref[3:4], vec_ref[4:5]).astype(bf16)
            over_mem(u).start()
        give.start()
        drain()
        cotangent.wait()
        g[...] = dy[...].astype(f32)
        turn(ht, h[...])
        give.wait()
        for u in range(utts):
            over_dmem(u).wait_recv()
        norm_back(total, out, vec_ref[3:4], dmem, g, vg, 3)

        dy[...] = g[...].astype(bf16)
        turn(dyt, dy[...])
        vg[7:8, :] = jnp.sum(g[...], axis=0, keepdims=True)
        dh[...] = jnp.zeros_like(dh)

        def ffn_step(i, carry):
            m = shard_of(i)
            hidden_grad(m, gp, w2, dy, sg)
            w2[m] = nn(dyt[...], a[m]).astype(bf16)
            send_core(3, i)

            @pl.when(i > 0)
            def _():
                stage_core(2, i - 1)
            dh[...] += nt(gp[m], w1[m])
            w1[m] = nn(ht[...], gp[m]).astype(bf16)
            send_core(2, i)
            stage_core(3, i)

            @pl.when(i >= mp // 2)
            def _():
                ffn_ticks(i - mp // 2)
            return carry
        lax.fori_loop(0, mp, ffn_step, 0)
        norm_back(total, x1, vec_ref[5:6], dh, g, vg, 5)
        stage_core(2, mp - 1)
        over_cb.wait_recv()
        sg[pl.ds(0, mp), 1:2, :PROJ] = cb[:, 0:1, :]

    @pl.when(decoding)
    def _():
        def cross_utt(u, carry):
            over_mem(u).wait_recv()
            rws = utt(u)
            for m in range(mp):
                qkv[m, rws, :KV] = (nt(mem[rws], wc[m, :KV]) + smalls[m, 1:2, :KV]).astype(bf16)
            attend([(m, u) for m in range(mp)], length, qkv, ctx, p, frames, None)
            y2[rws] += sum(nn(ctx[m, rws], wc[m, CTX:]) for m in range(mp))
            ffn_start(rws, y2, out, h, vec_ref)

            def one(m, carry):
                ffn_shard(m, rws, h, w1, w2, a, gp, smalls[m, 2:3], out)
                return carry
            return lax.fori_loop(0, mp, one, carry)
        lax.fori_loop(0, utts, cross_utt, 0)
        give.start()
        cotangent.wait()
        g[...] = dy[...].astype(f32)
        vg[7:8, :] = jnp.sum(g[...], axis=0, keepdims=True)
        dy[...] = g[...].astype(bf16)
        turn(dyt, dy[...])
        turn(ht, h[...])
        drain()
        give.wait()
        dh[...] = jnp.zeros_like(dh)

        def dgrad(m, carry):
            hidden_grad(m, gp, w2, dy, sg)
            dh[...] += nt(gp[m], w1[m])
            return carry
        lax.fori_loop(0, mp, dgrad, 0)
        norm_back(total, y2, vec_ref[5:6], dh, g, vg, 5)

        early = 1

        def ffn_weights(i, carry):
            m = shard_of(i)
            w2[m] = nn(dyt[...], a[m]).astype(bf16)
            send_core(3, i)

            @pl.when((i > 0) & (i != early))
            def _():
                stage_core(2, i - 1)
            w1[m] = nn(ht[...], gp[m]).astype(bf16)
            send_core(2, i)
            stage_core(3, i)

            @pl.when(i >= mp // 2)
            def _():
                ffn_ticks(i - mp // 2)
            return carry
        lax.fori_loop(0, early, ffn_weights, 0)

        dy[...] = g[...].astype(bf16)

        def cross_back(u, carry):
            rws = utt(u)
            for pair in range(0, mp, 2):
                shards = (pair, pair + 1)
                for m in shards:
                    dctx[m - pair] = nt(dy[rws], wc[m, CTX:]).astype(bf16)
                attend_back([(m, u) for m in shards], length, qkv, p,
                            lambda m, rows, t: tile(dctx, m - pair, slice(None), t), qkv, None, None)
            dmem[rws] = sum(nn(qkv[m, rws, :KV], wc[m, :KV]) for m in range(mp)).astype(bf16)
            over_dmem(u).start()
            dh[rws] = sum(nn(qkv[m, rws, KV:], wc[m, KV:PROJ]) for m in range(mp))

            @pl.when(u == 0)
            def _():
                stage_core(2, early - 1)
            return carry
        lax.fori_loop(0, utts, cross_back, 0)
        lax.fori_loop(early, mp, ffn_weights, 0)

        def row_sums(m, carry):
            sums = jnp.sum(qkv[m].astype(f32), axis=0, keepdims=True)
            sg[m, 1:2, :PROJ] = sums
            cb[m, 0:1, :] = sums
            return carry
        lax.fori_loop(0, mp, row_sums, 0)
        over_cb.start()
        norm_back(total, x1, vec_ref[3:4], dh, g, vg, 3)
        turn(dyt, dy[...])
        turn(ht, hc[...])
        stream.start()

        def cross_weights(i, carry):
            m = shard_of(i)
            wc[m, :, :KV] = tn(mem[...], qkv[m, :, :KV]).astype(bf16)
            gq = nn(ht[...], qkv[m, :, KV:])
            go = nn(dyt[...], ctx[m])
            wc[m, :, KV:CTX] = gq[:, :T].astype(bf16)
            wc[m, :, CTX:PROJ] = (gq[:, T:] + go[:, :T]).astype(bf16)
            wc[m, :, PROJ:] = go[:, T:].astype(bf16)

            @pl.when(i == 0)
            def _():
                stage_core(2, mp - 1)
            send_core(1, i)

            @pl.when(i > 0)
            def _():
                stage_core(1, i - 1)

            @pl.when(i < mp // 2)
            def _():
                ffn_ticks(i + mp // 2)
            return carry
        lax.fori_loop(0, mp, cross_weights, 0)
        for copy in fetch:
            copy.start()
        stage_core(1, mp - 1)
        for copy in fetch:
            copy.wait()
        stream.wait()

    def prepare_self(rws):
        h[rws] = norm(hc[rws].astype(f32), vec_ref[0:1], vec_ref[1:2]).astype(bf16)
    row_loop(total, 256, prepare_self)
    vg[2:3, :] = jnp.sum(g[...], axis=0, keepdims=True)
    dy[...] = g[...].astype(bf16)
    turn(dyt, dy[...])
    turn(ht, h[...])
    dh[...] = jnp.zeros_like(dh)
    down = lax.broadcasted_iota(jnp.int32, (length, length), 0)
    right = lax.broadcasted_iota(jnp.int32, (length, length), 1)
    flip = (down + right == length - 1).astype(f32).astype(bf16)

    def dctx_at(rows, t):
        return tile(dctx, rows.start // length, slice(None), t)

    def self_step(i, carry):
        m = shard_of(i)
        for u in range(utts):
            dctx[u] = nt(dy[utt(u)], wa[m, CTX:]).astype(bf16)
        attend_back([(m, u) for u in range(utts)], length, qkv, p, lambda m, rows, t: dctx_at(rows, t), qkv, sg, flip)
        d = qkv[m]
        sg[m, 0:1, :PROJ] = jnp.sum(d.astype(f32), axis=0, keepdims=True)
        dh[...] += nn(d, wa[m, :PROJ])
        gd = nn(ht[...], d)
        go = nn(dyt[...], ctx[m])
        wa[m, :, :CTX] = gd[:, :CTX].astype(bf16)
        wa[m, :, CTX:PROJ] = (gd[:, CTX:] + go[:, :T]).astype(bf16)
        wa[m, :, PROJ:] = go[:, T:].astype(bf16)
        send_core(0, i)

        @pl.when(i > 0)
        def _():
            stage_core(0, i - 1)

        @pl.when(encoding & (i < mp // 2))
        def _():
            ffn_ticks(i + mp // 2)

        @pl.when(decoding)
        def _():
            cross_tick(i)
        return carry
    lax.fori_loop(0, mp, self_step, 0)
    norm_back(total, hc, vec_ref[0:1], dh, g, vg, 0)
    give_dx = pltpu.make_async_copy(g, dx_hbm, i_sem.at[3])
    give_dx.start()

    def small_sum(hop, src, to):
        return pltpu.make_async_remote_copy(
            src_ref=src, dst_ref=got_small.at[hop], send_sem=a_send.at[hop], recv_sem=a_recv.at[hop],
            device_id={"dp": to}, device_id_type=MESH)

    with_core, with_side = small_sum(0, sg, core), small_sum(1, pair_sg, side)
    with_core.start()
    with_core.wait_recv()
    pair_sg[...] = sg[...] + got_small[0]
    with_side.start()
    stage_core(0, mp - 1)
    self_tick(0)
    self_tick(1)
    with_side.wait_recv()
    with_core.wait_send()
    sg[...] = pair_sg[...] + got_small[1]

    def line_small(hop, which):
        peer = lax.rem(me + hop, mp)
        src = sg.at[peer] if which == 0 else sg.at[mp]
        return pltpu.make_async_remote_copy(
            src_ref=src, dst_ref=got_line.at[hop - 1, which],
            send_sem=b_send.at[hop - 1, which], recv_sem=b_recv.at[hop - 1, which],
            device_id={"mp": peer}, device_id_type=MESH)

    for hop in range(1, mp):
        for which in (0, 1):
            line_small(hop, which).start()
    stage = (x1.at[pl.ds(0, part)], x1.at[pl.ds(part, part)], y2.at[pl.ds(0, part)], y2.at[pl.ds(part, part)])

    def finish(b):
        stage[b][...] = bufs[b][me, rows(quarter)].astype(f32)

        @pl.when(me > 0)
        def _():
            for hh in range(HALVES):
                to_line(0, b, me, hh).wait_recv()
            stage[b][...] += from_line[me, b].astype(f32)

        @pl.when(me < mp - 1)
        def _():
            for hh in range(HALVES):
                to_line(1, b, me, hh).wait_recv()
            stage[b][...] += from_line[mp, b].astype(f32)

    def hand(b):
        return pltpu.make_async_copy(stage[b], own_hbm.at[b], l_sem.at[b, 0])

    self_tick(2)
    @pl.when(decoding)
    def _():
        finish(1)
        kv_grad[0] = stage[1][:, :2 * part].astype(bf16)
        over_kv.start()
        hand(1).start()
    for b in (3, 2):
        finish(b)
        hand(b).start()
    self_tick(3)
    stage_line(0, mp - 1, 1)
    stage_line(0, mp - 2, 2)
    stage_line(0, mp - 1, 2)
    small_out[0] = sg[me]
    small_out[1] = sg[mp]
    for hop in range(1, mp):
        for which in (0, 1):
            line_small(hop, which).wait_recv()
            small_out[which] += got_line[hop - 1, which]

    finish(0)
    hand(0).start()

    @pl.when(encoding)
    def _():
        over_kv.wait_recv()
        stage[1][:, :2 * part] = kv_grad[1].astype(f32)
        hand(1).start()

    @pl.when(encoding)
    def _():
        for i in (0, 1):
            over_rows(i).wait_send()
        over_small.wait_send()
        for u in range(utts):
            over_mem(u).wait_send()

    @pl.when(decoding)
    def _():
        for u in range(utts):
            over_dmem(u).wait_send()
        over_cb.wait_send()
        over_kv.wait_send()
    with_side.wait_send()
    for hop in range(1, mp):
        for which in (0, 1):
            line_small(hop, which).wait_send()

    def left(i, carry):
        m = shard_of(i)
        for b in range(BLOCKS):
            @pl.when(needed(b))
            def _():
                for k in (0, 1):
                    to_core(b, i, m, k).wait_send()
                for hh in range(HALVES):
                    to_side(b, m, hh).wait_send()
                    for way in (0, 1):
                        @pl.when((me < m) if way == 0 else (me > m))
                        def _():
                            to_line(way, b, m, hh).wait_send()
        return carry
    lax.fori_loop(0, mp, left, 0)
    for b in range(BLOCKS):
        hand(b).wait()
    give_dx.wait()


def layers(mp, dp, utts, length, lens, x, cot, vec, biases, b_one, rel, w_in, w_o, w_cross, w_one, w_two):
    total, width = x.shape
    hidden = w_one.shape[1]
    sds = jax.ShapeDtypeStruct
    v = pltpu.VMEM
    sem = pltpu.SemaphoreType.DMA
    shard = v((mp, width, hidden), bf16)
    part = width // 4
    wide_b, wide_f = v((total, width), bf16), v((total, width), f32)
    turned = v((width, total), bf16)
    heads = (utts, mp, HEADS, length, length)
    proj, context = (mp, total, PROJ), (mp, total, 2 * LANES)
    rows = (8, width)
    gather = (2, mp - 1, BLOCKS, HALVES)
    return pl.pallas_call(
        functools.partial(layers_kernel, mp, dp, utts, length),
        out_shape=(sds((2,) + rows, f32), sds((total, width), f32), sds((total, width), f32),
                   sds((BLOCKS, part, hidden), f32), sds(proj, bf16), sds(context, bf16), sds(heads, bf16)),
        in_specs=[SMEM, ANY, ANY, VM, VM, VM, VM] + [ANY] * 5,
        out_specs=(VM,) + (ANY,) * 6,
        scratch_shapes=[wide_f] + [shard] * 4 + [
            v((mp,) + rows, f32), v(rows, f32), v(rows, f32), v(proj, bf16), v(context, bf16), v(heads, bf16),
            v((mp, total, hidden), bf16), v((mp, total, hidden), bf16),
            wide_f, wide_f, wide_f, wide_b, wide_b, wide_b, wide_b,
            wide_b, turned, turned, v((max(utts, 2), length, 2 * LANES), bf16), v((mp + 1,) + rows, f32),
            v((mp, 8, PROJ), f32),
            v((RING, 2, part, hidden), bf16), v((BLOCKS, mp, part, hidden), bf16), v((mp + 1, BLOCKS, part, hidden), bf16),
            v((mp + 1,) + rows, f32), v((2, mp + 1) + rows, f32), v((mp - 1, 2) + rows, f32),
            v((2, part, 2 * part), bf16),
            sem((BLOCKS, 4)), sem(gather), sem(gather), sem((3,) + gather), sem((3,) + gather),
            sem((mp - 1,)), sem((mp - 1,)), sem((5 + 2 * utts,)), sem((5 + 2 * utts,)), sem((4,)),
            sem((BLOCKS, mp, 2)), sem((BLOCKS, mp, 2)), sem((BLOCKS, mp, HALVES)), sem((BLOCKS, mp, HALVES)),
            sem((2, BLOCKS, mp, HALVES)), sem((2, BLOCKS, mp, HALVES)), pltpu.SemaphoreType.REGULAR,
            sem((2,)), sem((2,)), sem((mp - 1, 2)), sem((mp - 1, 2))],
        compiler_params=pltpu.CompilerParams(collective_id=0, has_side_effects=True, vmem_limit_bytes=63 * 2**20),
        name="both_layers",
    )(lens, x, cot, vec, biases, b_one, rel, w_in, w_o, w_cross, w_one, w_two)


def finish_kernel(mp, dp, length, rel, own_in, small, out_in, dx_in,
                  out, dx, vectors, in_grad, bias, o_grad, rel_grad, cross, one, b1, two,
                  own, out_held, dx_held, in_sem, out_sem):
    me = lax.axis_index("mp")
    dp_index = lax.axis_index("dp")
    decoding = lax.axis_index("section") == 1
    loads = [pltpu.make_async_copy(src, dst, in_sem.at[j]) for j, (src, dst) in enumerate(
        ((out_in, out_held), (dx_in, dx_held), (own_in.at[2], own.at[2]), (own_in.at[3], own.at[3]),
         (own_in.at[0], own.at[0]), (own_in.at[1], own.at[1])))]
    stores = [pltpu.make_async_copy(src, dst, out_sem.at[j]) for j, (src, dst) in enumerate(
        ((out_held, out), (dx_held, dx), (own.at[2], one), (own.at[3], two)))]
    for copy in loads:
        copy.start()
    for load, store in zip(loads, stores):
        load.wait()
        store.start()
    for copy in loads[4:]:
        copy.wait()
    part = own.shape[1]
    k, v, q, o = (slice(t * part, (t + 1) * part) for t in range(4))
    mine = own[0]
    in_grad[0], in_grad[1], in_grad[2] = mine[:, q], mine[:, k], mine[:, v]
    o_grad[...] = mine[:, o].T
    mine = own[1]
    cross[0] = jnp.where(decoding, mine[:, q], mine[:, k])
    cross[1] = jnp.where(decoding, mine[:, o], mine[:, v])
    width = small.shape[2]

    def back(value, by):
        return pltpu.roll(value, lax.rem(width - by, width), 1)

    vectors[...] = back(small[1], (dp_index * mp + me) * vectors.shape[1])[:, :vectors.shape[1]]
    size = bias.shape[2]
    turned = back(small[0], dp_index * size)
    cross_row = jnp.where(decoding, turned[1:2, q], turned[1:2, v])
    for t, row in enumerate((turned[0:1, q], turned[0:1, v], cross_row)):
        for r in range(HEADS):
            bias[3 * t + r] = row[:, 64 * r:64 * r + size]
    size = b1.shape[2]
    turned = back(small[0], dp_index * size)
    for r in range(b1.shape[0]):
        b1[r] = turned[2:3, 128 * r:128 * r + size]
    lines = small[0]
    low, high = length - rel // 2, length + rel // 2 - 2
    lane = lax.broadcasted_iota(jnp.int32, lines.shape, 1)
    first = jnp.sum(jnp.where(lane < low, lines, 0.0), axis=1, keepdims=True)
    last = jnp.sum(jnp.where((lane >= high) & (lane < 2 * length), lines, 0.0), axis=1, keepdims=True)
    moved = pltpu.roll(lines, width - (low - 1), 1)
    moved = jnp.where(lane == 0, first, jnp.where(lane == rel - 1, last, moved))
    moved = back(moved, dp_index * rel_grad.shape[2])
    for r in range(HEADS):
        rel_grad[r] = moved[3 + r:4 + r, :rel_grad.shape[2]]
    for store in stores:
        store.wait()


def finish(mp, dp, length, rel, own, small, out, dx):
    sds = jax.ShapeDtypeStruct
    part, hidden = own.shape[1:]
    width = small.shape[2]
    shard = width // mp
    return pl.pallas_call(
        functools.partial(finish_kernel, mp, dp, length, rel),
        out_shape=(sds(out.shape, f32), sds(dx.shape, f32), sds((8, width // (dp * mp)), f32),
                   sds((3, part, shard), f32), sds((3 * HEADS, 1, 64 // dp), f32), sds((shard, part), f32),
                   sds((HEADS, 1, rel // dp), f32), sds((2, part, shard), f32), sds((part, hidden), f32),
                   sds((hidden // 128, 1, 128 // dp), f32), sds((part, hidden), f32)),
        in_specs=[ANY, VM, ANY, ANY], out_specs=(ANY,) * 2 + (VM,) * 6 + (ANY, VM, ANY),
        scratch_shapes=[pltpu.VMEM(own.shape, f32), pltpu.VMEM(out.shape, f32), pltpu.VMEM(dx.shape, f32),
                        pltpu.SemaphoreType.DMA((6,)), pltpu.SemaphoreType.DMA((4,))],
        compiler_params=pltpu.CompilerParams(vmem_limit_bytes=60 * 2**20), name="finish",
    )(own, small, out, dx)


def per_device(streams, lengths, vectors, attn_in, attn_bias, attn_out, rel_table, cross, ffn_in, ffn_bias, ffn_out,
               cotangent):
    mp = lax.axis_size("mp")
    dp = lax.axis_size("dp")
    utts, length, width = streams.shape[1:]
    total = utts * length
    x = streams[0].reshape(total, width)
    cot = cotangent[0].reshape(total, width)
    vec = vectors[0]

    small_sum, g, out, own, _, _, _ = layers(
        mp, dp, utts, length, lengths, x, cot, vec, jnp.transpose(attn_bias, (1, 2, 0, 3)).reshape(3 * HEADS, 1, -1),
        jnp.swapaxes(ffn_bias, 0, 1), jnp.swapaxes(rel_table, 0, 1), jnp.swapaxes(attn_in[0], 1, 2), attn_out[0],
        jnp.swapaxes(cross[0], 1, 2), ffn_in[0], ffn_out[0])
    if dp > 4:
        near = [[q * (dp // 4) + i for i in range(dp // 4)] for q in range(4)]
        small_sum = lax.psum(small_sum, "dp", axis_index_groups=near)
    out, dx, vectors_grad, in_grad, bias_grad, o_grad, rel_grad, cross_grad, one_grad, b1_grad, two_grad = finish(
        mp, dp, length, rel_table.shape[2], own, small_sum, out, g)
    two_grad = two_grad.T
    if dp > 4:
        per = dp // 4
        groups = [[q * per + i for i in range(per)] for q in range(4)]

        def rest(value, axis):
            return lax.psum_scatter(value.astype(bf16), "dp", scatter_dimension=axis, axis_index_groups=groups,
                                    tiled=True).astype(f32)

        in_grad, o_grad, cross_grad = rest(in_grad, 1), rest(o_grad, 1), rest(cross_grad, 1)
        one_grad, two_grad = rest(one_grad, 0), rest(two_grad, 1)
    shape = (1, utts, length, width)
    bias_grad = bias_grad.reshape(3, HEADS, 1, -1)
    return (out.reshape(shape), dx.reshape(shape), vectors_grad[None], in_grad[None],
            jnp.transpose(bias_grad, (2, 0, 1, 3)), o_grad[None], jnp.swapaxes(rel_grad, 0, 1), cross_grad[None],
            one_grad[None], jnp.swapaxes(b1_grad, 0, 1), two_grad[None])


def solution(mesh):
    placed = (
        P("section", ("dp", "mp"), None, None),
        P(None, "dp"),
        P("section", None, None),
        P("section", None, None, "mp"),
        P("section", None, "mp", None),
        P("section", "mp", None),
        P("section", "mp", None),
        P("section", None, None, "mp"),
        P("section", None, "mp"),
        P("section", "mp", None),
        P("section", "mp", None),
        P("section", ("dp", "mp"), None, None),
    )
    return jax.shard_map(
        per_device,
        mesh=mesh,
        in_specs=placed,
        out_specs=(
            P("section", ("dp", "mp"), None, None),
            P("section", ("dp", "mp"), None, None),
            P("section", None, ("dp", "mp")),
            P("section", None, "dp", "mp"),
            P("section", None, "mp", "dp"),
            P("section", "mp", "dp"),
            P("section", "mp", "dp"),
            P("section", None, "dp", "mp"),
            P("section", "dp", "mp"),
            P("section", "mp", "dp"),
            P("section", "mp", "dp"),
        ),
        check_vma=False,
    )
```
